32 devices in a mesh: dp: 2 (over y), ctx: 8 (over z, x), tensor: 2 (over core).
Axes of the slice: x: 2, y: 2, z: 4, core: 2. Of those that a mesh axis runs over, the one named last changes fastest.
Arguments:
- tokens: bfloat16 [2, 2, 2048, 768], P(None, 'dp', 'ctx'), may hold values from -6 to 6
- prefix: int32 [2, 2], P(None, 'dp'), may hold values from 204 to 1024
- w_query: bfloat16 [768, 768], P(('dp', 'ctx'), 'tensor'), may hold values from -0.21875 to 0.21875
- w_key: bfloat16 [768, 768], P(('dp', 'ctx'), 'tensor'), may hold values from -0.21875 to 0.21875
- w_value: bfloat16 [768, 768], P(('dp', 'ctx'), 'tensor'), may hold values from -0.21875 to 0.21875
- w_score: bfloat16 [768, 12], P(('dp', 'ctx'), 'tensor'), may hold values from -0.4375 to 0.4375
- w_attn_out: bfloat16 [768, 768], P('tensor', ('dp', 'ctx')), may hold values from -1.5 to 1.5
- w_fc: bfloat16 [768, 3072], P(('dp', 'ctx'), 'tensor'), may hold values from -0.21875 to 0.21875
- w_proj: bfloat16 [3072, 768], P('tensor', ('dp', 'ctx')), may hold values from -0.109375 to 0.109375
- ln1_gain: bfloat16 [768], P(('dp', 'ctx')), may hold values from 0.5 to 1.5
- ln1_bias: bfloat16 [768], P(('dp', 'ctx')), may hold values from -2 to 2
- ln2_gain: bfloat16 [768], P(('dp', 'ctx')), may hold values from 0.5 to 1.5
- ln2_bias: bfloat16 [768], P(('dp', 'ctx')), may hold values from -2 to 2
- attn_bias: bfloat16 [768], P(('dp', 'ctx')), may hold values from -2 to 2
- fc_bias: bfloat16 [3072], P('tensor'), may hold values from -2 to 2
- proj_bias: bfloat16 [768], P(('dp', 'ctx')), may hold values from -2 to 2
- cotangent: bfloat16 [2, 2, 2048, 768], P(None, 'dp', 'ctx'), may hold values from -6 to 6
Outputs:
- output: bfloat16 [2, 2, 2048, 768], P(None, 'dp', 'ctx')
- tokens_grad: float32 [2, 2, 2048, 768], P(None, 'dp', 'ctx')
- w_query_grad: float32 [768, 768], P(('dp', 'ctx'), 'tensor')
- w_key_grad: float32 [768, 768], P(('dp', 'ctx'), 'tensor')
- w_value_grad: float32 [768, 768], P(('dp', 'ctx'), 'tensor')
- w_score_grad: float32 [768, 12], P(('dp', 'ctx'), 'tensor')
- w_attn_out_grad: float32 [768, 768], P('tensor', ('dp', 'ctx'))
- w_fc_grad: float32 [768, 3072], P(('dp', 'ctx'), 'tensor')
- w_proj_grad: float32 [3072, 768], P('tensor', ('dp', 'ctx'))
- ln1_gain_grad: float32 [768], P(('dp', 'ctx'))
- ln1_bias_grad: float32 [768], P(('dp', 'ctx'))
- ln2_gain_grad: float32 [768], P(('dp', 'ctx'))
- ln2_bias_grad: float32 [768], P(('dp', 'ctx'))
- attn_bias_grad: float32 [768], P(('dp', 'ctx'))
- fc_bias_grad: float32 [3072], P('tensor')
- proj_bias_grad: float32 [768], P(('dp', 'ctx'))
The draws below stay inside these ranges and needn't reach their ends.
All inputs are finite; a program needn't handle non-finite values.
Results may differ from the reference program's by a relative error of at most 0.017.
Values may be sent and summed in bfloat16 or wider, within the bound.
No kernel may reach another device: no remote copies, remote signals or barrier semaphores. Data moves between devices by JAX's collectives and lax.ppermute only.
A program may use at most 192 MiB of HBM per device.

```python
from functools import partial
import jax
import jax.numpy as jnp
from jax import lax

D = 768
HEADS = 12
HEAD_DIM = 64
FF = 3072
WIN = 64
TOPK = 64
MB = 2
TOK = 256
LEN = 2048
SEQS = 2


def plant(array, stream_key, smallest, top_value):
    longest = array.shape.index(max(array.shape))
    spots = []
    for shift in (0, 1):
        where = [jax.random.randint(jax.random.fold_in(stream_key, axis), (), 0, length) for axis, length in enumerate(array.shape)]
        where[longest] = (where[longest] + shift) % array.shape[longest]
        spots.append(tuple(where))
    return array.at[spots[0]].set(smallest).at[spots[1]].set(top_value)


def block_levels(own_key, shape, pieces, smallest, high):
    loudness, own = 1.0, jax.random.fold_in(own_key, 6)
    for position, parts in pieces:
        draws = jnp.exp(jax.random.uniform(jax.random.fold_in(own, position), (parts,), jnp.float32, smallest / len(pieces), high / len(pieces)))
        loudness = loudness * jnp.repeat(draws, shape[position] // parts).reshape([-1 if axis == position else 1 for axis in range(len(shape))])
    return loudness


def bell_draw(stream_key, shape, scale, limit, cuts=(), kind=jnp.bfloat16):
    factor_of = block_levels(stream_key, shape, cuts, -0.22, 0.18) if cuts else 1.0
    values = jax.random.normal(stream_key, shape, jnp.float32) * scale * factor_of
    return jnp.minimum(jnp.maximum(values, -limit), limit).astype(kind)


def setup_inputs(seed: int = 0) -> dict:
    key_of = jax.random.split(jax.random.key(seed), 18)
    return {
        "tokens": bell_draw(key_of[0], (MB, SEQS, LEN, D), 1.0, 6.0, ((1, 2), (2, 8))),
        "prefix": plant(jax.random.randint(key_of[1], (MB, SEQS), LEN // 10, LEN // 2 + 1), jax.random.fold_in(key_of[1], 1), LEN // 10, (LEN // 2 + 1) - 1).astype(jnp.int32),
        "w_query": bell_draw(key_of[2], (D, D), D ** -0.5, 0.21875, ((0, 16), (1, 2))),
        "w_key": bell_draw(key_of[3], (D, D), D ** -0.5, 0.21875, ((0, 16), (1, 2))),
        "w_value": bell_draw(key_of[4], (D, D), D ** -0.5, 0.21875, ((0, 16), (1, 2))),
        "w_score": bell_draw(key_of[5], (D, HEADS), (D // 4) ** -0.5, 0.4375, ((0, 16), (1, 2))),
        "w_attn_out": bell_draw(key_of[6], (D, D), 16 ** -0.5, 1.5, ((0, 2), (1, 16))),
        "w_fc": bell_draw(key_of[7], (D, FF), D ** -0.5, 0.21875, ((0, 16), (1, 2))),
        "w_proj": bell_draw(key_of[8], (FF, D), FF ** -0.5, 0.109375, ((0, 2), (1, 16))),
        "ln1_gain": jnp.clip(1.0 + 0.1 * jax.random.normal(key_of[9], (D,), jnp.float32), 0.5, 1.5).astype(jnp.bfloat16),
        "ln1_bias": bell_draw(key_of[10], (D,), 0.3, 2.0, ((0, 16),)),
        "ln2_gain": jnp.clip(1.0 + 0.1 * jax.random.normal(key_of[11], (D,), jnp.float32), 0.5, 1.5).astype(jnp.bfloat16),
        "ln2_bias": bell_draw(key_of[12], (D,), 0.3, 2.0, ((0, 16),)),
        "attn_bias": bell_draw(key_of[13], (D,), 0.3, 2.0, ((0, 16),)),
        "fc_bias": bell_draw(key_of[14], (FF,), 0.3, 2.0, ((0, 2),)),
        "proj_bias": bell_draw(key_of[15], (D,), 0.3, 2.0, ((0, 16),)),
        "cotangent": bell_draw(key_of[16], (MB, SEQS, LEN, D), 1.0, 6.0, ((1, 2), (2, 8))),
    }


@jax.custom_vjp
def low(v):
    return lax.optimization_barrier(v.astype(jnp.bfloat16)).astype(jnp.float32)

@jax.custom_vjp
def low_back(v):
    return v

def low_keep(v):
    return (low(v), None)

def low_pass(kept, grad):
    return (grad,)

def back_keep(v):
    return (v, None)

def back_low(kept, grad):
    return (low(grad),)
low.defvjp(low_keep, low_pass)
low_back.defvjp(back_keep, back_low)
norm_epsilon = 1e-05
search_steps = 24
search_bound = 64.0

def matmul(left, right):
    return jnp.dot(left, right, precision=lax.Precision.HIGHEST, preferred_element_type=jnp.float32)

def layer_normalize(values, norm_gain, norm_shift):
    centre = lax.optimization_barrier(jnp.mean(values, axis=-1, keepdims=True))
    centred = values - centre
    spread = lax.optimization_barrier(jnp.mean(centred * centred, axis=-1, keepdims=True))
    return centred * lax.rsqrt(spread + norm_epsilon) * norm_gain + norm_shift

def threshold_search(score_row, candidate):
    score_mat = score_row[None, :]
    lower_end = jnp.zeros((candidate.shape[0],), score_row.dtype) - search_bound
    upper_end = jnp.zeros((candidate.shape[0],), score_row.dtype) + search_bound

    def bisect(step, bounds):
        lower_now, upper_now = bounds
        centre_val = 0.5 * (lower_now + upper_now)
        filled = lax.optimization_barrier(jnp.sum(jnp.where(candidate, jax.nn.sigmoid(score_mat - centre_val[:, None]), 0.0), axis=1))
        above = filled > TOPK
        return (jnp.where(above, centre_val, lower_now), jnp.where(above, upper_now, centre_val))
    lower_end, upper_end = lax.fori_loop(0, search_steps, bisect, (lower_end, upper_end))
    return 0.5 * (lower_end + upper_end)

def sparse_mask(score_row, candidate, pivot):
    score_mat = score_row[None, :]
    mask = jnp.where(candidate, jax.nn.sigmoid(score_mat - pivot[:, None]), 0.0)
    enough = lax.optimization_barrier(jnp.sum(jnp.where(candidate, 1.0, 0.0), axis=1)) > TOPK
    return jnp.where(enough[:, None], mask, jnp.where(candidate, 1.0, 0.0))

def block_forward(packed, key_head, value_head, score_head, prefix_len):
    query_block, start = packed
    key_block = low_back(key_head)
    value_block = low_back(value_head)
    score_block = low_back(score_head)
    query_pos = start + jnp.arange(TOK, dtype=jnp.int32)
    key_pos = jnp.arange(LEN, dtype=jnp.int32)
    logits = low_back(matmul(query_block, key_block.T) * HEAD_DIM ** (-0.5))
    allowed = (key_pos[None, :] <= query_pos[:, None]) | (key_pos[None, :] < prefix_len)
    nearby = jnp.abs(query_pos[:, None] - key_pos[None, :]) < WIN
    local_keys = allowed & nearby
    candidate = allowed & jnp.logical_not(nearby)
    pivot = threshold_search(score_block, candidate)
    mask = sparse_mask(score_block, candidate, pivot)
    key_gate = jnp.where(local_keys, 1.0, mask)
    row_top = lax.optimization_barrier(jnp.max(jnp.where(local_keys, logits, -1e+30), axis=1, keepdims=True))
    weights = key_gate * jnp.exp(jnp.where(allowed, logits - row_top, -1e+30))
    probs = weights / lax.optimization_barrier(jnp.sum(weights, axis=1, keepdims=True))
    return matmul(low(probs), value_block)

def head_forward(packed, prefix_len):
    query_head, key_head, value_head, score_head = packed
    query_blocks = query_head.reshape(LEN // TOK, TOK, HEAD_DIM)
    starts = jnp.arange(LEN // TOK, dtype=jnp.int32) * TOK
    step_fn = jax.checkpoint(partial(block_forward, key_head=key_head, value_head=value_head, score_head=score_head, prefix_len=prefix_len))
    attended = lax.map(step_fn, (query_blocks, starts))
    return attended.reshape(LEN, HEAD_DIM)

def sequence_forward(seq_tokens, params, prefix_len):
    w_query, w_key, w_value, w_score, w_attn_out, w_fc, w_proj, ln1_gain, ln1_bias, ln2_gain, ln2_bias, attn_bias, fc_bias, proj_bias = params
    normed = low(layer_normalize(seq_tokens, ln1_gain, ln1_bias))
    queries = low(low_back(matmul(normed, w_query)))
    keys_all = low(low_back(matmul(normed, w_key)))
    values_all = low(low_back(matmul(normed, w_value)))
    key_scores = low(low_back(matmul(normed, w_score)))
    query_heads = queries.reshape(LEN, HEADS, HEAD_DIM).transpose(1, 0, 2)
    key_heads = keys_all.reshape(LEN, HEADS, HEAD_DIM).transpose(1, 0, 2)
    value_heads = values_all.reshape(LEN, HEADS, HEAD_DIM).transpose(1, 0, 2)
    attended = lax.map(partial(head_forward, prefix_len=prefix_len), (query_heads, key_heads, value_heads, key_scores.T))
    merged = low(low_back(attended.transpose(1, 0, 2).reshape(LEN, D)))
    middle = seq_tokens + low_back(matmul(merged, w_attn_out)) + attn_bias
    normed_two = low(layer_normalize(middle, ln2_gain, ln2_bias))
    hidden_pre = low_back(matmul(normed_two, w_fc) + fc_bias)
    active = low(jax.nn.gelu(hidden_pre, approximate=True))
    return middle + low_back(matmul(active, w_proj)) + proj_bias

def reference(tokens, prefix, w_query, w_key, w_value, w_score, w_attn_out, w_fc, w_proj, ln1_gain, ln1_bias, ln2_gain, ln2_bias, attn_bias, fc_bias, proj_bias, cotangent):
    params = tuple((matrix.astype(jnp.float32) for matrix in (w_query, w_key, w_value, w_score, w_attn_out, w_fc, w_proj, ln1_gain, ln1_bias, ln2_gain, ln2_bias, attn_bias, fc_bias, proj_bias)))
    flat_tokens = tokens.reshape(-1, LEN, D).astype(jnp.float32)
    flat_prefix = prefix.reshape(-1).astype(jnp.int32)
    flat_cot = cotangent.reshape(-1, LEN, D).astype(jnp.float32)

    def one_sequence(totals, packed):
        seq_tokens, seq_prefix, seq_cot = packed
        result, pull_back = jax.vjp(partial(sequence_forward, prefix_len=seq_prefix), seq_tokens, params)
        grad_tokens, grad_params = pull_back(seq_cot)
        totals = jax.tree.map(jnp.add, totals, grad_params)
        return (totals, (result.astype(jnp.bfloat16), grad_tokens))
    initial = jax.tree.map(jnp.zeros_like, params)
    totals, (results, grads_in) = lax.scan(one_sequence, initial, (flat_tokens, flat_prefix, flat_cot))
    return (results.reshape(tokens.shape), grads_in.reshape(tokens.shape), totals[0], totals[1], totals[2], totals[3], totals[4], totals[5], totals[6], totals[7], totals[8], totals[9], totals[10], totals[11], totals[12], totals[13])
```

```python
from functools import partial

import jax
import jax.numpy as jnp
import numpy as np
from jax import lax
from jax.experimental import pallas as pl
from jax.experimental.pallas import tpu as pltpu
from jax.sharding import PartitionSpec as P

WIN = 64
TOPK = 64
HEAD = 64
LANES = 128

norm_epsilon = 1e-05
search_steps = 24
search_bound = 64.0

CHUNK = 256
FAR = 1e9
OPEN_PIVOT = -1e6
NEWTON_TOLERANCE = 3e-3
NT = (((1,), (1,)), ((), ()))


def over_chunks(first, rows, prefix, body, carry):
    below = lax.div(jnp.maximum(first - (WIN - 1), 0), CHUNK)
    total = lax.div(jnp.maximum(first + rows, prefix) + CHUNK - 1, CHUNK)
    above = jnp.minimum(lax.div(first + rows + WIN - 1 + CHUNK - 1, CHUNK), total)
    whole = jnp.maximum(lax.div(prefix, CHUNK), above)
    carry = lax.fori_loop(0, below, body(False), carry)
    carry = lax.fori_loop(below, above, body(True), carry)
    carry = lax.fori_loop(above, whole, body(False), carry)
    return lax.fori_loop(whole, total, body(True), carry)


def fold(values, how):
    return how(values.reshape(values.shape[0] // 8, 8, values.shape[1]), axis=0)


def own_head(values, slot):
    lane = lax.broadcasted_iota(jnp.int32, values.shape, 1)
    kept = jnp.where(lax.div(lane, HEAD) == slot, values.astype(jnp.float32), 0.0)
    return kept.astype(jnp.bfloat16)


def masks(start, first, prefix, rows):
    key = lax.broadcasted_iota(jnp.int32, (CHUNK, rows), 0)
    row = lax.broadcasted_iota(jnp.int32, (CHUNK, rows), 1)
    behind = row - key + (first - start)
    allowed = (behind >= 0) | (key < prefix - start)
    return allowed, allowed & (jnp.abs(behind) < WIN)


def forward_kernel(table, prefix_ref, p_ref, vt_ref, o_ref, lse_ref, pivot_ref, sm_ref, st_ref):
    unit_count, rows, _ = o_ref.shape
    prefix = prefix_ref[0]
    lane = lax.broadcasted_iota(jnp.int32, (1, rows), 1)

    def unit(step, guess):
        slot, first, place = table[step, 0], table[step, 1], table[step, 2]
        query = own_head(p_ref[pl.ds(pl.multiple_of(first, rows), rows), 0:LANES], slot)
        score_lane = pl.multiple_of((3 + slot) * LANES, LANES)

        def build(masked):
            def run(chunk, top):
                start = pl.multiple_of(chunk * CHUNK, CHUNK)
                here = pl.ds(start, CHUNK)
                logits = lax.dot_general(
                    p_ref[here, LANES : 2 * LANES], query, NT, preferred_element_type=jnp.float32
                )
                score = p_ref[here, pl.ds(score_lane, LANES)].astype(jnp.float32)[:, :rows]
                if masked:
                    allowed, local = masks(start, first, prefix, rows)
                    logits = jnp.where(allowed, logits, -1e30)
                    score = jnp.where(local, FAR, jnp.where(allowed, score, -FAR))
                    top = jnp.maximum(top, fold(jnp.where(local, logits, -1e30), jnp.max))
                st_ref[here, :] = logits
                sm_ref[here, :] = score
                return top

            return run

        top = over_chunks(first, rows, prefix, build, jnp.full((8, rows), -1e30, jnp.float32))
        top = jnp.max(top, axis=0, keepdims=True)

        row = first + lane
        local_count = (
            jnp.minimum(row, WIN - 1) + 1 + jnp.clip(prefix - 1 - row, 0, WIN - 1)
        ).astype(jnp.float32)
        candidates = jnp.maximum(row + 1, prefix).astype(jnp.float32) - local_count
        chunks = lax.div(jnp.maximum(first + rows, prefix) + CHUNK - 1, CHUNK)
        entries = (chunks * CHUNK).astype(jnp.float32)
        searched = candidates > TOPK
        count = jnp.maximum(candidates, TOPK + 1.0)
        goal = jnp.log(TOPK / (count - TOPK))

        def measure(half):
            def run(chunk, sums):
                bent = jnp.tanh(sm_ref[pl.ds(pl.multiple_of(chunk * CHUNK, CHUNK), CHUNK), :] - half)
                return sums[0] + fold(bent, jnp.sum), sums[1] + fold(bent * bent, jnp.sum)

            zero = jnp.zeros((8, rows), jnp.float32)
            first_sum, second_sum = lax.fori_loop(0, chunks, run, (zero, zero))
            filled = 0.5 * (entries + jnp.sum(first_sum, axis=0, keepdims=True)) - local_count
            slope = 0.25 * (entries - jnp.sum(second_sum, axis=0, keepdims=True))
            return filled, slope

        def improve(state):
            turn, _, half, lower, upper, done = state
            filled, slope = measure(half)
            above = filled > TOPK
            lower = jnp.where(above, half, lower)
            upper = jnp.where(above, upper, half)
            newton = (filled - TOPK) / slope
            held = jnp.clip(filled, 1e-3, count - 1e-3)
            bent = (jnp.log(held / (count - held)) - goal) * (held * (count - held) / (count * slope))
            close = jnp.abs(newton) <= NEWTON_TOLERANCE
            following = half + 0.5 * jnp.where(close, newton, bent)
            inside = (following > lower) & (following < upper)
            halve = (turn >= 12) & (lax.rem(turn, 2) == 1)
            middle = 0.5 * (lower + upper)
            following = jnp.where(close | (inside & jnp.logical_not(halve)), following, middle)
            half = jnp.where(done > 0.0, half, following)
            done = jnp.where(close, 1.0, done)
            return turn + 1, jnp.min(done), half, lower, upper, done

        start_done = jnp.where(searched, 0.0, 1.0)
        bound = jnp.full((1, rows), 0.5 * search_bound, jnp.float32)
        _, _, half, lower, upper, done = lax.while_loop(
            lambda state: (state[0] < 12 + 2 * search_steps) & (state[1] < 0.5),
            improve,
            (0, jnp.min(start_done), guess, -bound, bound, start_done),
        )
        half = jnp.where(done > 0.0, half, 0.5 * (lower + upper))
        pivot = jnp.where(searched, half, OPEN_PIVOT)

        def weigh(chunk, sums):
            here = pl.ds(pl.multiple_of(chunk * CHUNK, CHUNK), CHUNK)
            raised = jnp.exp(st_ref[here, :] - top)
            weight = raised / (1.0 + jnp.exp(2.0 * (pivot - sm_ref[here, :])))
            merged = sums[1] + jnp.dot(
                vt_ref[:, here], weight.astype(jnp.bfloat16), preferred_element_type=jnp.float32
            )
            return sums[0] + fold(weight, jnp.sum), merged

        total, merged = lax.fori_loop(
            0,
            chunks,
            weigh,
            (jnp.zeros((8, rows), jnp.float32), jnp.zeros((LANES, rows), jnp.float32)),
        )
        total = jnp.sum(total, axis=0, keepdims=True)
        merged = merged / total
        own = jnp.where(slot == 0, merged[:HEAD], merged[HEAD:])
        o_ref[place] = own.T
        lse_ref[place] = top + jnp.log(total)
        pivot_ref[place] = pivot
        return jnp.where(searched, half, guess)

    lax.fori_loop(0, unit_count, unit, jnp.zeros((1, rows), jnp.float32))


def backward_kernel(
    table, prefix_ref, p_ref, kt_ref, do_ref, dot_ref, lse_ref, pivot_ref, d_ref, dq_ref, dk_ref, dv_ref, ds_ref
):
    unit_count, rows, _ = do_ref.shape
    length = p_ref.shape[0]
    prefix = prefix_ref[0]

    def clear(chunk, _):
        here = pl.ds(pl.multiple_of(chunk * CHUNK, CHUNK), CHUNK)
        for ref in (dq_ref, dk_ref, dv_ref):
            ref[here, :] = jnp.zeros((CHUNK, LANES), jnp.float32)
        for slot in range(2):
            ds_ref[slot, here, :] = jnp.zeros((CHUNK, rows), jnp.float32)
        return 0

    lax.fori_loop(0, length // CHUNK, clear, 0)

    def unit(step, _):
        slot, first, place = table[step, 0], table[step, 1], table[step, 2]
        whose = pl.ds(pl.multiple_of(first, rows), rows)
        query = own_head(p_ref[whose, 0:LANES], slot)
        grad = own_head(do_ref[place], slot)
        row_dot, lse, pivot = dot_ref[place], lse_ref[place], pivot_ref[place]
        score_lane = pl.multiple_of((3 + slot) * LANES, LANES)

        def body(masked):
            def run(chunk, grad_query):
                start = pl.multiple_of(chunk * CHUNK, CHUNK)
                here = pl.ds(start, CHUNK)
                logits = lax.dot_general(
                    p_ref[here, LANES : 2 * LANES], query, NT, preferred_element_type=jnp.float32
                )
                grad_probs = lax.dot_general(
                    p_ref[here, 2 * LANES : 3 * LANES], grad, NT, preferred_element_type=jnp.float32
                )
                score = p_ref[here, pl.ds(score_lane, LANES)].astype(jnp.float32)[:, :rows]
                if masked:
                    allowed, local = masks(start, first, prefix, rows)
                    logits = jnp.where(allowed, logits, -1e30)
                    score = jnp.where(local, FAR, jnp.where(allowed, score, -FAR))
                unit_probs = jnp.exp(logits - lse)
                gate = 1.0 / (1.0 + jnp.exp(2.0 * (pivot - score)))
                probs = gate * unit_probs
                grad_logits = probs * (grad_probs - row_dot)
                ds_ref[slot, here, :] += grad_logits * (1.0 - gate)
                low = grad_logits.astype(jnp.bfloat16)
                dk_ref[here, :] += jnp.dot(low, query, preferred_element_type=jnp.float32)
                dv_ref[here, :] += jnp.dot(
                    probs.astype(jnp.bfloat16), grad, preferred_element_type=jnp.float32
                )
                return grad_query + jnp.dot(
                    kt_ref[:, here], low, preferred_element_type=jnp.float32
                )

            return run

        grad_query = over_chunks(
            first, rows, prefix, body, jnp.zeros((LANES, rows), jnp.float32)
        ).T
        lane = lax.broadcasted_iota(jnp.int32, grad_query.shape, 1)
        dq_ref[whose, :] += jnp.where(lax.div(lane, HEAD) == slot, grad_query, 0.0)
        return 0

    lax.fori_loop(0, unit_count, unit, 0)

    def finish(chunk, _):
        here = pl.ds(pl.multiple_of(chunk * CHUNK, CHUNK), CHUNK)
        d_ref[here, 0:LANES] = (dq_ref[here, :] * HEAD**-0.5).astype(jnp.bfloat16)
        d_ref[here, LANES : 2 * LANES] = dk_ref[here, :].astype(jnp.bfloat16)
        d_ref[here, 2 * LANES : 3 * LANES] = dv_ref[here, :].astype(jnp.bfloat16)
        lane = lax.broadcasted_iota(jnp.int32, (CHUNK, LANES), 1)
        columns = [jnp.sum(ds_ref[slot, here, :], axis=1, keepdims=True) for slot in range(2)]
        grad_score = jnp.where(lane == 0, columns[0], jnp.where(lane == 1, columns[1], 0.0))
        d_ref[here, 3 * LANES : 4 * LANES] = grad_score.astype(jnp.bfloat16)
        return 0

    lax.fori_loop(0, length // CHUNK, finish, 0)


VMEM_LIMIT = 48 * 1024 * 1024


def attend(table, prefix, projected, values_t, rows):
    unit_count = table.shape[0]
    length = projected.shape[0]
    smem = pl.BlockSpec(memory_space=pltpu.SMEM)
    vmem = pl.BlockSpec(memory_space=pltpu.VMEM)
    pairs = unit_count * rows * length
    return pl.pallas_call(
        forward_kernel,
        out_shape=(
            jax.ShapeDtypeStruct((unit_count, rows, HEAD), jnp.float32),
            jax.ShapeDtypeStruct((unit_count, 1, rows), jnp.float32),
            jax.ShapeDtypeStruct((unit_count, 1, rows), jnp.float32),
        ),
        in_specs=[smem, smem, vmem, vmem],
        out_specs=(vmem, vmem, vmem),
        scratch_shapes=[pltpu.VMEM((length, rows), jnp.float32), pltpu.VMEM((length, rows), jnp.float32)],
        compiler_params=pltpu.CompilerParams(vmem_limit_bytes=VMEM_LIMIT),
        cost_estimate=pl.CostEstimate(
            flops=pairs * 512, bytes_accessed=projected.size * 4, transcendentals=pairs * 8
        ),
        name="attend",
    )(table, prefix, projected, values_t)


def attend_back(table, prefix, projected, keys_t, grads, row_dots, log_totals, pivots):
    unit_count, rows, _ = grads.shape
    length = projected.shape[0]
    smem = pl.BlockSpec(memory_space=pltpu.SMEM)
    vmem = pl.BlockSpec(memory_space=pltpu.VMEM)
    pairs = unit_count * rows * length
    return pl.pallas_call(
        backward_kernel,
        out_shape=jax.ShapeDtypeStruct((length, 4 * LANES), jnp.bfloat16),
        in_specs=[smem, smem] + [vmem] * 6,
        out_specs=vmem,
        scratch_shapes=[
            pltpu.VMEM((length, LANES), jnp.float32),
            pltpu.VMEM((length, LANES), jnp.float32),
            pltpu.VMEM((length, LANES), jnp.float32),
            pltpu.VMEM((2, length, rows), jnp.float32),
        ],
        compiler_params=pltpu.CompilerParams(vmem_limit_bytes=VMEM_LIMIT),
        cost_estimate=pl.CostEstimate(
            flops=pairs * 1280, bytes_accessed=projected.size * 4, transcendentals=pairs * 3
        ),
        name="attend_back",
    )(table, prefix, projected, keys_t, grads, row_dots, log_totals, pivots)


class Grid:
    def __init__(self, count):
        self.deep = 4 if count % 4 == 0 else 1
        self.wide = count // self.deep
        self.count = count

    def index(self, place, across):
        return place * self.wide + across


def hop(values, pairs):
    return lax.ppermute(values, "ctx", pairs)


def line_gather(values, length, pair_of):
    pieces = {0: values}
    ahead = behind = values
    for step in range(1, length):
        ahead = hop(ahead, [p for s in range(step - 1, length - 1) for p in pair_of(s, s + 1)])
        behind = hop(behind, [p for s in range(1, length - step + 1) for p in pair_of(s, s - 1)])
        pieces[-step], pieces[step] = ahead, behind
    return pieces


def gather_ctx(values, grid):
    me = lax.axis_index("ctx")
    place, across = me // grid.wide, me % grid.wide
    rows = values.shape[0]

    def along(s, r):
        return [(grid.index(s, w), grid.index(r, w)) for w in range(grid.wide)]

    deep = line_gather(values, grid.deep, along)
    slots = {}
    for distance, piece in deep.items():
        held = [z for z in range(grid.deep) if 0 <= z + distance < grid.deep]

        def sideways(s, r, held=held):
            return [(grid.index(z, s), grid.index(z, r)) for z in held]

        for shift, part in line_gather(piece, grid.wide, sideways).items():
            slot = (distance % grid.deep, shift % grid.wide)
            slots[slot] = part if slot not in slots else slots[slot] + part
    whole = jnp.zeros((rows * grid.count,) + values.shape[1:], values.dtype)
    for (distance, shift), part in slots.items():
        target = grid.index((place + distance) % grid.deep, (across + shift) % grid.wide)
        whole = lax.dynamic_update_slice_in_dim(whole, part, target * rows, 0)
    return whole


def line_scatter(block, length, place, pair_of):
    ahead = behind = None
    for step in range(length - 1, 0, -1):
        outgoing = block(step) if ahead is None else (block(step) + ahead)
        ahead = hop(
            outgoing.astype(jnp.bfloat16), [p for s in range(length - step) for p in pair_of(s, s + 1)]
        ).astype(jnp.float32)
        outgoing = block(-step) if behind is None else (block(-step) + behind)
        behind = hop(
            outgoing.astype(jnp.bfloat16), [p for s in range(step, length) for p in pair_of(s, s - 1)]
        ).astype(jnp.float32)
    total = block(0)
    return total if ahead is None else total + ahead + behind


def scatter_ctx(values, grid):
    me = lax.axis_index("ctx")
    place, across = me // grid.wide, me % grid.wide
    rows = values.shape[0] // grid.count

    def sideways(s, r):
        return [(grid.index(z, s), grid.index(z, r)) for z in range(grid.deep)]

    def along(s, r):
        return [(grid.index(s, w), grid.index(r, w)) for w in range(grid.wide)]

    lines = {}
    order = sorted(range(grid.deep), key=lambda d: -abs(d - grid.deep / 2 + 0.1))
    for distance in [d for d in order if d] + [0]:
        target = (place + distance) % grid.deep

        def block(shift, target=target):
            which = grid.index(target, (across + shift) % grid.wide)
            return lax.dynamic_slice_in_dim(values, which * rows, rows, 0).astype(jnp.float32)

        lines[distance] = line_scatter(block, grid.wide, across, sideways)
    return line_scatter(lambda d: lines[d % grid.deep], grid.deep, place, along)


def other_core(values):
    return lax.ppermute(values, "tensor", [(0, 1), (1, 0)])


def normalize(values):
    centred = values - jnp.mean(values, axis=-1, keepdims=True)
    scale = lax.rsqrt(jnp.mean(centred * centred, axis=-1, keepdims=True) + norm_epsilon)
    return centred * scale, scale


def normalize_back(grad, hat, scale, gain):
    scaled = grad * gain
    return scale * (
        scaled
        - jnp.mean(scaled, axis=-1, keepdims=True)
        - hat * jnp.mean(scaled * hat, axis=-1, keepdims=True)
    )


def head_plan(ctx_count, head_count, block):
    parts = 1
    while head_count * parts % ctx_count:
        parts += 1
    share = head_count * parts // ctx_count
    rows = block // parts
    lows, tables = [], []
    for device in range(ctx_count):
        pieces = range(share * device, share * (device + 1))
        lows.append(pieces[0] // parts)
        tables.append(
            [
                (piece // parts - lows[-1], at * block + (piece % parts) * rows, at * share + order)
                for order, piece in enumerate(pieces)
                for at in range(ctx_count)
            ]
        )
        assert all(entry[0] in (0, 1) for entry in tables[-1])
    return parts, share, rows, lows, np.asarray(tables, np.int32)


def on_device(
    tokens,
    prefix,
    w_query,
    w_key,
    w_value,
    w_score,
    w_attn_out,
    w_fc,
    w_proj,
    ln1_gain,
    ln1_bias,
    ln2_gain,
    ln2_bias,
    attn_bias,
    fc_bias,
    proj_bias,
    cotangent,
    dp_count,
    ctx_count,
):
    f32, bf16 = jnp.float32, jnp.bfloat16
    micro_count, seq_count, block, width = tokens.shape
    local_heads = w_score.shape[1]
    head_count = 2 * local_heads
    assert micro_count == 2 and seq_count == 1
    core = lax.axis_index("tensor")
    me = lax.axis_index("ctx")
    grid = Grid(ctx_count)
    both = ("dp", "ctx")
    shards = dp_count * ctx_count
    shard_rows = width // shards
    parts, share, rows, lows, tables = head_plan(ctx_count, head_count, block)
    near = ctx_count // 2
    local_low = [low % local_heads for low in lows[:near]]
    local_high = [min(low + 1, local_heads - 1) for low in local_low]

    own_tokens = lax.dynamic_index_in_dim(tokens, core, 0, keepdims=False)[0]
    own_cot = lax.dynamic_index_in_dim(cotangent, core, 0, keepdims=False)[0]
    other_cot = lax.dynamic_index_in_dim(cotangent, 1 - core, 0, keepdims=False)[0]
    own_prefix = lax.dynamic_index_in_dim(prefix, core, 0, keepdims=False)
    table = jnp.asarray(tables)[me]

    all_tokens = gather_ctx(own_tokens, grid)

    vectors = jnp.stack([ln1_gain, ln1_bias, ln2_gain, ln2_bias, attn_bias, proj_bias], axis=1)
    spare = jnp.zeros((shard_rows, LANES - 2 - vectors.shape[1]), bf16)

    def columns(weight, head):
        return weight[:, head * HEAD : (head + 1) * HEAD]

    outgoing = jnp.stack(
        [
            jnp.concatenate(
                [columns(w, h) for w in (w_query, w_key, w_value) for h in (low, high)]
                + [w_score[:, low : low + 1], w_score[:, high : high + 1], vectors, spare],
                axis=1,
            )
            for low, high in zip(local_low, local_high)
        ]
    )
    outgoing = jnp.tile(outgoing, (2 * dp_count, 1, 1))
    head_weights = lax.all_to_all(outgoing, both, 0, 0, tiled=True).reshape(width, 4 * LANES)
    from_half = (me >= near).astype(jnp.int32)
    head_weights = jnp.where(from_half == core, head_weights, other_core(head_weights))
    gains = head_weights[:, 3 * LANES + 2 : 3 * LANES + 8].astype(f32).T
    gain_one, shift_one, gain_two, shift_two, attn_shift, proj_shift = [gains[i : i + 1] for i in range(6)]

    packed = jnp.concatenate([w_fc, w_proj.T, w_attn_out.T], axis=1)
    packed = lax.all_gather(packed, both, axis=0, tiled=True)
    hidden = w_fc.shape[1]
    full_fc, full_proj_t, half_out_t = packed[:, :hidden], packed[:, hidden : 2 * hidden], packed[:, 2 * hidden :]
    other_out_t = other_core(half_out_t)
    out_t = jnp.where(
        core == 0,
        jnp.concatenate([half_out_t, other_out_t], axis=1),
        jnp.concatenate([other_out_t, half_out_t], axis=1),
    )

    hat_one, scale_one = normalize(all_tokens.astype(f32))
    normed = (hat_one * gain_one + shift_one).astype(bf16)
    w_q, w_k, w_v = [head_weights[:, i * LANES : (i + 1) * LANES] for i in range(3)]
    score_columns = head_weights[:, 3 * LANES : 3 * LANES + 2]
    wide_weights = jnp.concatenate(
        [w_q * HEAD**-0.5, w_k, w_v]
        + [jnp.broadcast_to(score_columns[:, i : i + 1], (width, LANES)) for i in range(2)],
        axis=1,
    )
    projected = jnp.dot(normed, wide_weights, preferred_element_type=f32).astype(bf16)
    halver = jnp.where(jnp.arange(5 * LANES) < 3 * LANES, 1.0, 0.5).astype(bf16)
    projected = projected * halver
    turned = lax.dot_general(
        head_weights[:, LANES : 3 * LANES], normed, (((0,), (1,)), ((), ())), preferred_element_type=f32
    ).astype(bf16)
    keys_t, values_t = turned[:LANES], turned[LANES:]

    attended, log_totals, pivots = attend(table, own_prefix, projected, values_t, rows)

    sent = attended.astype(bf16).reshape(ctx_count, share * rows * HEAD // LANES, LANES)
    merged = lax.all_to_all(sent, "ctx", 0, 0, tiled=True)
    merged = merged.reshape(head_count, parts, rows, HEAD).transpose(1, 2, 0, 3).reshape(block, width)

    own_block = own_tokens.astype(f32)
    attn = lax.dot_general(merged, out_t, NT, preferred_element_type=f32)
    middle = own_block + attn + attn_shift
    hat_two, scale_two = normalize(middle)
    normed_two = (hat_two * gain_two + shift_two).astype(bf16)
    normed_two = jnp.concatenate([normed_two, other_core(normed_two)])
    hidden_pre = jnp.dot(normed_two, full_fc, preferred_element_type=f32) + fc_bias.astype(f32)
    active, pull_gelu = jax.vjp(partial(jax.nn.gelu, approximate=True), hidden_pre)
    active = active.astype(bf16)
    mlp = lax.dot_general(active, full_proj_t, NT, preferred_element_type=f32)
    result = middle + mlp[:block] + other_core(mlp[block:].astype(bf16)).astype(f32) + proj_shift
    result = result.astype(bf16)

    both_cot = jnp.concatenate([own_cot, other_cot])
    grad_active = jnp.dot(both_cot, full_proj_t, preferred_element_type=f32)
    grad_pre = pull_gelu(grad_active)[0].astype(bf16)
    grad_two = lax.dot_general(grad_pre, full_fc, NT, preferred_element_type=f32)
    grad_two = grad_two[:block] + other_core(grad_two[block:].astype(bf16)).astype(f32)
    cot = own_cot.astype(f32)
    grad_middle = cot + normalize_back(grad_two, hat_two, scale_two, gain_two)
    grad_middle_low = grad_middle.astype(bf16)
    grad_merged = jnp.dot(grad_middle_low, out_t, preferred_element_type=f32).astype(bf16)

    sent = grad_merged.reshape(parts, rows, head_count, HEAD).transpose(2, 0, 1, 3)
    sent = sent.reshape(ctx_count, share * rows * HEAD // LANES, LANES)
    grad_attended = lax.all_to_all(sent, "ctx", 0, 0, tiled=True).reshape(attended.shape)

    grad_fc = lax.dot_general(normed_two, grad_pre, (((0,), (0,)), ((), ())), preferred_element_type=f32)
    grad_proj_t = lax.dot_general(both_cot, active, (((0,), (0,)), ((), ())), preferred_element_type=f32)
    grad_out_t = lax.dot_general(
        grad_middle_low, merged, (((0,), (0,)), ((), ())), preferred_element_type=f32
    ).astype(bf16)
    half_width = width // 2
    mine, theirs = grad_out_t[:, :half_width], grad_out_t[:, half_width:]
    mine, theirs = jnp.where(core == 0, mine, theirs), jnp.where(core == 0, theirs, mine)
    grad_out_t = (mine.astype(f32) + other_core(theirs).astype(f32)).astype(bf16)
    grad_packed = jnp.concatenate([grad_fc.astype(bf16), grad_proj_t.astype(bf16), grad_out_t], axis=1)
    grad_packed = lax.psum_scatter(grad_packed, both, scatter_dimension=0, tiled=True).astype(f32)
    fc_bias_grad = lax.psum(jnp.sum(grad_pre.astype(f32), axis=0), both)

    row_dots = jnp.sum(attended * grad_attended.astype(f32), axis=-1)[:, None, :]
    doubled = jnp.concatenate([grad_attended, grad_attended], axis=-1)
    grads = attend_back(table, own_prefix, projected, keys_t, doubled, row_dots, log_totals, pivots)

    grad_normed = lax.dot_general(grads, head_weights, NT, preferred_element_type=f32)
    grad_one = scatter_ctx(grad_normed.astype(bf16), grid)
    own_hat, own_scale = normalize(own_block)
    tokens_grad = grad_middle + normalize_back(grad_one, own_hat, own_scale, gain_one)

    grad_vectors = jnp.stack(
        [
            jnp.sum(grad_normed * hat_one, axis=0),
            jnp.sum(grad_normed, axis=0),
            jnp.sum(grad_two * hat_two, axis=0),
            jnp.sum(grad_two, axis=0),
            jnp.sum(grad_middle, axis=0),
            jnp.sum(cot, axis=0),
        ],
        axis=1,
    )
    grad_heads = lax.dot_general(normed, grads, (((0,), (0,)), ((), ())), preferred_element_type=f32)
    grad_heads = jnp.concatenate(
        [grad_heads[:, : 3 * LANES + 2], grad_vectors, jnp.zeros((width, LANES - 8), f32)], axis=1
    )
    grad_heads = grad_heads + other_core(grad_heads.astype(bf16)).astype(f32)
    grad_heads = grad_heads.astype(bf16).reshape(shards, shard_rows, 4 * LANES)
    grad_heads = lax.all_to_all(grad_heads, both, 0, 0, tiled=True)
    grad_heads = grad_heads.reshape(dp_count, ctx_count, shard_rows, 4 * LANES).astype(f32)
    vector_grads = jnp.sum(grad_heads[..., 3 * LANES + 2 : 3 * LANES + 8], axis=(0, 1))
    from_own = lax.dynamic_slice_in_dim(grad_heads, core * near, near, 1)
    from_own = jnp.sum(from_own, axis=0)
    pieces = [[[] for _ in range(local_heads)] for _ in range(4)]
    used = [sorted({entry[0] for entry in tables[device].tolist()}) for device in range(near)]
    for device in range(near):
        for slot in used[device]:
            head = local_low[device] + slot
            for kind in range(3):
                at = kind * LANES + slot * HEAD
                pieces[kind][head].append(from_own[device, :, at : at + HEAD])
            at = 3 * LANES + slot
            pieces[3][head].append(from_own[device, :, at : at + 1])
    grad_query, grad_key, grad_value, grad_score = [
        jnp.concatenate([sum(terms[1:], terms[0]) for terms in kind], axis=1) for kind in pieces
    ]

    def both_micro(own):
        other = other_core(own)
        return jnp.where(core == 0, jnp.stack([own, other]), jnp.stack([other, own]))[:, None]

    return (
        both_micro(result),
        both_micro(tokens_grad),
        grad_query,
        grad_key,
        grad_value,
        grad_score,
        grad_packed[:, 2 * hidden :].T,
        grad_packed[:, :hidden],
        grad_packed[:, hidden : 2 * hidden].T,
        vector_grads[:, 0],
        vector_grads[:, 1],
        vector_grads[:, 2],
        vector_grads[:, 3],
        vector_grads[:, 4],
        fc_bias_grad,
        vector_grads[:, 5],
    )


def solution(mesh):
    rows, columns, vector = P(("dp", "ctx"), "tensor"), P("tensor", ("dp", "ctx")), P(("dp", "ctx"))
    tokens = P(None, "dp", "ctx", None)
    in_specs = (
        (tokens, P(None, "dp"))
        + (rows,) * 4
        + (columns, rows, columns)
        + (vector,) * 5
        + (P("tensor"), vector, tokens)
    )
    out_specs = (
        (tokens, tokens)
        + (rows,) * 4
        + (columns, rows, columns)
        + (vector,) * 5
        + (P("tensor"), vector)
    )
    return jax.shard_map(
        partial(on_device, dp_count=mesh.shape["dp"], ctx_count=mesh.shape["ctx"]),
        mesh=mesh,
        in_specs=in_specs,
        out_specs=out_specs,
        check_vma=False,
    )
```

```python
from functools import partial

import jax
import jax.numpy as jnp
import numpy as np
from jax import lax
from jax.experimental import pallas as pl
from jax.experimental.pallas import tpu as pltpu
from jax.sharding import PartitionSpec as P

WIN = 64
TOPK = 64
HEAD = 64
LANES = 128

norm_epsilon = 1e-05
search_steps = 24
search_bound = 64.0

CHUNK = 256
FAR = 1e9
OPEN_PIVOT = -1e6
NEWTON_TOLERANCE = 3e-3
SCORE_ROWS = 16
NT = (((1,), (1,)), ((), ()))


def over_chunks(first, last, prefix, body, carry):
    below = lax.div(jnp.maximum(first - (WIN - 1), 0), CHUNK)
    total = lax.div(jnp.maximum(last + 1, prefix) + CHUNK - 1, CHUNK)
    above = jnp.minimum(lax.div(last + WIN + CHUNK - 1, CHUNK), total)
    whole = jnp.maximum(lax.div(prefix, CHUNK), above)
    carry = lax.fori_loop(0, below, body(False), carry)
    carry = lax.fori_loop(below, above, body(True), carry)
    carry = lax.fori_loop(above, whole, body(False), carry)
    return lax.fori_loop(whole, total, body(True), carry)


def fold(values, how):
    while values.shape[0] > 8:
        half = values.shape[0] // 2
        values = how(values[:half], values[half:])
    return values


def own_head(values, slot):
    lane = lax.broadcasted_iota(jnp.int32, values.shape, 1)
    kept = jnp.where(lax.div(lane, HEAD) == slot, values.astype(jnp.float32), 0.0)
    return kept


def rows_of(first, shape, rows, block):
    lane = lax.broadcasted_iota(jnp.int32, shape, 1)
    return first + lax.div(lane, rows) * block + lax.rem(lane, rows)


def masks(start, first, prefix, rows, block, together):
    shape = (CHUNK, rows * together)
    key = lax.broadcasted_iota(jnp.int32, shape, 0)
    behind = rows_of(first - start, shape, rows, block) - key
    allowed = (behind >= 0) | (key < prefix - start)
    return allowed, allowed & (jnp.abs(behind) < WIN)


def spread_lanes(values, lanes):
    values = values.astype(jnp.float32)
    return jnp.concatenate([values] * (lanes // LANES), axis=1)


def turn(source_ref, lanes, target_ref):
    def run(chunk, _):
        here = pl.ds(pl.multiple_of(chunk * CHUNK, CHUNK), CHUNK)
        flipped = source_ref[here, lanes : lanes + LANES].astype(jnp.float32).T
        target_ref[:, here] = flipped.astype(jnp.bfloat16)
        return 0

    lax.fori_loop(0, source_ref.shape[0] // CHUNK, run, 0)


def forward_kernel(
    block, table, prefix_ref, p_ref, o_ref, low_ref, lse_ref, pivot_ref, sm_ref, st_ref, vt_ref
):
    unit_count, _, lanes = o_ref.shape
    rows = low_ref.shape[2]
    together = lanes // rows
    prefix = prefix_ref[0]
    turn(p_ref, 2 * LANES, vt_ref)

    def unit(step, guess):
        slot, first = table[step, 0], table[step, 1]
        last = first + (together - 1) * block + rows - 1
        query = jnp.concatenate(
            [
                p_ref[pl.ds(pl.multiple_of(first + at * block, rows), rows), 0:LANES]
                for at in range(together)
            ],
            axis=0,
        )
        query_t = own_head(query, slot).T.astype(jnp.bfloat16)
        score_lane = pl.multiple_of((3 + slot) * LANES, LANES)

        def build(masked):
            def run(chunk, top):
                start = pl.multiple_of(chunk * CHUNK, CHUNK)
                here = pl.ds(start, CHUNK)
                logits = jnp.dot(
                    p_ref[here, LANES : 2 * LANES], query_t, preferred_element_type=jnp.float32
                )
                score = spread_lanes(p_ref[here, pl.ds(score_lane, LANES)], lanes)
                if masked:
                    allowed, local = masks(start, first, prefix, rows, block, together)
                    logits = jnp.where(allowed, logits, -1e30)
                    score = jnp.where(local, FAR, jnp.where(allowed, score, -FAR))
                    top = jnp.maximum(top, fold(jnp.where(local, logits, -1e30), jnp.maximum))
                st_ref[here, :] = logits
                sm_ref[here, :] = score
                return top

            return run

        top = over_chunks(first, last, prefix, build, jnp.full((8, lanes), -1e30, jnp.float32))
        top = jnp.max(top, axis=0, keepdims=True)

        row = rows_of(first, (1, lanes), rows, block)
        local_count = (
            jnp.minimum(row, WIN - 1) + 1 + jnp.clip(prefix - 1 - row, 0, WIN - 1)
        ).astype(jnp.float32)
        candidates = jnp.maximum(row + 1, prefix).astype(jnp.float32) - local_count
        chunks = lax.div(jnp.maximum(last + 1, prefix) + CHUNK - 1, CHUNK)
        entries = (chunks * CHUNK).astype(jnp.float32)
        searched = candidates > TOPK
        count = jnp.maximum(candidates, TOPK + 1.0)
        goal = jnp.log(TOPK / (count - TOPK))

        def measure(half):
            def run(chunk, sums):
                bent = jnp.tanh(sm_ref[pl.ds(pl.multiple_of(chunk * CHUNK, CHUNK), CHUNK), :] - half)
                return sums[0] + fold(bent, jnp.add), sums[1] + fold(bent * bent, jnp.add)

            zero = jnp.zeros((8, lanes), jnp.float32)
            first_sum, second_sum = lax.fori_loop(0, chunks, run, (zero, zero))
            filled = 0.5 * (entries + jnp.sum(first_sum, axis=0, keepdims=True)) - local_count
            slope = 0.25 * (entries - jnp.sum(second_sum, axis=0, keepdims=True))
            return filled, slope

        def improve(state):
            turn, _, half, lower, upper, done = state
            filled, slope = measure(half)
            above = filled > TOPK
            lower = jnp.where(above, half, lower)
            upper = jnp.where(above, upper, half)
            newton = (filled - TOPK) / slope
            held = jnp.clip(filled, 1e-3, count - 1e-3)
            bent = (jnp.log(held / (count - held)) - goal) * (held * (count - held) / (count * slope))
            close = jnp.abs(newton) <= NEWTON_TOLERANCE
            following = half + 0.5 * jnp.where(close, newton, bent)
            inside = (following > lower) & (following < upper)
            halve = (turn >= 12) & (lax.rem(turn, 2) == 1)
            middle = 0.5 * (lower + upper)
            following = jnp.where(close | (inside & jnp.logical_not(halve)), following, middle)
            half = jnp.where(done > 0.0, half, following)
            done = jnp.where(close, 1.0, done)
            return turn + 1, jnp.min(done), half, lower, upper, done

        start_done = jnp.where(searched, 0.0, 1.0)
        bound = jnp.full((1, lanes), 0.5 * search_bound, jnp.float32)
        _, _, half, lower, upper, done = lax.while_loop(
            lambda state: (state[0] < 12 + 2 * search_steps) & (state[1] < 0.5),
            improve,
            (0, jnp.min(start_done), guess, -bound, bound, start_done),
        )
        half = jnp.where(done > 0.0, half, 0.5 * (lower + upper))
        pivot = jnp.where(searched, half, OPEN_PIVOT)

        def weigh(chunk, sums):
            here = pl.ds(pl.multiple_of(chunk * CHUNK, CHUNK), CHUNK)
            raised = jnp.exp(st_ref[here, :] - top)
            weight = raised / (1.0 + jnp.exp(2.0 * (pivot - sm_ref[here, :])))
            merged = sums[1] + jnp.dot(
                vt_ref[:, here], weight.astype(jnp.bfloat16), preferred_element_type=jnp.float32
            )
            return sums[0] + fold(weight, jnp.add), merged

        total, merged = lax.fori_loop(
            0,
            chunks,
            weigh,
            (jnp.zeros((8, lanes), jnp.float32), jnp.zeros((LANES, lanes), jnp.float32)),
        )
        total = jnp.sum(total, axis=0, keepdims=True)
        merged = merged / total
        own = jnp.where(slot == 0, merged[:HEAD], merged[HEAD:])
        o_ref[step] = own
        for at in range(together):
            low_ref[table[step, 2 + at]] = own[:, at * rows : (at + 1) * rows].astype(jnp.bfloat16)
        lse_ref[step] = top + jnp.log(total)
        pivot_ref[step] = pivot
        return jnp.where(searched, half, guess)

    lax.fori_loop(0, unit_count, unit, jnp.zeros((1, lanes), jnp.float32))


def backward_kernel(
    block,
    table,
    prefix_ref,
    p_ref,
    do_ref,
    o_ref,
    lse_ref,
    pivot_ref,
    message_ref,
    d_ref,
    score_ref,
    dq_ref,
    dk_ref,
    dv_ref,
    ds_ref,
    kt_ref,
):
    unit_count, _, lanes = o_ref.shape
    rows = do_ref.shape[2]
    together = lanes // rows
    length = p_ref.shape[0]
    prefix = prefix_ref[0]
    turn(p_ref, LANES, kt_ref)

    def clear(chunk, _):
        here = pl.ds(pl.multiple_of(chunk * CHUNK, CHUNK), CHUNK)
        for ref in (dq_ref, dk_ref, dv_ref):
            ref[here, :] = jnp.zeros((CHUNK, LANES), jnp.float32)
        for slot in range(2):
            ds_ref[slot, here, :] = jnp.zeros((CHUNK, lanes), jnp.float32)
        return 0

    lax.fori_loop(0, length // CHUNK, clear, 0)

    def unit(step, _):
        slot, first = table[step, 0], table[step, 1]
        last = first + (together - 1) * block + rows - 1
        whose = [pl.ds(pl.multiple_of(first + at * block, rows), rows) for at in range(together)]
        query = own_head(jnp.concatenate([p_ref[here, 0:LANES] for here in whose], axis=0), slot)
        query_t = query.T.astype(jnp.bfloat16)
        query = query.astype(jnp.bfloat16)
        grad = jnp.concatenate([do_ref[table[step, 2 + at]] for at in range(together)], axis=1)
        grad = grad.astype(jnp.float32)
        row_dot = jnp.sum(grad * o_ref[step], axis=0, keepdims=True)
        empty = jnp.zeros_like(grad)
        grad = jnp.where(
            slot == 0,
            jnp.concatenate([grad, empty], axis=0),
            jnp.concatenate([empty, grad], axis=0),
        )
        grad_t = grad.T.astype(jnp.bfloat16)
        grad = grad.astype(jnp.bfloat16)
        lse, pivot = lse_ref[step], pivot_ref[step]
        score_lane = pl.multiple_of((3 + slot) * LANES, LANES)

        def body(masked):
            def run(chunk, grad_query):
                start = pl.multiple_of(chunk * CHUNK, CHUNK)
                here = pl.ds(start, CHUNK)
                logits = jnp.dot(
                    p_ref[here, LANES : 2 * LANES], query_t, preferred_element_type=jnp.float32
                )
                grad_probs = jnp.dot(
                    p_ref[here, 2 * LANES : 3 * LANES], grad, preferred_element_type=jnp.float32
                )
                score = spread_lanes(p_ref[here, pl.ds(score_lane, LANES)], lanes)
                if masked:
                    allowed, local = masks(start, first, prefix, rows, block, together)
                    logits = jnp.where(allowed, logits, -1e30)
                    score = jnp.where(local, FAR, jnp.where(allowed, score, -FAR))
                unit_probs = jnp.exp(logits - lse)
                gate = 1.0 / (1.0 + jnp.exp(2.0 * (pivot - score)))
                probs = gate * unit_probs
                grad_logits = probs * (grad_probs - row_dot)
                ds_ref[slot, here, :] += grad_logits * (1.0 - gate)
                low = grad_logits.astype(jnp.bfloat16)
                dk_ref[here, :] += jnp.dot(low, query, preferred_element_type=jnp.float32)
                dv_ref[here, :] += jnp.dot(
                    probs.astype(jnp.bfloat16), grad_t, preferred_element_type=jnp.float32
                )
                return grad_query + jnp.dot(
                    kt_ref[:, here], low, preferred_element_type=jnp.float32
                )

            return run

        grad_query = over_chunks(
            first, last, prefix, body, jnp.zeros((LANES, lanes), jnp.float32)
        ).T
        lane = lax.broadcasted_iota(jnp.int32, grad_query.shape, 1)
        grad_query = jnp.where(lax.div(lane, HEAD) == slot, grad_query, 0.0)
        for at, here in enumerate(whose):
            dq_ref[here, :] += grad_query[at * rows : (at + 1) * rows]
        return 0

    lax.fori_loop(0, unit_count, unit, 0)

    def finish(chunk, _):
        here = pl.ds(pl.multiple_of(chunk * CHUNK, CHUNK), CHUNK)
        lane = lax.broadcasted_iota(jnp.int32, (CHUNK, LANES), 1)
        columns = [jnp.sum(ds_ref[slot, here, :], axis=1, keepdims=True) for slot in range(2)]
        grad_score = jnp.where(lane == 0, columns[0], jnp.where(lane == 1, columns[1], 0.0))
        grad_score = grad_score.T[:SCORE_ROWS].astype(jnp.bfloat16)
        score_ref[:, here] = grad_score
        message_ref[chunk, CHUNK:, 0:CHUNK] = grad_score
        message_ref[chunk, CHUNK:, CHUNK:] = jnp.zeros_like(message_ref[chunk, CHUNK:, CHUNK:])
        grads = (dq_ref[here, :] * HEAD**-0.5, dk_ref[here, :], dv_ref[here, :])
        for kind, grad in enumerate(grads):
            low = grad.astype(jnp.bfloat16)
            d_ref[here, kind * LANES : (kind + 1) * LANES] = low
            message_ref[chunk, 0:CHUNK, kind * LANES : (kind + 1) * LANES] = low
        return 0

    lax.fori_loop(0, length // CHUNK, finish, 0)


VMEM_LIMIT = 48 * 1024 * 1024


def kernel_params():
    return pltpu.CompilerParams(vmem_limit_bytes=VMEM_LIMIT)


def in_vmem():
    return pl.BlockSpec(memory_space=pltpu.VMEM)


def in_smem():
    return pl.BlockSpec(memory_space=pltpu.SMEM)


def attend(table, prefix, projected, rows, block):
    unit_count = table.shape[0]
    together = table.shape[1] - 2
    lanes = rows * together
    length = projected.shape[0]
    pairs = unit_count * lanes * length
    return pl.pallas_call(
        partial(forward_kernel, block),
        out_shape=(
            jax.ShapeDtypeStruct((unit_count, HEAD, lanes), jnp.float32),
            jax.ShapeDtypeStruct((unit_count * together, HEAD, rows), jnp.bfloat16),
            jax.ShapeDtypeStruct((unit_count, 1, lanes), jnp.float32),
            jax.ShapeDtypeStruct((unit_count, 1, lanes), jnp.float32),
        ),
        in_specs=[in_smem(), in_smem(), in_vmem()],
        out_specs=(in_vmem(),) * 4,
        scratch_shapes=[
            pltpu.VMEM((length, lanes), jnp.float32),
            pltpu.VMEM((length, lanes), jnp.float32),
            pltpu.VMEM((LANES, length), jnp.bfloat16),
        ],
        compiler_params=kernel_params(),
        cost_estimate=pl.CostEstimate(
            flops=pairs * 12000, bytes_accessed=projected.size * 4, transcendentals=pairs * 8
        ),
        name="attend",
    )(table, prefix, projected)


def attend_back(table, prefix, projected, grads, attended, log_totals, pivots, block):
    unit_count, _, lanes = attended.shape
    length = projected.shape[0]
    pairs = unit_count * lanes * length
    return pl.pallas_call(
        partial(backward_kernel, block),
        out_shape=(
            jax.ShapeDtypeStruct((length // CHUNK, CHUNK + SCORE_ROWS, 3 * LANES), jnp.bfloat16),
            jax.ShapeDtypeStruct((length, 3 * LANES), jnp.bfloat16),
            jax.ShapeDtypeStruct((SCORE_ROWS, length), jnp.bfloat16),
        ),
        in_specs=[in_smem(), in_smem()] + [in_vmem()] * 5,
        out_specs=(in_vmem(),) * 3,
        scratch_shapes=[
            pltpu.VMEM((length, LANES), jnp.float32),
            pltpu.VMEM((length, LANES), jnp.float32),
            pltpu.VMEM((length, LANES), jnp.float32),
            pltpu.VMEM((2, length, lanes), jnp.float32),
            pltpu.VMEM((LANES, length), jnp.bfloat16),
        ],
        compiler_params=kernel_params(),
        cost_estimate=pl.CostEstimate(
            flops=pairs * 9000, bytes_accessed=projected.size * 4, transcendentals=pairs * 3
        ),
        name="attend_back",
    )(table, prefix, projected, grads, attended, log_totals, pivots)


def project_kernel(count, offset, *refs):
    tokens, (gain_ref, shift_ref, weight_ref, _, __, normed_ref, projected_ref) = refs[:count], refs[count:]
    for step, tokens_ref in enumerate(tokens):

        @pl.when(pl.program_id(0) == step)
        def _(tokens_ref=tokens_ref):
            hat, _ = normalize(tokens_ref[...].astype(jnp.float32))
            normed = (hat * gain_ref[...] + shift_ref[...]).astype(jnp.bfloat16)
            normed_ref[...] = normed
            low = jnp.dot(normed, weight_ref[...], preferred_element_type=jnp.float32)
            low = low.astype(jnp.bfloat16).astype(jnp.float32)
            lane = lax.broadcasted_iota(jnp.int32, low.shape, 1)
            projected_ref[...] = jnp.where(lane < 3 * LANES, low, 0.5 * low).astype(jnp.bfloat16)


def project(places, tokens, gain, shift, weight, normed, projected):
    count = len(tokens)
    rows, width = tokens[0].shape
    columns = weight.shape[1]

    def whole(shape):
        return pl.BlockSpec(shape, lambda i, at: (0, 0))

    anywhere = pl.BlockSpec(memory_space=pl.ANY)
    return pl.pallas_call(
        partial(project_kernel, count),
        grid_spec=pltpu.PrefetchScalarGridSpec(
            num_scalar_prefetch=1,
            grid=(count,),
            in_specs=[whole((rows, width))] * count
            + [whole((1, width)), whole((1, width)), whole((width, columns)), anywhere, anywhere],
            out_specs=(
                pl.BlockSpec((rows, width), lambda i, at: (at[i], 0)),
                pl.BlockSpec((rows, columns), lambda i, at: (at[i], 0)),
            ),
        ),
        out_shape=(
            jax.ShapeDtypeStruct(normed.shape, normed.dtype),
            jax.ShapeDtypeStruct(projected.shape, projected.dtype),
        ),
        input_output_aliases={count + 4: 0, count + 5: 1},
        compiler_params=kernel_params(),
        cost_estimate=pl.CostEstimate(
            flops=2 * count * rows * width * columns * 20,
            bytes_accessed=rows * width * 12,
            transcendentals=0,
        ),
        name="project",
    )(jnp.stack(places).astype(jnp.int32), *tokens, gain, shift, weight, normed, projected)


def pack_kernel(pairs, vector_ref, query_ref, key_ref, value_ref, score_ref, out_ref):
    rows = query_ref.shape[0]
    spare = vector_ref[...].astype(jnp.float32).T[:rows]
    lane = lax.broadcasted_iota(jnp.int32, spare.shape, 1)
    for pattern, heads in enumerate(pairs):
        tail = spare
        for slot, head in enumerate(heads):
            score = score_ref[:, head : head + 1].astype(jnp.float32)
            tail = jnp.where(lane == slot, score, tail)
        for kind, ref in enumerate((query_ref, key_ref, value_ref)):
            pair = jnp.concatenate([ref[:, h * HEAD : (h + 1) * HEAD] for h in heads], axis=1)
            for copy in range(pattern, out_ref.shape[0], len(pairs)):
                out_ref[copy, :, kind * LANES : (kind + 1) * LANES] = pair
        for copy in range(pattern, out_ref.shape[0], len(pairs)):
            out_ref[copy, :, 3 * LANES :] = tail.astype(jnp.bfloat16)


def pack_heads(copies, pairs, vectors, query, key, value, score):
    return pl.pallas_call(
        partial(pack_kernel, pairs),
        out_shape=jax.ShapeDtypeStruct((copies, query.shape[0], 4 * LANES), jnp.bfloat16),
        in_specs=[in_vmem()] * 5,
        out_specs=in_vmem(),
        compiler_params=kernel_params(),
        name="pack_heads",
    )(jnp.pad(vectors, ((2, LANES - 2 - vectors.shape[0]), (0, LANES - vectors.shape[1]))), query, key, value, score)


def unpack_kernel(
    near, owners, first, arrived_ref, query_ref, key_ref, value_ref, score_ref, vector_ref, bias_ref
):
    rows = query_ref.shape[0]
    kinds = (query_ref, key_ref, value_ref)
    sources = [arrived_ref[first[0] + device].astype(jnp.float32) for device in range(near)]
    lane = lax.broadcasted_iota(jnp.int32, (rows, LANES), 1)
    scores = jnp.zeros((rows, LANES), jnp.float32)
    for head, terms in enumerate(owners):
        for kind, ref in enumerate(kinds):
            at = [kind * LANES + slot * HEAD for _, slot in terms]
            parts = [sources[d][:rows, a : a + HEAD] for (d, _), a in zip(terms, at)]
            ref[:, head * HEAD : (head + 1) * HEAD] = sum(parts[1:], parts[0])
        parts = [sources[d][:rows, 3 * LANES + slot : 3 * LANES + slot + 1] for d, slot in terms]
        scores = jnp.where(lane == head, sum(parts[1:], parts[0]), scores)
    score_ref[...] = scores[:, : score_ref.shape[1]]
    total = arrived_ref[0].astype(jnp.float32)
    for device in range(1, arrived_ref.shape[0]):
        total = total + arrived_ref[device].astype(jnp.float32)
    tail = jnp.concatenate([total[:rows, 3 * LANES :], jnp.zeros((LANES - rows, LANES), jnp.float32)], axis=0)
    vector_ref[...] = tail.T[:8, :rows]
    bias_ref[...] = total[rows:]


def unpack_heads(near, owners, first, arrived, heads, hidden):
    sources, rows, lanes = arrived.shape
    rows = rows - SCORE_ROWS
    shapes = [(rows, heads * HEAD)] * 3 + [(rows, heads), (8, rows), (SCORE_ROWS, lanes)]
    return pl.pallas_call(
        partial(unpack_kernel, near, owners),
        out_shape=[jax.ShapeDtypeStruct(shape, jnp.float32) for shape in shapes],
        in_specs=[in_smem(), in_vmem()],
        out_specs=[in_vmem()] * 6,
        compiler_params=kernel_params(),
        name="unpack_heads",
    )(first, arrived)


def finish_kernel(pairs, arrived_ref, halves_ref, tokens_ref, middle_ref, gain_ref, out_ref):
    rows, width = tokens_ref.shape
    near = len(pairs)
    half = width // 2
    total = jnp.zeros((rows, width), jnp.float32)
    for device in range(arrived_ref.shape[0]):
        heads = pairs[device % near]
        side = device // near
        weight = jnp.concatenate(
            [
                halves_ref[side, :, kind * half + head * HEAD : kind * half + (head + 1) * HEAD]
                for kind in range(3)
                for head in heads
            ],
            axis=1,
        )
        total += lax.dot_general(
            arrived_ref[device, :rows], weight, NT, preferred_element_type=jnp.float32
        )
        at = 3 * half
        lane = lax.broadcasted_iota(jnp.int32, (width, SCORE_ROWS), 1)
        columns = [halves_ref[side, :, at + head : at + head + 1].astype(jnp.float32) for head in heads]
        weight = jnp.where(lane == 0, columns[0], jnp.where(lane == 1, columns[1], 0.0))
        grads = arrived_ref[device, rows:, :rows].astype(jnp.float32).T
        total += lax.dot_general(
            grads.astype(jnp.bfloat16), weight.astype(jnp.bfloat16), NT, preferred_element_type=jnp.float32
        )
    hat, scale = normalize(tokens_ref[...].astype(jnp.float32))
    out_ref[...] = middle_ref[...] + normalize_back(total, hat, scale, gain_ref[...])


def finish_tokens(pairs, arrived, halves, tokens, grad_middle, gain):
    return pl.pallas_call(
        partial(finish_kernel, pairs),
        out_shape=jax.ShapeDtypeStruct(grad_middle.shape, jnp.float32),
        in_specs=[in_vmem()] * 5,
        out_specs=in_vmem(),
        compiler_params=kernel_params(),
        name="finish_tokens",
    )(arrived, halves, tokens, grad_middle, gain)


def ring_order(count):
    deep = 4 if count % 4 == 0 else 1
    wide = count // deep
    if deep == 1 or wide == 1:
        return list(range(count))
    walk = []
    for place in range(deep):
        across = range(1, wide) if place % 2 == 0 else range(wide - 1, 0, -1)
        walk += [place * wide + at for at in across]
    return walk + [place * wide for place in reversed(range(deep))]


def ring_gather(values, order):
    count = len(order)
    spot = jnp.asarray(np.argsort(order), jnp.int32)[lax.axis_index("ctx")]
    forward = [(order[i], order[(i + 1) % count]) for i in range(count)]
    backward = [(receiver, sender) for sender, receiver in forward]
    held = {0: values}
    for step in range(1, count // 2 + 1):
        held[-step] = lax.ppermute(held[1 - step], "ctx", forward)
        if step < count - step:
            held[step] = lax.ppermute(held[step - 1], "ctx", backward)
    walk = jnp.asarray(order, jnp.int32)
    return {distance: (walk[(spot + distance) % count], block) for distance, block in held.items()}


def other_core(values):
    return lax.ppermute(values, "tensor", [(0, 1), (1, 0)])


def normalize(values):
    centred = values - jnp.mean(values, axis=-1, keepdims=True)
    scale = lax.rsqrt(jnp.mean(centred * centred, axis=-1, keepdims=True) + norm_epsilon)
    return centred * scale, scale


def normalize_back(grad, hat, scale, gain):
    scaled = grad * gain
    return scale * (
        scaled
        - jnp.mean(scaled, axis=-1, keepdims=True)
        - hat * jnp.mean(scaled * hat, axis=-1, keepdims=True)
    )


def head_plan(ctx_count, head_count, block):
    parts = 1
    while head_count * parts % ctx_count:
        parts += 1
    share = head_count * parts // ctx_count
    rows = block // parts
    lows, tables = [], []
    for device in range(ctx_count):
        pieces = range(share * device, share * (device + 1))
        lows.append(pieces[0] // parts)
        tables.append(
            [
                (piece // parts - lows[-1], at * block + (piece % parts) * rows)
                + tuple((at + more) * share + order for more in range(parts))
                for order, piece in enumerate(pieces)
                for at in range(0, ctx_count, parts)
            ]
        )
        assert all(entry[0] in (0, 1) for entry in tables[-1])
    assert ctx_count % parts == 0
    return parts, share, rows, lows, np.asarray(tables, np.int32)


def on_device(
    tokens,
    prefix,
    w_query,
    w_key,
    w_value,
    w_score,
    w_attn_out,
    w_fc,
    w_proj,
    ln1_gain,
    ln1_bias,
    ln2_gain,
    ln2_bias,
    attn_bias,
    fc_bias,
    proj_bias,
    cotangent,
    dp_count,
    ctx_count,
):
    f32, bf16 = jnp.float32, jnp.bfloat16
    micro_count, seq_count, block, width = tokens.shape
    local_heads = w_score.shape[1]
    head_count = 2 * local_heads
    assert micro_count == 2 and seq_count == 1
    core = lax.axis_index("tensor")
    me = lax.axis_index("ctx")
    both = ("dp", "ctx")
    shards = dp_count * ctx_count
    shard_rows = width // shards
    parts, share, rows, lows, tables = head_plan(ctx_count, head_count, block)
    near = ctx_count // 2
    local_low = [low % local_heads for low in lows[:near]]
    local_high = [min(low + 1, local_heads - 1) for low in local_low]

    own_tokens = lax.dynamic_index_in_dim(tokens, core, 0, keepdims=False)[0]
    own_cot = lax.dynamic_index_in_dim(cotangent, core, 0, keepdims=False)[0]
    other_cot = lax.dynamic_index_in_dim(cotangent, 1 - core, 0, keepdims=False)[0]
    own_prefix = lax.dynamic_index_in_dim(prefix, core, 0, keepdims=False)
    table = jnp.asarray(tables)[me]

    blocks = ring_gather(own_tokens, ring_order(ctx_count))

    def columns(weight, head):
        return weight[:, head * HEAD : (head + 1) * HEAD]

    vectors = jnp.stack([ln1_gain, ln1_bias, ln2_gain, ln2_bias, attn_bias, proj_bias])
    pairs = tuple(zip(local_low, local_high))
    outgoing = pack_heads(shards, pairs, vectors, w_query, w_key, w_value, w_score)
    if ctx_count >= 6:
        outgoing, *_ = lax.optimization_barrier((outgoing, blocks[-1][1], blocks[1][1]))
    head_weights = lax.all_to_all(outgoing, both, 0, 0, tiled=True).reshape(width, 4 * LANES)
    if ctx_count >= 6:
        head_weights, *_ = lax.optimization_barrier((head_weights, blocks[-2][1], blocks[2][1]))
    from_half = (me >= near).astype(jnp.int32)
    head_weights = jnp.where(from_half == core, head_weights, other_core(head_weights))
    gains = head_weights[:, 3 * LANES + 2 : 3 * LANES + 8].astype(f32).T
    gain_one, shift_one, gain_two, shift_two, attn_shift, proj_shift = [gains[i : i + 1] for i in range(6)]

    score_columns = head_weights[:, 3 * LANES : 3 * LANES + 2]
    wide_weights = jnp.concatenate(
        [head_weights[:, :LANES] * HEAD**-0.5, head_weights[:, LANES : 3 * LANES]]
        + [jnp.broadcast_to(score_columns[:, i : i + 1], (width, LANES)) for i in range(2)],
        axis=1,
    )
    length = ctx_count * block
    normed = jnp.zeros((length, width), bf16)
    projected = jnp.zeros((length, 5 * LANES), bf16)
    near_first = sorted(blocks, key=lambda distance: (abs(distance), distance))
    batches = [near_first[: ctx_count - 3], near_first[ctx_count - 3 :]]
    for batch in batches:
        normed, projected = project(
            [blocks[d][0] for d in batch],
            [blocks[d][1] for d in batch],
            gain_one,
            shift_one,
            wide_weights,
            normed,
            projected,
        )

    packed = jnp.concatenate(
        [w_fc, w_proj.T, w_attn_out.T, w_query, w_key, w_value, w_score, jnp.zeros((shard_rows, LANES - local_heads), bf16)],
        axis=1,
    )
    packed, projected = lax.optimization_barrier((packed, projected))
    packed = lax.all_gather(packed, both, axis=0, tiled=True)
    attended, attended_low, log_totals, pivots = attend(table, own_prefix, projected, rows, block)
    packed, _ = lax.optimization_barrier((packed, log_totals))
    hidden = w_fc.shape[1]
    full_fc, full_proj_t = packed[:, :hidden], packed[:, hidden : 2 * hidden]
    half_out_t = packed[:, 2 * hidden : 2 * hidden + width // 2]
    half_heads = packed[:, 2 * hidden + width // 2 :]
    other_out_t, other_heads = other_core(half_out_t), other_core(half_heads)
    out_t = jnp.where(
        core == 0,
        jnp.concatenate([half_out_t, other_out_t], axis=1),
        jnp.concatenate([other_out_t, half_out_t], axis=1),
    )

    sent = attended_low.reshape(ctx_count, share * HEAD, rows)
    merged = lax.all_to_all(sent, "ctx", 0, 0, tiled=True)
    merged = merged.reshape(head_count, parts, HEAD, rows).transpose(0, 2, 1, 3).reshape(width, block)

    own_block = own_tokens.astype(f32)
    attn = lax.dot_general(merged, out_t, (((0,), (1,)), ((), ())), preferred_element_type=f32)
    middle = own_block + attn + attn_shift
    hat_two, scale_two = normalize(middle)
    normed_two = (hat_two * gain_two + shift_two).astype(bf16)
    normed_two = jnp.concatenate([normed_two, other_core(normed_two)])
    hidden_pre = jnp.dot(normed_two, full_fc, preferred_element_type=f32) + fc_bias.astype(f32)
    active, pull_gelu = jax.vjp(partial(jax.nn.gelu, approximate=True), hidden_pre)
    active = active.astype(bf16)
    mlp = lax.dot_general(active, full_proj_t, NT, preferred_element_type=f32)
    result = middle + mlp[:block] + other_core(mlp[block:].astype(bf16)).astype(f32) + proj_shift
    result = result.astype(bf16)

    both_cot = jnp.concatenate([own_cot, other_cot])
    grad_active = jnp.dot(both_cot, full_proj_t, preferred_element_type=f32)
    grad_pre = pull_gelu(grad_active)[0].astype(bf16)
    grad_two = lax.dot_general(grad_pre, full_fc, NT, preferred_element_type=f32)
    grad_two = grad_two[:block] + other_core(grad_two[block:].astype(bf16)).astype(f32)
    cot = own_cot.astype(f32)
    grad_middle = cot + normalize_back(grad_two, hat_two, scale_two, gain_two)
    grad_middle_low = grad_middle.astype(bf16)
    grad_merged = lax.dot_general(
        out_t, grad_middle_low, (((0,), (1,)), ((), ())), preferred_element_type=f32
    ).astype(bf16)
    sent = grad_merged.reshape(head_count, HEAD, parts, rows).transpose(0, 2, 1, 3)
    sent = sent.reshape(ctx_count, share * HEAD, rows)
    grad_attended = lax.all_to_all(sent, "ctx", 0, 0, tiled=True).reshape(attended_low.shape)

    grad_fc = lax.dot_general(normed_two, grad_pre, (((0,), (0,)), ((), ())), preferred_element_type=f32)
    grad_proj_t = lax.dot_general(both_cot, active, (((0,), (0,)), ((), ())), preferred_element_type=f32)
    grad_out_t = lax.dot_general(
        grad_middle_low, merged, (((0,), (1,)), ((), ())), preferred_element_type=f32
    ).astype(bf16)
    half_width = width // 2
    mine, theirs = grad_out_t[:, :half_width], grad_out_t[:, half_width:]
    mine, theirs = jnp.where(core == 0, mine, theirs), jnp.where(core == 0, theirs, mine)
    grad_out_t = (mine.astype(f32) + other_core(theirs).astype(f32)).astype(bf16)
    grad_packed = jnp.concatenate([grad_fc.astype(bf16), grad_proj_t.astype(bf16), grad_out_t], axis=1)
    grad_packed = lax.psum_scatter(grad_packed, both, scatter_dimension=0, tiled=True).astype(f32)

    message, grads, grad_scores = attend_back(
        table, own_prefix, projected, grad_attended, attended, log_totals, pivots, block
    )

    arrived = lax.all_to_all(message, "ctx", 0, 0, tiled=True)
    half_heads, other_heads, grads = lax.optimization_barrier((half_heads, other_heads, grads))
    halves = jnp.where(
        core == 0, jnp.stack([half_heads, other_heads]), jnp.stack([other_heads, half_heads])
    )
    tokens_grad = finish_tokens(pairs, arrived, halves, own_tokens, grad_middle, gain_one)

    grad_normed = lax.dot_general(grads, head_weights[:, : 3 * LANES], NT, preferred_element_type=f32)
    grad_normed = grad_normed + lax.dot_general(
        grad_scores[:2], score_columns, (((0,), (1,)), ((), ())), preferred_element_type=f32
    )
    hat_one = (normed.astype(f32) - shift_one) / gain_one

    grad_vectors = jnp.stack(
        [
            jnp.sum(grad_normed * hat_one, axis=0),
            jnp.sum(grad_normed, axis=0),
            jnp.sum(grad_two * hat_two, axis=0),
            jnp.sum(grad_two, axis=0),
            jnp.sum(grad_middle, axis=0),
            jnp.sum(cot, axis=0),
        ],
        axis=1,
    )
    over_rows = (((0,), (0,)), ((), ()))
    grad_heads = lax.dot_general(normed, grads, over_rows, preferred_element_type=f32)
    grad_columns = lax.dot_general(normed, grad_scores[:2], (((0,), (1,)), ((), ())), preferred_element_type=f32)
    spare = jnp.zeros((width, LANES - 8), f32)
    grad_heads = jnp.concatenate([grad_heads, grad_columns, grad_vectors, spare], axis=1)
    grad_heads = grad_heads + other_core(grad_heads.astype(bf16)).astype(f32)
    bias = jnp.sum(grad_pre.astype(f32), axis=0).reshape(hidden // (4 * LANES), 4 * LANES)
    bias = jnp.pad(bias, ((0, SCORE_ROWS - bias.shape[0]), (0, 0)))
    grad_heads = jnp.concatenate(
        [
            grad_heads.reshape(dp_count, ctx_count, shard_rows, 4 * LANES),
            jnp.broadcast_to(bias, (dp_count, ctx_count) + bias.shape),
        ],
        axis=2,
    ).astype(bf16)
    where = lax.axis_index("dp")
    summed = lax.dynamic_index_in_dim(grad_heads, where, 0, keepdims=False).astype(f32)
    for shift in range(1, dp_count):
        sent = lax.dynamic_index_in_dim(grad_heads, (where + shift) % dp_count, 0, keepdims=False)
        summed = summed + lax.ppermute(
            sent, "dp", [(i, (i + shift) % dp_count) for i in range(dp_count)]
        ).astype(f32)
    arrived = lax.all_to_all(summed.astype(bf16), "ctx", 0, 0, tiled=True)
    owners = [[] for _ in range(local_heads)]
    for device in range(near):
        for slot in sorted({entry[0] for entry in tables[device].tolist()}):
            owners[local_low[device] + slot].append((device, slot))
    grad_query, grad_key, grad_value, grad_score, vector_grads, fc_bias_grad = unpack_heads(
        near, owners, (core * near).astype(jnp.int32)[None], arrived, local_heads, hidden
    )
    vector_grads = vector_grads[2:].T
    fc_bias_grad = fc_bias_grad[: hidden // (4 * LANES)].reshape(hidden)

    def both_micro(own):
        other = other_core(own)
        return jnp.where(core == 0, jnp.stack([own, other]), jnp.stack([other, own]))[:, None]

    return (
        both_micro(result),
        both_micro(tokens_grad),
        grad_query,
        grad_key,
        grad_value,
        grad_score,
        grad_packed[:, 2 * hidden :].T,
        grad_packed[:, :hidden],
        grad_packed[:, hidden : 2 * hidden].T,
        vector_grads[:, 0],
        vector_grads[:, 1],
        vector_grads[:, 2],
        vector_grads[:, 3],
        vector_grads[:, 4],
        fc_bias_grad,
        vector_grads[:, 5],
    )


def solution(mesh):
    rows, columns, vector = P(("dp", "ctx"), "tensor"), P("tensor", ("dp", "ctx")), P(("dp", "ctx"))
    tokens = P(None, "dp", "ctx", None)
    in_specs = (
        (tokens, P(None, "dp"))
        + (rows,) * 4
        + (columns, rows, columns)
        + (vector,) * 5
        + (P("tensor"), vector, tokens)
    )
    out_specs = (
        (tokens, tokens)
        + (rows,) * 4
        + (columns, rows, columns)
        + (vector,) * 5
        + (P("tensor"), vector)
    )
    return jax.shard_map(
        partial(on_device, dp_count=mesh.shape["dp"], ctx_count=mesh.shape["ctx"]),
        mesh=mesh,
        in_specs=in_specs,
        out_specs=out_specs,
        check_vma=False,
    )
```

```python
from functools import partial

import jax
import jax.numpy as jnp
import numpy as np
from jax import lax
from jax.experimental import pallas as pl
from jax.experimental.pallas import tpu as pltpu
from jax.sharding import PartitionSpec as P

WIN = 64
TOPK = 64
HEAD = 64
LANES = 128

norm_epsilon = 1e-05
search_steps = 24
search_bound = 64.0

CHUNK = 256
FAR = 1e9
OPEN_PIVOT = -1e6
NEWTON_TOLERANCE = 3e-3
SCORE_ROWS = 16
NT = (((1,), (1,)), ((), ()))


def over_chunks(first, last, prefix, body, carry):
    below = lax.div(jnp.maximum(first - (WIN - 1), 0), CHUNK)
    total = lax.div(jnp.maximum(last + 1, prefix) + CHUNK - 1, CHUNK)
    above = jnp.minimum(lax.div(last + WIN + CHUNK - 1, CHUNK), total)
    whole = jnp.maximum(lax.div(prefix, CHUNK), above)
    carry = lax.fori_loop(0, below, body(False), carry)
    carry = lax.fori_loop(below, above, body(True), carry)
    carry = lax.fori_loop(above, whole, body(False), carry)
    return lax.fori_loop(whole, total, body(True), carry)


def fold(values, how):
    while values.shape[0] > 8:
        half = values.shape[0] // 2
        values = how(values[:half], values[half:])
    return values


def own_head(values, slot):
    lane = lax.broadcasted_iota(jnp.int32, values.shape, 1)
    kept = jnp.where(lax.div(lane, HEAD) == slot, values.astype(jnp.float32), 0.0)
    return kept


def rows_of(first, shape, rows, block):
    lane = lax.broadcasted_iota(jnp.int32, shape, 1)
    return first + lax.div(lane, rows) * block + lax.rem(lane, rows)


def masks(start, first, prefix, rows, block, together):
    shape = (CHUNK, rows * together)
    key = lax.broadcasted_iota(jnp.int32, shape, 0)
    behind = rows_of(first - start, shape, rows, block) - key
    allowed = (behind >= 0) | (key < prefix - start)
    return allowed, allowed & (jnp.abs(behind) < WIN)


def spread_lanes(values, lanes):
    values = values.astype(jnp.float32)
    return jnp.concatenate([values] * (lanes // LANES), axis=1)


def turn(source_ref, lanes, target_ref):
    def run(chunk, _):
        here = pl.ds(pl.multiple_of(chunk * CHUNK, CHUNK), CHUNK)
        flipped = source_ref[here, lanes : lanes + LANES].astype(jnp.float32).T
        target_ref[:, here] = flipped.astype(jnp.bfloat16)
        return 0

    lax.fori_loop(0, source_ref.shape[0] // CHUNK, run, 0)


def forward_kernel(
    block, table, prefix_ref, p_ref, o_ref, low_ref, lse_ref, pivot_ref, sm_ref, st_ref, vt_ref
):
    unit_count, _, lanes = o_ref.shape
    rows = low_ref.shape[2]
    together = lanes // rows
    prefix = prefix_ref[0]
    turn(p_ref, 2 * LANES, vt_ref)

    def unit(step, guess):
        slot, first = table[step, 0], table[step, 1]
        last = first + (together - 1) * block + rows - 1
        query = jnp.concatenate(
            [
                p_ref[pl.ds(pl.multiple_of(first + at * block, rows), rows), 0:LANES]
                for at in range(together)
            ],
            axis=0,
        )
        query_t = own_head(query, slot).T.astype(jnp.bfloat16)
        score_lane = pl.multiple_of((3 + slot) * LANES, LANES)

        def build(masked):
            def run(chunk, top):
                start = pl.multiple_of(chunk * CHUNK, CHUNK)
                here = pl.ds(start, CHUNK)
                logits = jnp.dot(
                    p_ref[here, LANES : 2 * LANES], query_t, preferred_element_type=jnp.float32
                )
                score = spread_lanes(p_ref[here, pl.ds(score_lane, LANES)], lanes)
                if masked:
                    allowed, local = masks(start, first, prefix, rows, block, together)
                    logits = jnp.where(allowed, logits, -1e30)
                    score = jnp.where(local, FAR, jnp.where(allowed, score, -FAR))
                    top = jnp.maximum(top, fold(jnp.where(local, logits, -1e30), jnp.maximum))
                st_ref[here, :] = logits
                sm_ref[here, :] = score
                return top

            return run

        top = over_chunks(first, last, prefix, build, jnp.full((8, lanes), -1e30, jnp.float32))
        top = jnp.max(top, axis=0, keepdims=True)

        row = rows_of(first, (1, lanes), rows, block)
        local_count = (
            jnp.minimum(row, WIN - 1) + 1 + jnp.clip(prefix - 1 - row, 0, WIN - 1)
        ).astype(jnp.float32)
        candidates = jnp.maximum(row + 1, prefix).astype(jnp.float32) - local_count
        chunks = lax.div(jnp.maximum(last + 1, prefix) + CHUNK - 1, CHUNK)
        entries = (chunks * CHUNK).astype(jnp.float32)
        searched = candidates > TOPK
        count = jnp.maximum(candidates, TOPK + 1.0)
        goal = jnp.log(TOPK / (count - TOPK))

        def measure(half):
            def run(chunk, sums):
                bent = jnp.tanh(sm_ref[pl.ds(pl.multiple_of(chunk * CHUNK, CHUNK), CHUNK), :] - half)
                return sums[0] + fold(bent, jnp.add), sums[1] + fold(bent * bent, jnp.add)

            zero = jnp.zeros((8, lanes), jnp.float32)
            first_sum, second_sum = lax.fori_loop(0, chunks, run, (zero, zero))
            filled = 0.5 * (entries + jnp.sum(first_sum, axis=0, keepdims=True)) - local_count
            slope = 0.25 * (entries - jnp.sum(second_sum, axis=0, keepdims=True))
            return filled, slope

        def improve(state):
            turn, _, half, lower, upper, done = state
            filled, slope = measure(half)
            above = filled > TOPK
            lower = jnp.where(above, half, lower)
            upper = jnp.where(above, upper, half)
            newton = (filled - TOPK) / slope
            held = jnp.clip(filled, 1e-3, count - 1e-3)
            bent = (jnp.log(held / (count - held)) - goal) * (held * (count - held) / (count * slope))
            close = jnp.abs(newton) <= NEWTON_TOLERANCE
            following = half + 0.5 * jnp.where(close, newton, bent)
            inside = (following > lower) & (following < upper)
            halve = (turn >= 12) & (lax.rem(turn, 2) == 1)
            middle = 0.5 * (lower + upper)
            following = jnp.where(close | (inside & jnp.logical_not(halve)), following, middle)
            half = jnp.where(done > 0.0, half, following)
            done = jnp.where(close, 1.0, done)
            return turn + 1, jnp.min(done), half, lower, upper, done

        start_done = jnp.where(searched, 0.0, 1.0)
        bound = jnp.full((1, lanes), 0.5 * search_bound, jnp.float32)
        _, _, half, lower, upper, done = lax.while_loop(
            lambda state: (state[0] < 12 + 2 * search_steps) & (state[1] < 0.5),
            improve,
            (0, jnp.min(start_done), guess, -bound, bound, start_done),
        )
        half = jnp.where(done > 0.0, half, 0.5 * (lower + upper))
        pivot = jnp.where(searched, half, OPEN_PIVOT)

        def weigh(chunk, sums):
            here = pl.ds(pl.multiple_of(chunk * CHUNK, CHUNK), CHUNK)
            raised = jnp.exp(st_ref[here, :] - top)
            weight = raised / (1.0 + jnp.exp(2.0 * (pivot - sm_ref[here, :])))
            merged = sums[1] + jnp.dot(
                vt_ref[:, here], weight.astype(jnp.bfloat16), preferred_element_type=jnp.float32
            )
            return sums[0] + fold(weight, jnp.add), merged

        total, merged = lax.fori_loop(
            0,
            chunks,
            weigh,
            (jnp.zeros((8, lanes), jnp.float32), jnp.zeros((LANES, lanes), jnp.float32)),
        )
        total = jnp.sum(total, axis=0, keepdims=True)
        merged = merged / total
        own = jnp.where(slot == 0, merged[:HEAD], merged[HEAD:])
        o_ref[step] = own
        for at in range(together):
            low_ref[table[step, 2 + at]] = own[:, at * rows : (at + 1) * rows].astype(jnp.bfloat16)
        lse_ref[step] = top + jnp.log(total)
        pivot_ref[step] = pivot
        return jnp.where(searched, half, guess)

    lax.fori_loop(0, unit_count, unit, jnp.zeros((1, lanes), jnp.float32))


def backward_kernel(
    block,
    table,
    prefix_ref,
    p_ref,
    do_ref,
    o_ref,
    lse_ref,
    pivot_ref,
    message_ref,
    d_ref,
    score_ref,
    dq_ref,
    dk_ref,
    dv_ref,
    ds_ref,
    kt_ref,
):
    unit_count, _, lanes = o_ref.shape
    rows = do_ref.shape[2]
    together = lanes // rows
    length = p_ref.shape[0]
    prefix = prefix_ref[0]
    turn(p_ref, LANES, kt_ref)

    def clear(chunk, _):
        here = pl.ds(pl.multiple_of(chunk * CHUNK, CHUNK), CHUNK)
        for ref in (dq_ref, dk_ref, dv_ref):
            ref[here, :] = jnp.zeros((CHUNK, LANES), jnp.float32)
        for slot in range(2):
            ds_ref[slot, here, :] = jnp.zeros((CHUNK, lanes), jnp.float32)
        return 0

    lax.fori_loop(0, length // CHUNK, clear, 0)

    def unit(step, _):
        slot, first = table[step, 0], table[step, 1]
        last = first + (together - 1) * block + rows - 1
        whose = [pl.ds(pl.multiple_of(first + at * block, rows), rows) for at in range(together)]
        query = own_head(jnp.concatenate([p_ref[here, 0:LANES] for here in whose], axis=0), slot)
        query_t = query.T.astype(jnp.bfloat16)
        query = query.astype(jnp.bfloat16)
        grad = jnp.concatenate([do_ref[table[step, 2 + at]] for at in range(together)], axis=1)
        grad = grad.astype(jnp.float32)
        row_dot = jnp.sum(grad * o_ref[step], axis=0, keepdims=True)
        empty = jnp.zeros_like(grad)
        grad = jnp.where(
            slot == 0,
            jnp.concatenate([grad, empty], axis=0),
            jnp.concatenate([empty, grad], axis=0),
        )
        grad_t = grad.T.astype(jnp.bfloat16)
        grad = grad.astype(jnp.bfloat16)
        lse, pivot = lse_ref[step], pivot_ref[step]
        score_lane = pl.multiple_of((3 + slot) * LANES, LANES)

        def body(masked):
            def run(chunk, grad_query):
                start = pl.multiple_of(chunk * CHUNK, CHUNK)
                here = pl.ds(start, CHUNK)
                logits = jnp.dot(
                    p_ref[here, LANES : 2 * LANES], query_t, preferred_element_type=jnp.float32
                )
                grad_probs = jnp.dot(
                    p_ref[here, 2 * LANES : 3 * LANES], grad, preferred_element_type=jnp.float32
                )
                score = spread_lanes(p_ref[here, pl.ds(score_lane, LANES)], lanes)
                if masked:
                    allowed, local = masks(start, first, prefix, rows, block, together)
                    logits = jnp.where(allowed, logits, -1e30)
                    score = jnp.where(local, FAR, jnp.where(allowed, score, -FAR))
                unit_probs = jnp.exp(logits - lse)
                gate = 1.0 / (1.0 + jnp.exp(2.0 * (pivot - score)))
                probs = gate * unit_probs
                grad_logits = probs * (grad_probs - row_dot)
                ds_ref[slot, here, :] += grad_logits * (1.0 - gate)
                low = grad_logits.astype(jnp.bfloat16)
                dk_ref[here, :] += jnp.dot(low, query, preferred_element_type=jnp.float32)
                dv_ref[here, :] += jnp.dot(
                    probs.astype(jnp.bfloat16), grad_t, preferred_element_type=jnp.float32
                )
                return grad_query + jnp.dot(
                    kt_ref[:, here], low, preferred_element_type=jnp.float32
                )

            return run

        grad_query = over_chunks(
            first, last, prefix, body, jnp.zeros((LANES, lanes), jnp.float32)
        ).T
        lane = lax.broadcasted_iota(jnp.int32, grad_query.shape, 1)
        grad_query = jnp.where(lax.div(lane, HEAD) == slot, grad_query, 0.0)
        for at, here in enumerate(whose):
            dq_ref[here, :] += grad_query[at * rows : (at + 1) * rows]
        return 0

    lax.fori_loop(0, unit_count, unit, 0)

    def finish(chunk, _):
        here = pl.ds(pl.multiple_of(chunk * CHUNK, CHUNK), CHUNK)
        lane = lax.broadcasted_iota(jnp.int32, (CHUNK, LANES), 1)
        columns = [jnp.sum(ds_ref[slot, here, :], axis=1, keepdims=True) for slot in range(2)]
        grad_score = jnp.where(lane == 0, columns[0], jnp.where(lane == 1, columns[1], 0.0))
        grad_score = grad_score.T[:SCORE_ROWS].astype(jnp.bfloat16)
        score_ref[:, here] = grad_score
        message_ref[chunk, CHUNK:, 0:CHUNK] = grad_score
        message_ref[chunk, CHUNK:, CHUNK:] = jnp.zeros_like(message_ref[chunk, CHUNK:, CHUNK:])
        grads = (dq_ref[here, :] * HEAD**-0.5, dk_ref[here, :], dv_ref[here, :])
        for kind, grad in enumerate(grads):
            low = grad.astype(jnp.bfloat16)
            d_ref[here, kind * LANES : (kind + 1) * LANES] = low
            message_ref[chunk, 0:CHUNK, kind * LANES : (kind + 1) * LANES] = low
        return 0

    lax.fori_loop(0, length // CHUNK, finish, 0)


VMEM_LIMIT = 48 * 1024 * 1024


def kernel_params():
    return pltpu.CompilerParams(vmem_limit_bytes=VMEM_LIMIT)


def in_vmem():
    return pl.BlockSpec(memory_space=pltpu.VMEM)


def in_smem():
    return pl.BlockSpec(memory_space=pltpu.SMEM)


def attend(table, prefix, projected, rows, block):
    unit_count = table.shape[0]
    together = table.shape[1] - 2
    lanes = rows * together
    length = projected.shape[0]
    pairs = unit_count * lanes * length
    return pl.pallas_call(
        partial(forward_kernel, block),
        out_shape=(
            jax.ShapeDtypeStruct((unit_count, HEAD, lanes), jnp.float32),
            jax.ShapeDtypeStruct((unit_count * together, HEAD, rows), jnp.bfloat16),
            jax.ShapeDtypeStruct((unit_count, 1, lanes), jnp.float32),
            jax.ShapeDtypeStruct((unit_count, 1, lanes), jnp.float32),
        ),
        in_specs=[in_smem(), in_smem(), in_vmem()],
        out_specs=(in_vmem(),) * 4,
        scratch_shapes=[
            pltpu.VMEM((length, lanes), jnp.float32),
            pltpu.VMEM((length, lanes), jnp.float32),
            pltpu.VMEM((LANES, length), jnp.bfloat16),
        ],
        compiler_params=kernel_params(),
        cost_estimate=pl.CostEstimate(
            flops=pairs * 12000, bytes_accessed=projected.size * 4, transcendentals=pairs * 8
        ),
        name="attend",
    )(table, prefix, projected)


def attend_back(table, prefix, projected, grads, attended, log_totals, pivots, block):
    unit_count, _, lanes = attended.shape
    length = projected.shape[0]
    pairs = unit_count * lanes * length
    return pl.pallas_call(
        partial(backward_kernel, block),
        out_shape=(
            jax.ShapeDtypeStruct((length // CHUNK, CHUNK + SCORE_ROWS, 3 * LANES), jnp.bfloat16),
            jax.ShapeDtypeStruct((length, 3 * LANES), jnp.bfloat16),
            jax.ShapeDtypeStruct((SCORE_ROWS, length), jnp.bfloat16),
        ),
        in_specs=[in_smem(), in_smem()] + [in_vmem()] * 5,
        out_specs=(in_vmem(),) * 3,
        scratch_shapes=[
            pltpu.VMEM((length, LANES), jnp.float32),
            pltpu.VMEM((length, LANES), jnp.float32),
            pltpu.VMEM((length, LANES), jnp.float32),
            pltpu.VMEM((2, length, lanes), jnp.float32),
            pltpu.VMEM((LANES, length), jnp.bfloat16),
        ],
        compiler_params=kernel_params(),
        cost_estimate=pl.CostEstimate(
            flops=pairs * 9000, bytes_accessed=projected.size * 4, transcendentals=pairs * 3
        ),
        name="attend_back",
    )(table, prefix, projected, grads, attended, log_totals, pivots)


def project_kernel(count, offset, *refs):
    tokens, (gain_ref, shift_ref, weight_ref, _, __, normed_ref, projected_ref) = refs[:count], refs[count:]
    for step, tokens_ref in enumerate(tokens):

        @pl.when(pl.program_id(0) == step)
        def _(tokens_ref=tokens_ref):
            hat, _ = normalize(tokens_ref[...].astype(jnp.float32))
            normed = (hat * gain_ref[...] + shift_ref[...]).astype(jnp.bfloat16)
            normed_ref[...] = normed
            low = jnp.dot(normed, weight_ref[...], preferred_element_type=jnp.float32)
            low = low.astype(jnp.bfloat16).astype(jnp.float32)
            lane = lax.broadcasted_iota(jnp.int32, low.shape, 1)
            projected_ref[...] = jnp.where(lane < 3 * LANES, low, 0.5 * low).astype(jnp.bfloat16)


def project(places, tokens, gain, shift, weight, normed, projected):
    count = len(tokens)
    rows, width = tokens[0].shape
    columns = weight.shape[1]

    def whole(shape):
        return pl.BlockSpec(shape, lambda i, at: (0, 0))

    anywhere = pl.BlockSpec(memory_space=pl.ANY)
    return pl.pallas_call(
        partial(project_kernel, count),
        grid_spec=pltpu.PrefetchScalarGridSpec(
            num_scalar_prefetch=1,
            grid=(count,),
            in_specs=[whole((rows, width))] * count
            + [whole((1, width)), whole((1, width)), whole((width, columns)), anywhere, anywhere],
            out_specs=(
                pl.BlockSpec((rows, width), lambda i, at: (at[i], 0)),
                pl.BlockSpec((rows, columns), lambda i, at: (at[i], 0)),
            ),
        ),
        out_shape=(
            jax.ShapeDtypeStruct(normed.shape, normed.dtype),
            jax.ShapeDtypeStruct(projected.shape, projected.dtype),
        ),
        input_output_aliases={count + 4: 0, count + 5: 1},
        compiler_params=kernel_params(),
        cost_estimate=pl.CostEstimate(
            flops=2 * count * rows * width * columns * 20,
            bytes_accessed=rows * width * 12,
            transcendentals=0,
        ),
        name="project",
    )(places, *tokens, gain, shift, weight, normed, projected)


def pack_kernel(pairs, vector_ref, query_ref, key_ref, value_ref, score_ref, out_ref):
    rows = query_ref.shape[0]
    spare = vector_ref[...].astype(jnp.float32).T[:rows]
    lane = lax.broadcasted_iota(jnp.int32, spare.shape, 1)
    for pattern, heads in enumerate(pairs):
        tail = spare
        for slot, head in enumerate(heads):
            score = score_ref[:, head : head + 1].astype(jnp.float32)
            tail = jnp.where(lane == slot, score, tail)
        for kind, ref in enumerate((query_ref, key_ref, value_ref)):
            pair = jnp.concatenate([ref[:, h * HEAD : (h + 1) * HEAD] for h in heads], axis=1)
            for copy in range(pattern, out_ref.shape[0], len(pairs)):
                out_ref[copy, :, kind * LANES : (kind + 1) * LANES] = pair
        for copy in range(pattern, out_ref.shape[0], len(pairs)):
            out_ref[copy, :, 3 * LANES :] = tail.astype(jnp.bfloat16)


def pack_heads(copies, pairs, vectors, query, key, value, score):
    return pl.pallas_call(
        partial(pack_kernel, pairs),
        out_shape=jax.ShapeDtypeStruct((copies, query.shape[0], 4 * LANES), jnp.bfloat16),
        in_specs=[in_vmem()] * 5,
        out_specs=in_vmem(),
        compiler_params=kernel_params(),
        name="pack_heads",
    )(jnp.pad(vectors, ((2, LANES - 2 - vectors.shape[0]), (0, LANES - vectors.shape[1]))), query, key, value, score)


def unpack_kernel(
    near, owners, places, arrived_ref, query_ref, key_ref, value_ref, score_ref, vector_ref, bias_ref
):
    rows = query_ref.shape[0]
    sources = [arrived_ref[places[0] + device].astype(jnp.float32) for device in range(near)]
    for head, terms in enumerate(owners):
        for kind, ref in enumerate((query_ref, key_ref, value_ref)):
            at = [kind * LANES + slot * HEAD for _, slot in terms]
            parts = [sources[d][:rows, a : a + HEAD] for (d, _), a in zip(terms, at)]
            ref[:, head * HEAD : (head + 1) * HEAD] = sum(parts[1:], parts[0])

    def line(values, index):
        at = rows + 2 * index
        return jnp.concatenate([values[at : at + 1], values[at + 1 : at + 2]], axis=1)

    total = arrived_ref[0].astype(jnp.float32)
    for device in range(1, arrived_ref.shape[0]):
        total = total + arrived_ref[device].astype(jnp.float32)
    lines = [line(total, 2 + index) for index in range(6)]
    for terms in owners:
        parts = [line(sources[device], slot) for device, slot in terms]
        lines.append(sum(parts[1:], parts[0]))
    width = lines[0].shape[1]
    sublane = lax.broadcasted_iota(jnp.int32, (SCORE_ROWS, width), 0)
    table = jnp.zeros((SCORE_ROWS, width), jnp.float32)
    for index, values in enumerate(lines):
        table = jnp.where(sublane == index, values, table)
    table = pltpu.roll(table, width - places[1], 1)[:, :LANES]
    vector_ref[...] = table[:8, :rows]
    turned = jnp.concatenate([table, jnp.zeros((LANES - SCORE_ROWS, LANES), jnp.float32)], axis=0).T
    score_ref[...] = turned[:rows, 6 : 6 + len(owners)]
    for index in range(2):
        bias_ref[index : index + 1] = line(total, 8 + index)


def unpack_heads(near, owners, places, arrived, rows):
    lanes = arrived.shape[2]
    shapes = [(rows, lanes)] * 3 + [(rows, len(owners)), (8, rows), (2, 2 * lanes)]
    return pl.pallas_call(
        partial(unpack_kernel, near, owners),
        out_shape=[jax.ShapeDtypeStruct(shape, jnp.float32) for shape in shapes],
        in_specs=[in_smem(), in_vmem()],
        out_specs=[in_vmem()] * 6,
        compiler_params=kernel_params(),
        name="unpack_heads",
    )(places, arrived)


def finish_kernel(
    pairs, core_ref, arrived_ref, own_ref, other_ref, tokens_ref, middle_ref, gain_ref, out_ref
):
    rows, width = tokens_ref.shape
    near = len(pairs)
    half = width // 2
    total = jnp.zeros((rows, width), jnp.float32)
    for columns_ref, side in ((own_ref, core_ref[0]), (other_ref, 1 - core_ref[0])):
        for device, heads in enumerate(pairs):
            weight = jnp.concatenate(
                [
                    columns_ref[:, kind * half + head * HEAD : kind * half + (head + 1) * HEAD]
                    for kind in range(3)
                    for head in heads
                ],
                axis=1,
            )
            at = side * near + device
            total += lax.dot_general(
                arrived_ref[at, :rows], weight, NT, preferred_element_type=jnp.float32
            )
            lane = lax.broadcasted_iota(jnp.int32, (width, SCORE_ROWS), 1)
            columns = [
                columns_ref[:, 3 * half + head : 3 * half + head + 1].astype(jnp.float32)
                for head in heads
            ]
            weight = jnp.where(lane == 0, columns[0], jnp.where(lane == 1, columns[1], 0.0))
            grads = arrived_ref[at, rows:, :rows].astype(jnp.float32).T
            total += lax.dot_general(
                grads.astype(jnp.bfloat16),
                weight.astype(jnp.bfloat16),
                NT,
                preferred_element_type=jnp.float32,
            )
    hat, scale = normalize(tokens_ref[...].astype(jnp.float32))
    out_ref[...] = middle_ref[...] + normalize_back(total, hat, scale, gain_ref[...])


def finish_tokens(pairs, core, arrived, own_columns, other_columns, tokens, grad_middle, gain):
    return pl.pallas_call(
        partial(finish_kernel, pairs),
        out_shape=jax.ShapeDtypeStruct(grad_middle.shape, jnp.float32),
        in_specs=[in_smem()] + [in_vmem()] * 6,
        out_specs=in_vmem(),
        compiler_params=kernel_params(),
        name="finish_tokens",
    )(core, arrived, own_columns, other_columns, tokens, grad_middle, gain)


def ring_order(count):
    deep = 4 if count % 4 == 0 else 1
    wide = count // deep
    if deep == 1 or wide == 1:
        return list(range(count))
    walk = []
    for place in range(deep):
        across = range(1, wide) if place % 2 == 0 else range(wide - 1, 0, -1)
        walk += [place * wide + at for at in across]
    return walk + [place * wide for place in reversed(range(deep))]


def look_up(rows, index):
    table = jnp.asarray(np.asarray(rows, np.int32))
    return lax.dynamic_slice(table, (index, jnp.uint32(0)), (1, table.shape[1]))[0]


def pick(values, index):
    start = (index,) + (jnp.uint32(0),) * (values.ndim - 1)
    return lax.dynamic_slice(values, start, (1,) + values.shape[1:])[0]


def place_on(axis):
    return lax.axis_index(axis).astype(jnp.uint32)


def ring_distances(count):
    return sorted(range(-(count // 2), (count + 1) // 2), key=lambda d: (abs(d), d))


def ring_places(order):
    count = len(order)
    spots = np.argsort(order)
    return [[order[(spots[me] + d) % count] for d in ring_distances(count)] for me in range(count)]


def ring_hops(order):
    count = len(order)
    forward = [(order[i], order[(i + 1) % count]) for i in range(count)]
    return forward, [(receiver, sender) for sender, receiver in forward]


def ring_gather(values, order):
    count = len(order)
    forward, backward = ring_hops(order)
    held = {0: values}
    for step in range(1, count // 2 + 1):
        held[-step] = lax.ppermute(held[1 - step], "ctx", forward)
        if step < count - step:
            held[step] = lax.ppermute(held[step - 1], "ctx", backward)
    return held


def ring_scatter(terms, order, places):
    count = len(order)
    forward, backward = ring_hops(order)
    at = {d: places[i].astype(jnp.uint32) for i, d in enumerate(ring_distances(count))}

    def own(distance):
        here = at.get(distance, at.get(distance - count))
        return sum(pick(term, here).astype(jnp.float32) for term in terms)

    ahead = behind = 0.0
    for step in range(count // 2, 0, -1):
        ahead = lax.ppermute((own(step) + ahead).astype(jnp.bfloat16), "ctx", forward)
        ahead = ahead.astype(jnp.float32)
        if step < count - step:
            behind = lax.ppermute((own(-step) + behind).astype(jnp.bfloat16), "ctx", backward)
            behind = behind.astype(jnp.float32)
    return own(0) + ahead + behind


def dp_terms(values):
    count = values.shape[0]
    places = look_up([[(i + shift) % count for shift in range(count)] for i in range(count)], place_on("dp"))
    terms = [pick(values, places[0].astype(jnp.uint32))]
    for shift in range(1, count):
        sent = pick(values, places[shift].astype(jnp.uint32))
        terms.append(lax.ppermute(sent, "dp", [(i, (i + shift) % count) for i in range(count)]))
    return terms


def other_core(values):
    return lax.ppermute(values, "tensor", [(0, 1), (1, 0)])


def normalize(values):
    centred = values - jnp.mean(values, axis=-1, keepdims=True)
    scale = lax.rsqrt(jnp.mean(centred * centred, axis=-1, keepdims=True) + norm_epsilon)
    return centred * scale, scale


def normalize_back(grad, hat, scale, gain):
    scaled = grad * gain
    return scale * (
        scaled
        - jnp.mean(scaled, axis=-1, keepdims=True)
        - hat * jnp.mean(scaled * hat, axis=-1, keepdims=True)
    )


def head_plan(ctx_count, head_count, block):
    parts = 1
    while head_count * parts % ctx_count:
        parts += 1
    share = head_count * parts // ctx_count
    rows = block // parts
    lows, tables = [], []
    for device in range(ctx_count):
        pieces = range(share * device, share * (device + 1))
        lows.append(pieces[0] // parts)
        tables.append(
            [
                (piece // parts - lows[-1], at * block + (piece % parts) * rows)
                + tuple((at + more) * share + order for more in range(parts))
                for order, piece in enumerate(pieces)
                for at in range(0, ctx_count, parts)
            ]
        )
        assert all(entry[0] in (0, 1) for entry in tables[-1])
    assert ctx_count % parts == 0
    return parts, share, rows, lows, np.asarray(tables, np.int32)


def on_device(
    tokens,
    prefix,
    w_query,
    w_key,
    w_value,
    w_score,
    w_attn_out,
    w_fc,
    w_proj,
    ln1_gain,
    ln1_bias,
    ln2_gain,
    ln2_bias,
    attn_bias,
    fc_bias,
    proj_bias,
    cotangent,
    dp_count,
    ctx_count,
):
    f32, bf16 = jnp.float32, jnp.bfloat16
    micro_count, seq_count, block, width = tokens.shape
    local_heads = w_score.shape[1]
    head_count = 2 * local_heads
    assert micro_count == 2 and seq_count == 1
    core = place_on("tensor")
    me = place_on("ctx")
    both = ("dp", "ctx")
    shards = dp_count * ctx_count
    shard_rows = width // shards
    parts, share, rows, lows, tables = head_plan(ctx_count, head_count, block)
    near = ctx_count // 2
    local_low = [low % local_heads for low in lows[:near]]
    local_high = [min(low + 1, local_heads - 1) for low in local_low]

    own_tokens = pick(tokens, core)[0]
    own_cot = pick(cotangent, core)[0]
    other_cot = pick(cotangent, 1 - core)[0]
    own_prefix = pick(prefix, core)
    table = pick(jnp.asarray(tables), me)

    order = ring_order(ctx_count)
    blocks = ring_gather(own_tokens, order)
    places = look_up(ring_places(order), me)

    def columns(weight, head):
        return weight[:, head * HEAD : (head + 1) * HEAD]

    vectors = jnp.stack([ln1_gain, ln1_bias, ln2_gain, ln2_bias, attn_bias, proj_bias])
    pairs = tuple(zip(local_low, local_high))
    outgoing = pack_heads(shards, pairs, vectors, w_query, w_key, w_value, w_score)
    if ctx_count >= 6:
        outgoing, *_ = lax.optimization_barrier((outgoing, blocks[-1], blocks[1]))
    head_weights = lax.all_to_all(outgoing, both, 0, 0, tiled=True).reshape(width, 4 * LANES)
    if ctx_count >= 6:
        head_weights, *_ = lax.optimization_barrier((head_weights, blocks[-2], blocks[2]))
    from_half = (me >= near).astype(jnp.uint32)
    head_weights = jnp.where(from_half == core, head_weights, other_core(head_weights))
    gains = head_weights[:, 3 * LANES + 2 : 3 * LANES + 8].astype(f32).T
    gain_one, shift_one, gain_two, shift_two, attn_shift, proj_shift = [gains[i : i + 1] for i in range(6)]

    score_columns = head_weights[:, 3 * LANES : 3 * LANES + 2]
    wide_weights = jnp.concatenate(
        [head_weights[:, :LANES] * HEAD**-0.5, head_weights[:, LANES : 3 * LANES]]
        + [jnp.broadcast_to(score_columns[:, i : i + 1], (width, LANES)) for i in range(2)],
        axis=1,
    )
    length = ctx_count * block
    normed = jnp.zeros((length, width), bf16)
    projected = jnp.zeros((length, 5 * LANES), bf16)
    distances = ring_distances(ctx_count)
    early = max(ctx_count - 3, 1)
    for batch, batch_places in ((distances[:early], places[:early]), (distances[early:], places[early:])):
        normed, projected = project(
            batch_places,
            [blocks[d] for d in batch],
            gain_one,
            shift_one,
            wide_weights,
            normed,
            projected,
        )

    packed = jnp.concatenate([w_fc, w_proj.T, w_attn_out.T], axis=1)
    packed_heads = jnp.concatenate(
        [w_query, w_key, w_value, w_score, jnp.zeros((shard_rows, LANES - local_heads), bf16)], axis=1
    )
    packed, *_ = lax.optimization_barrier((packed, blocks[-2], blocks[2]))
    packed = lax.all_gather(packed, both, axis=0, tiled=True)
    attended, attended_low, log_totals, pivots = attend(table, own_prefix, projected, rows, block)
    packed, _ = lax.optimization_barrier((packed, log_totals))
    hidden = w_fc.shape[1]
    full_fc, full_proj_t = packed[:, :hidden], packed[:, hidden : 2 * hidden]
    half_out_t = packed[:, 2 * hidden :]
    other_out_t = other_core(half_out_t)
    packed_heads, _ = lax.optimization_barrier((packed_heads, other_out_t))
    half_heads = lax.all_gather(packed_heads, both, axis=0, tiled=True)
    out_t = jnp.where(
        core == 0,
        jnp.concatenate([half_out_t, other_out_t], axis=1),
        jnp.concatenate([other_out_t, half_out_t], axis=1),
    )

    sent = attended_low.reshape(ctx_count, share * HEAD, rows)
    merged = lax.all_to_all(sent, "ctx", 0, 0, tiled=True)
    merged = merged.reshape(head_count, parts, HEAD, rows).transpose(0, 2, 1, 3).reshape(width, block)

    own_block = own_tokens.astype(f32)
    attn = lax.dot_general(merged, out_t, (((0,), (1,)), ((), ())), preferred_element_type=f32)
    middle = own_block + attn + attn_shift
    hat_two, scale_two = normalize(middle)
    normed_two = (hat_two * gain_two + shift_two).astype(bf16)
    normed_two = jnp.concatenate([normed_two, other_core(normed_two)])
    hidden_pre = jnp.dot(normed_two, full_fc, preferred_element_type=f32) + fc_bias.astype(f32)
    active, pull_gelu = jax.vjp(partial(jax.nn.gelu, approximate=True), hidden_pre)
    active = active.astype(bf16)
    mlp = lax.dot_general(active, full_proj_t, NT, preferred_element_type=f32)
    result = middle + mlp[:block] + other_core(mlp[block:].astype(bf16)).astype(f32) + proj_shift
    result = result.astype(bf16)

    both_cot = jnp.concatenate([own_cot, other_cot])
    grad_active = jnp.dot(both_cot, full_proj_t, preferred_element_type=f32)
    grad_pre = pull_gelu(grad_active)[0].astype(bf16)
    grad_two = lax.dot_general(grad_pre, full_fc, NT, preferred_element_type=f32)
    grad_two = grad_two[:block] + other_core(grad_two[block:].astype(bf16)).astype(f32)
    cot = own_cot.astype(f32)
    grad_middle = cot + normalize_back(grad_two, hat_two, scale_two, gain_two)
    grad_middle_low = grad_middle.astype(bf16)
    grad_merged = lax.dot_general(
        out_t, grad_middle_low, (((0,), (1,)), ((), ())), preferred_element_type=f32
    ).astype(bf16)
    sent = grad_merged.reshape(head_count, HEAD, parts, rows).transpose(0, 2, 1, 3)
    sent = sent.reshape(ctx_count, share * HEAD, rows)
    grad_attended = lax.all_to_all(sent, "ctx", 0, 0, tiled=True).reshape(attended_low.shape)

    grad_fc = lax.dot_general(normed_two, grad_pre, (((0,), (0,)), ((), ())), preferred_element_type=f32)
    grad_proj_t = lax.dot_general(both_cot, active, (((0,), (0,)), ((), ())), preferred_element_type=f32)
    grad_out_t = lax.dot_general(
        grad_middle_low, merged, (((0,), (1,)), ((), ())), preferred_element_type=f32
    ).astype(bf16)
    half_width = width // 2
    mine, theirs = grad_out_t[:, :half_width], grad_out_t[:, half_width:]
    mine, theirs = jnp.where(core == 0, mine, theirs), jnp.where(core == 0, theirs, mine)
    grad_out_t = (mine.astype(f32) + other_core(theirs).astype(f32)).astype(bf16)
    grad_packed = jnp.concatenate([grad_fc.astype(bf16), grad_proj_t.astype(bf16), grad_out_t], axis=1)
    grad_packed = grad_packed.reshape(dp_count, ctx_count, shard_rows, grad_packed.shape[1])
    grad_packed_terms = dp_terms(grad_packed)
    early_lines = jnp.concatenate(
        [
            jnp.sum(grad_two * hat_two, axis=0, keepdims=True),
            jnp.sum(grad_two, axis=0, keepdims=True),
            jnp.sum(grad_middle, axis=0, keepdims=True),
            jnp.sum(cot, axis=0, keepdims=True),
        ]
    )
    bias_lines = jnp.sum(grad_pre.astype(f32), axis=0).reshape(hidden // width, width)
    bias_lines = jnp.pad(bias_lines, ((0, 8 - bias_lines.shape[0]), (0, 0)))

    message, grads, grad_scores = attend_back(
        table, own_prefix, projected, grad_attended, attended, log_totals, pivots, block
    )

    log_totals_after = grad_scores[:1]
    shard = place_on("dp") * ctx_count + me
    arrived = lax.all_to_all(message, "ctx", 0, 0, tiled=True)
    half_heads, _ = lax.optimization_barrier((half_heads, log_totals_after))
    other_heads = other_core(half_heads)
    *grad_packed_terms, _ = lax.optimization_barrier((*grad_packed_terms, log_totals_after))
    grad_packed = ring_scatter(grad_packed_terms, order, places)
    tokens_grad = finish_tokens(
        pairs, core.astype(jnp.int32)[None], arrived, half_heads, other_heads, own_tokens, grad_middle, gain_one
    )

    grad_normed = lax.dot_general(grads, head_weights[:, : 3 * LANES], NT, preferred_element_type=f32)
    grad_normed = grad_normed + lax.dot_general(
        grad_scores[:2], score_columns, (((0,), (1,)), ((), ())), preferred_element_type=f32
    )
    hat_one = (normed.astype(f32) - shift_one) / gain_one

    over_rows = (((0,), (0,)), ((), ()))
    grad_heads = lax.dot_general(normed, grads, over_rows, preferred_element_type=f32)
    grad_heads = grad_heads + other_core(grad_heads.astype(bf16)).astype(f32)
    grad_heads = dp_terms(
        grad_heads.astype(bf16).reshape(dp_count, ctx_count, shard_rows, 3 * LANES)
    )
    grad_columns = jnp.dot(grad_scores, normed, preferred_element_type=f32)
    lines = jnp.concatenate(
        [
            grad_columns[:2],
            jnp.sum(grad_normed * hat_one, axis=0, keepdims=True),
            jnp.sum(grad_normed, axis=0, keepdims=True),
            early_lines,
        ]
    )
    lines = lines + other_core(lines.astype(bf16)).astype(f32)
    lines = jnp.concatenate([lines, bias_lines])
    lines = jnp.broadcast_to(lines.astype(bf16)[None], (dp_count,) + lines.shape)
    lines = sum(term.astype(f32) for term in dp_terms(lines)).astype(bf16)
    lines = lines.reshape(2 * lines.shape[0], 3 * LANES)
    message = sum(term.astype(f32) for term in grad_heads).astype(bf16)
    message = jnp.concatenate(
        [message, jnp.broadcast_to(lines[None], (ctx_count,) + lines.shape)], axis=1
    )
    message, _ = lax.optimization_barrier((message, arrived))
    arrived = lax.all_to_all(message, "ctx", 0, 0, tiled=True)
    owners = [[] for _ in range(local_heads)]
    for device in range(near):
        for slot in sorted({entry[0] for entry in tables[device].tolist()}):
            owners[local_low[device] + slot].append((device, slot))
    grad_query, grad_key, grad_value, grad_score, vector_grads, fc_bias_grad = unpack_heads(
        near, owners, jnp.stack([core * near, shard * shard_rows]).astype(jnp.int32), arrived, shard_rows
    )
    fc_bias_grad = fc_bias_grad.reshape(hidden)

    def both_micro(own):
        other = other_core(own)
        return jnp.where(core == 0, jnp.stack([own, other]), jnp.stack([other, own]))[:, None]

    return (
        both_micro(result),
        both_micro(tokens_grad),
        grad_query,
        grad_key,
        grad_value,
        grad_score,
        grad_packed[:, 2 * hidden :].T,
        grad_packed[:, :hidden],
        grad_packed[:, hidden : 2 * hidden].T,
        vector_grads[0],
        vector_grads[1],
        vector_grads[2],
        vector_grads[3],
        vector_grads[4],
        fc_bias_grad,
        vector_grads[5],
    )


def solution(mesh):
    rows, columns, vector = P(("dp", "ctx"), "tensor"), P("tensor", ("dp", "ctx")), P(("dp", "ctx"))
    tokens = P(None, "dp", "ctx", None)
    in_specs = (
        (tokens, P(None, "dp"))
        + (rows,) * 4
        + (columns, rows, columns)
        + (vector,) * 5
        + (P("tensor"), vector, tokens)
    )
    out_specs = (
        (tokens, tokens)
        + (rows,) * 4
        + (columns, rows, columns)
        + (vector,) * 5
        + (P("tensor"), vector)
    )
    return jax.shard_map(
        partial(on_device, dp_count=mesh.shape["dp"], ctx_count=mesh.shape["ctx"]),
        mesh=mesh,
        in_specs=in_specs,
        out_specs=out_specs,
        check_vma=False,
    )
```

```python
from functools import partial

import jax
import jax.numpy as jnp
import numpy as np
from jax import lax
from jax.experimental import pallas as pl
from jax.experimental.pallas import tpu as pltpu
from jax.sharding import PartitionSpec as P

WIN = 64
TOPK = 64
HEAD = 64
LANES = 128

norm_epsilon = 1e-05
search_steps = 24
search_bound = 64.0

CHUNK = 256
FAR = 1e9
OPEN_PIVOT = -1e6
NEWTON_TOLERANCE = 3e-3
SCORE_ROWS = 16
NT = (((1,), (1,)), ((), ()))


def over_chunks(first, last, prefix, body, carry):
    below = lax.div(jnp.maximum(first - (WIN - 1), 0), CHUNK)
    total = lax.div(jnp.maximum(last + 1, prefix) + CHUNK - 1, CHUNK)
    above = jnp.minimum(lax.div(last + WIN + CHUNK - 1, CHUNK), total)
    whole = jnp.maximum(lax.div(prefix, CHUNK), above)
    carry = lax.fori_loop(0, below, body(False), carry)
    carry = lax.fori_loop(below, above, body(True), carry)
    carry = lax.fori_loop(above, whole, body(False), carry)
    return lax.fori_loop(whole, total, body(True), carry)


def fold(values, how):
    while values.shape[0] > 8:
        half = values.shape[0] // 2
        values = how(values[:half], values[half:])
    return values


def own_head(values, slot):
    lane = lax.broadcasted_iota(jnp.int32, values.shape, 1)
    kept = jnp.where(lax.div(lane, HEAD) == slot, values.astype(jnp.float32), 0.0)
    return kept


def rows_of(first, shape, rows, block):
    lane = lax.broadcasted_iota(jnp.int32, shape, 1)
    return first + lax.div(lane, rows) * block + lax.rem(lane, rows)


def masks(start, first, prefix, rows, block, together):
    shape = (CHUNK, rows * together)
    key = lax.broadcasted_iota(jnp.int32, shape, 0)
    behind = rows_of(first - start, shape, rows, block) - key
    allowed = (behind >= 0) | (key < prefix - start)
    return allowed, allowed & (jnp.abs(behind) < WIN)


def spread_lanes(values, lanes):
    values = values.astype(jnp.float32)
    return jnp.concatenate([values] * (lanes // LANES), axis=1)


def turn(source_ref, lanes, target_ref):
    def run(chunk, _):
        here = pl.ds(pl.multiple_of(chunk * CHUNK, CHUNK), CHUNK)
        flipped = source_ref[here, lanes : lanes + LANES].astype(jnp.float32).T
        target_ref[:, here] = flipped.astype(jnp.bfloat16)
        return 0

    lax.fori_loop(0, source_ref.shape[0] // CHUNK, run, 0)


def forward_kernel(
    block, table, prefix_ref, p_ref, o_ref, low_ref, lse_ref, pivot_ref, sm_ref, st_ref, vt_ref
):
    unit_count, _, lanes = o_ref.shape
    rows = low_ref.shape[2]
    together = lanes // rows
    prefix = prefix_ref[0]
    turn(p_ref, 2 * LANES, vt_ref)

    def unit(step, guess):
        slot, first = table[step, 0], table[step, 1]
        last = first + (together - 1) * block + rows - 1
        query = jnp.concatenate(
            [
                p_ref[pl.ds(pl.multiple_of(first + at * block, rows), rows), 0:LANES]
                for at in range(together)
            ],
            axis=0,
        )
        query_t = own_head(query, slot).T.astype(jnp.bfloat16)
        score_lane = pl.multiple_of((3 + slot) * LANES, LANES)

        def build(masked):
            def run(chunk, top):
                start = pl.multiple_of(chunk * CHUNK, CHUNK)
                here = pl.ds(start, CHUNK)
                logits = jnp.dot(
                    p_ref[here, LANES : 2 * LANES], query_t, preferred_element_type=jnp.float32
                )
                score = spread_lanes(p_ref[here, pl.ds(score_lane, LANES)], lanes)
                if masked:
                    allowed, local = masks(start, first, prefix, rows, block, together)
                    logits = jnp.where(allowed, logits, -1e30)
                    score = jnp.where(local, FAR, jnp.where(allowed, score, -FAR))
                    top = jnp.maximum(top, fold(jnp.where(local, logits, -1e30), jnp.maximum))
                st_ref[here, :] = logits
                sm_ref[here, :] = score
                return top

            return run

        top = over_chunks(first, last, prefix, build, jnp.full((8, lanes), -1e30, jnp.float32))
        top = jnp.max(top, axis=0, keepdims=True)

        row = rows_of(first, (1, lanes), rows, block)
        local_count = (
            jnp.minimum(row, WIN - 1) + 1 + jnp.clip(prefix - 1 - row, 0, WIN - 1)
        ).astype(jnp.float32)
        candidates = jnp.maximum(row + 1, prefix).astype(jnp.float32) - local_count
        chunks = lax.div(jnp.maximum(last + 1, prefix) + CHUNK - 1, CHUNK)
        entries = (chunks * CHUNK).astype(jnp.float32)
        searched = candidates > TOPK
        count = jnp.maximum(candidates, TOPK + 1.0)
        goal = jnp.log(TOPK / (count - TOPK))

        def measure(half):
            def run(chunk, sums):
                bent = jnp.tanh(sm_ref[pl.ds(pl.multiple_of(chunk * CHUNK, CHUNK), CHUNK), :] - half)
                return sums[0] + fold(bent, jnp.add), sums[1] + fold(bent * bent, jnp.add)

            zero = jnp.zeros((8, lanes), jnp.float32)
            first_sum, second_sum = lax.fori_loop(0, chunks, run, (zero, zero))
            filled = 0.5 * (entries + jnp.sum(first_sum, axis=0, keepdims=True)) - local_count
            slope = 0.25 * (entries - jnp.sum(second_sum, axis=0, keepdims=True))
            return filled, slope

        def improve(state):
            turn, _, half, lower, upper, done = state
            filled, slope = measure(half)
            above = filled > TOPK
            lower = jnp.where(above, half, lower)
            upper = jnp.where(above, upper, half)
            newton = (filled - TOPK) / slope
            held = jnp.clip(filled, 1e-3, count - 1e-3)
            bent = (jnp.log(held / (count - held)) - goal) * (held * (count - held) / (count * slope))
            close = jnp.abs(newton) <= NEWTON_TOLERANCE
            following = half + 0.5 * jnp.where(close, newton, bent)
            inside = (following > lower) & (following < upper)
            halve = (turn >= 12) & (lax.rem(turn, 2) == 1)
            middle = 0.5 * (lower + upper)
            following = jnp.where(close | (inside & jnp.logical_not(halve)), following, middle)
            half = jnp.where(done > 0.0, half, following)
            done = jnp.where(close, 1.0, done)
            return turn + 1, jnp.min(done), half, lower, upper, done

        start_done = jnp.where(searched, 0.0, 1.0)
        bound = jnp.full((1, lanes), 0.5 * search_bound, jnp.float32)
        _, _, half, lower, upper, done = lax.while_loop(
            lambda state: (state[0] < 12 + 2 * search_steps) & (state[1] < 0.5),
            improve,
            (0, jnp.min(start_done), guess, -bound, bound, start_done),
        )
        half = jnp.where(done > 0.0, half, 0.5 * (lower + upper))
        pivot = jnp.where(searched, half, OPEN_PIVOT)

        def weigh(chunk, sums):
            here = pl.ds(pl.multiple_of(chunk * CHUNK, CHUNK), CHUNK)
            raised = jnp.exp(st_ref[here, :] - top)
            weight = raised / (1.0 + jnp.exp(2.0 * (pivot - sm_ref[here, :])))
            merged = sums[1] + jnp.dot(
                vt_ref[:, here], weight.astype(jnp.bfloat16), preferred_element_type=jnp.float32
            )
            return sums[0] + fold(weight, jnp.add), merged

        total, merged = lax.fori_loop(
            0,
            chunks,
            weigh,
            (jnp.zeros((8, lanes), jnp.float32), jnp.zeros((LANES, lanes), jnp.float32)),
        )
        total = jnp.sum(total, axis=0, keepdims=True)
        merged = merged / total
        own = jnp.where(slot == 0, merged[:HEAD], merged[HEAD:])
        o_ref[step] = own
        for at in range(together):
            low_ref[table[step, 2 + at]] = own[:, at * rows : (at + 1) * rows].astype(jnp.bfloat16)
        lse_ref[step] = top + jnp.log(total)
        pivot_ref[step] = pivot
        return jnp.where(searched, half, guess)

    lax.fori_loop(0, unit_count, unit, jnp.zeros((1, lanes), jnp.float32))


def backward_kernel(
    block,
    table,
    prefix_ref,
    p_ref,
    do_ref,
    o_ref,
    lse_ref,
    pivot_ref,
    message_ref,
    d_ref,
    score_ref,
    dq_ref,
    dk_ref,
    dv_ref,
    ds_ref,
    kt_ref,
):
    unit_count, _, lanes = o_ref.shape
    rows = do_ref.shape[2]
    together = lanes // rows
    length = p_ref.shape[0]
    prefix = prefix_ref[0]
    turn(p_ref, LANES, kt_ref)

    def clear(chunk, _):
        here = pl.ds(pl.multiple_of(chunk * CHUNK, CHUNK), CHUNK)
        for ref in (dq_ref, dk_ref, dv_ref):
            ref[here, :] = jnp.zeros((CHUNK, LANES), jnp.float32)
        for slot in range(2):
            ds_ref[slot, here, :] = jnp.zeros((CHUNK, lanes), jnp.float32)
        return 0

    lax.fori_loop(0, length // CHUNK, clear, 0)

    def unit(step, _):
        slot, first = table[step, 0], table[step, 1]
        last = first + (together - 1) * block + rows - 1
        whose = [pl.ds(pl.multiple_of(first + at * block, rows), rows) for at in range(together)]
        query = own_head(jnp.concatenate([p_ref[here, 0:LANES] for here in whose], axis=0), slot)
        query_t = query.T.astype(jnp.bfloat16)
        query = query.astype(jnp.bfloat16)
        grad = jnp.concatenate([do_ref[table[step, 2 + at]] for at in range(together)], axis=1)
        grad = grad.astype(jnp.float32)
        row_dot = jnp.sum(grad * o_ref[step], axis=0, keepdims=True)
        empty = jnp.zeros_like(grad)
        grad = jnp.where(
            slot == 0,
            jnp.concatenate([grad, empty], axis=0),
            jnp.concatenate([empty, grad], axis=0),
        )
        grad_t = grad.T.astype(jnp.bfloat16)
        grad = grad.astype(jnp.bfloat16)
        lse, pivot = lse_ref[step], pivot_ref[step]
        score_lane = pl.multiple_of((3 + slot) * LANES, LANES)

        def body(masked):
            def run(chunk, grad_query):
                start = pl.multiple_of(chunk * CHUNK, CHUNK)
                here = pl.ds(start, CHUNK)
                logits = jnp.dot(
                    p_ref[here, LANES : 2 * LANES], query_t, preferred_element_type=jnp.float32
                )
                grad_probs = jnp.dot(
                    p_ref[here, 2 * LANES : 3 * LANES], grad, preferred_element_type=jnp.float32
                )
                score = spread_lanes(p_ref[here, pl.ds(score_lane, LANES)], lanes)
                if masked:
                    allowed, local = masks(start, first, prefix, rows, block, together)
                    logits = jnp.where(allowed, logits, -1e30)
                    score = jnp.where(local, FAR, jnp.where(allowed, score, -FAR))
                unit_probs = jnp.exp(logits - lse)
                gate = 1.0 / (1.0 + jnp.exp(2.0 * (pivot - score)))
                probs = gate * unit_probs
                grad_logits = probs * (grad_probs - row_dot)
                ds_ref[slot, here, :] += grad_logits * (1.0 - gate)
                low = grad_logits.astype(jnp.bfloat16)
                dk_ref[here, :] += jnp.dot(low, query, preferred_element_type=jnp.float32)
                dv_ref[here, :] += jnp.dot(
                    probs.astype(jnp.bfloat16), grad_t, preferred_element_type=jnp.float32
                )
                return grad_query + jnp.dot(
                    kt_ref[:, here], low, preferred_element_type=jnp.float32
                )

            return run

        grad_query = over_chunks(
            first, last, prefix, body, jnp.zeros((LANES, lanes), jnp.float32)
        ).T
        lane = lax.broadcasted_iota(jnp.int32, grad_query.shape, 1)
        grad_query = jnp.where(lax.div(lane, HEAD) == slot, grad_query, 0.0)
        for at, here in enumerate(whose):
            dq_ref[here, :] += grad_query[at * rows : (at + 1) * rows]
        return 0

    lax.fori_loop(0, unit_count, unit, 0)

    def finish(chunk, _):
        here = pl.ds(pl.multiple_of(chunk * CHUNK, CHUNK), CHUNK)
        lane = lax.broadcasted_iota(jnp.int32, (CHUNK, LANES), 1)
        columns = [jnp.sum(ds_ref[slot, here, :], axis=1, keepdims=True) for slot in range(2)]
        grad_score = jnp.where(lane == 0, columns[0], jnp.where(lane == 1, columns[1], 0.0))
        grad_score = grad_score.T[:SCORE_ROWS].astype(jnp.bfloat16)
        score_ref[:, here] = grad_score
        message_ref[chunk, CHUNK:, 0:CHUNK] = grad_score
        message_ref[chunk, CHUNK:, CHUNK:] = jnp.zeros_like(message_ref[chunk, CHUNK:, CHUNK:])
        grads = (dq_ref[here, :] * HEAD**-0.5, dk_ref[here, :], dv_ref[here, :])
        for kind, grad in enumerate(grads):
            low = grad.astype(jnp.bfloat16)
            d_ref[here, kind * LANES : (kind + 1) * LANES] = low
            message_ref[chunk, 0:CHUNK, kind * LANES : (kind + 1) * LANES] = low
        return 0

    lax.fori_loop(0, length // CHUNK, finish, 0)


VMEM_LIMIT = 48 * 1024 * 1024


def kernel_params():
    return pltpu.CompilerParams(vmem_limit_bytes=VMEM_LIMIT)


def in_vmem():
    return pl.BlockSpec(memory_space=pltpu.VMEM)


def in_smem():
    return pl.BlockSpec(memory_space=pltpu.SMEM)


def attend(table, prefix, projected, rows, block):
    unit_count = table.shape[0]
    together = table.shape[1] - 2
    lanes = rows * together
    length = projected.shape[0]
    pairs = unit_count * lanes * length
    return pl.pallas_call(
        partial(forward_kernel, block),
        out_shape=(
            jax.ShapeDtypeStruct((unit_count, HEAD, lanes), jnp.float32),
            jax.ShapeDtypeStruct((unit_count * together, HEAD, rows), jnp.bfloat16),
            jax.ShapeDtypeStruct((unit_count, 1, lanes), jnp.float32),
            jax.ShapeDtypeStruct((unit_count, 1, lanes), jnp.float32),
        ),
        in_specs=[in_smem(), in_smem(), in_vmem()],
        out_specs=(in_vmem(),) * 4,
        scratch_shapes=[
            pltpu.VMEM((length, lanes), jnp.float32),
            pltpu.VMEM((length, lanes), jnp.float32),
            pltpu.VMEM((LANES, length), jnp.bfloat16),
        ],
        compiler_params=kernel_params(),
        cost_estimate=pl.CostEstimate(
            flops=pairs * 12000, bytes_accessed=projected.size * 4, transcendentals=pairs * 8
        ),
        name="attend",
    )(table, prefix, projected)


def attend_back(table, prefix, projected, grads, attended, log_totals, pivots, block):
    unit_count, _, lanes = attended.shape
    length = projected.shape[0]
    pairs = unit_count * lanes * length
    return pl.pallas_call(
        partial(backward_kernel, block),
        out_shape=(
            jax.ShapeDtypeStruct((length // CHUNK, CHUNK + SCORE_ROWS, 3 * LANES), jnp.bfloat16),
            jax.ShapeDtypeStruct((length, 3 * LANES), jnp.bfloat16),
            jax.ShapeDtypeStruct((SCORE_ROWS, length), jnp.bfloat16),
        ),
        in_specs=[in_smem(), in_smem()] + [in_vmem()] * 5,
        out_specs=(in_vmem(),) * 3,
        scratch_shapes=[
            pltpu.VMEM((length, LANES), jnp.float32),
            pltpu.VMEM((length, LANES), jnp.float32),
            pltpu.VMEM((length, LANES), jnp.float32),
            pltpu.VMEM((2, length, lanes), jnp.float32),
            pltpu.VMEM((LANES, length), jnp.bfloat16),
        ],
        compiler_params=kernel_params(),
        cost_estimate=pl.CostEstimate(
            flops=pairs * 9000, bytes_accessed=projected.size * 4, transcendentals=pairs * 3
        ),
        name="attend_back",
    )(table, prefix, projected, grads, attended, log_totals, pivots)


def project_kernel(count, offset, *refs):
    tokens, (gain_ref, shift_ref, weight_ref, _, __, normed_ref, projected_ref) = refs[:count], refs[count:]
    for step, tokens_ref in enumerate(tokens):

        @pl.when(pl.program_id(0) == step)
        def _(tokens_ref=tokens_ref):
            hat, _ = normalize(tokens_ref[...].astype(jnp.float32))
            normed = (hat * gain_ref[...] + shift_ref[...]).astype(jnp.bfloat16)
            normed_ref[...] = normed
            low = jnp.dot(normed, weight_ref[...], preferred_element_type=jnp.float32)
            low = low.astype(jnp.bfloat16).astype(jnp.float32)
            lane = lax.broadcasted_iota(jnp.int32, low.shape, 1)
            projected_ref[...] = jnp.where(lane < 3 * LANES, low, 0.5 * low).astype(jnp.bfloat16)


def project(places, tokens, gain, shift, weight, normed, projected):
    count = len(tokens)
    rows, width = tokens[0].shape
    columns = weight.shape[1]

    def whole(shape):
        return pl.BlockSpec(shape, lambda i, at: (0, 0))

    anywhere = pl.BlockSpec(memory_space=pl.ANY)
    return pl.pallas_call(
        partial(project_kernel, count),
        grid_spec=pltpu.PrefetchScalarGridSpec(
            num_scalar_prefetch=1,
            grid=(count,),
            in_specs=[whole((rows, width))] * count
            + [whole((1, width)), whole((1, width)), whole((width, columns)), anywhere, anywhere],
            out_specs=(
                pl.BlockSpec((rows, width), lambda i, at: (at[i], 0)),
                pl.BlockSpec((rows, columns), lambda i, at: (at[i], 0)),
            ),
        ),
        out_shape=(
            jax.ShapeDtypeStruct(normed.shape, normed.dtype),
            jax.ShapeDtypeStruct(projected.shape, projected.dtype),
        ),
        input_output_aliases={count + 4: 0, count + 5: 1},
        compiler_params=kernel_params(),
        cost_estimate=pl.CostEstimate(
            flops=2 * count * rows * width * columns * 20,
            bytes_accessed=rows * width * 12,
            transcendentals=0,
        ),
        name="project",
    )(places, *tokens, gain, shift, weight, normed, projected)


VECTOR_LANE = 8


def pack_kernel(vector_ref, query_ref, key_ref, value_ref, score_ref, out_ref):
    rows, width = query_ref.shape
    for kind, ref in enumerate((query_ref, key_ref, value_ref)):
        out_ref[:, kind * width : (kind + 1) * width] = ref[...]
    tail = vector_ref[...].astype(jnp.float32).T[:rows]
    lane = lax.broadcasted_iota(jnp.int32, tail.shape, 1)
    for head in range(score_ref.shape[1]):
        tail = jnp.where(lane == head, score_ref[:, head : head + 1].astype(jnp.float32), tail)
    out_ref[:, 3 * width :] = tail.astype(jnp.bfloat16)


def pack_heads(vectors, query, key, value, score):
    below = LANES - VECTOR_LANE - vectors.shape[0]
    return pl.pallas_call(
        pack_kernel,
        out_shape=jax.ShapeDtypeStruct((query.shape[0], 3 * query.shape[1] + LANES), jnp.bfloat16),
        in_specs=[in_vmem()] * 5,
        out_specs=in_vmem(),
        compiler_params=kernel_params(),
        name="pack_heads",
    )(jnp.pad(vectors, ((VECTOR_LANE, below), (0, LANES - vectors.shape[1]))), query, key, value, score)


def select_kernel(pairs, ctx_ref, columns_ref, out_ref):
    half = (columns_ref.shape[1] - LANES) // 3
    for pattern, heads in enumerate(pairs):

        @pl.when(lax.rem(ctx_ref[0], len(pairs)) == pattern)
        def _(heads=heads):
            for kind in range(3):
                starts = [kind * half + head * HEAD for head in heads]
                out_ref[:, kind * LANES : (kind + 1) * LANES] = jnp.concatenate(
                    [columns_ref[:, at : at + HEAD] for at in starts], axis=1
                )
            tail = columns_ref[:, 3 * half :].astype(jnp.float32)
            lane = lax.broadcasted_iota(jnp.int32, tail.shape, 1)
            for slot, head in enumerate(heads):
                tail = jnp.where(lane == LANES - 2 + slot, tail[:, head : head + 1], tail)
            out_ref[:, 3 * LANES :] = tail.astype(jnp.bfloat16)


def select_heads(pairs, ctx, columns):
    return pl.pallas_call(
        partial(select_kernel, pairs),
        out_shape=jax.ShapeDtypeStruct((columns.shape[0], 4 * LANES), jnp.bfloat16),
        in_specs=[in_smem(), in_vmem()],
        out_specs=in_vmem(),
        compiler_params=kernel_params(),
        name="select_heads",
    )(ctx, columns)


def unpack_kernel(
    near, owners, core_ref, dp_ref, ctx_ref, arrived_ref, query_ref, key_ref, value_ref, score_ref, vector_ref, bias_ref
):
    rows = query_ref.shape[0]
    sources = [arrived_ref[core_ref[0] * near + device].astype(jnp.float32) for device in range(near)]
    for head, terms in enumerate(owners):
        for kind, ref in enumerate((query_ref, key_ref, value_ref)):
            at = [kind * LANES + slot * HEAD for _, slot in terms]
            parts = [sources[d][:rows, a : a + HEAD] for (d, _), a in zip(terms, at)]
            ref[:, head * HEAD : (head + 1) * HEAD] = sum(parts[1:], parts[0])

    def line(values, index):
        at = rows + 2 * index
        return jnp.concatenate([values[at : at + 1], values[at + 1 : at + 2]], axis=1)

    total = arrived_ref[0].astype(jnp.float32)
    for device in range(1, arrived_ref.shape[0]):
        total = total + arrived_ref[device].astype(jnp.float32)
    lines = [line(total, 2 + index) for index in range(6)]
    for terms in owners:
        parts = [line(sources[device], slot) for device, slot in terms]
        lines.append(sum(parts[1:], parts[0]))
    width = lines[0].shape[1]
    sublane = lax.broadcasted_iota(jnp.int32, (SCORE_ROWS, width), 0)
    table = jnp.zeros((SCORE_ROWS, width), jnp.float32)
    for index, values in enumerate(lines):
        table = jnp.where(sublane == index, values, table)
    first = dp_ref[0] * rows * arrived_ref.shape[0] + ctx_ref[0] * rows
    table = pltpu.roll(table, width - first, 1)[:, :LANES]
    vector_ref[...] = table[:8, :rows]
    turned = jnp.concatenate([table, jnp.zeros((LANES - SCORE_ROWS, LANES), jnp.float32)], axis=0).T
    score_ref[...] = turned[:rows, 6 : 6 + len(owners)]
    for index in range(2):
        bias_ref[index : index + 1] = line(total, 8 + index)


def unpack_heads(near, owners, core, dp, ctx, arrived, rows):
    lanes = arrived.shape[2]
    shapes = [(rows, lanes)] * 3 + [(rows, len(owners)), (8, rows), (2, 2 * lanes)]
    return pl.pallas_call(
        partial(unpack_kernel, near, owners),
        out_shape=[jax.ShapeDtypeStruct(shape, jnp.float32) for shape in shapes],
        in_specs=[in_smem(), in_smem(), in_smem(), in_vmem()],
        out_specs=[in_vmem()] * 6,
        compiler_params=kernel_params(),
        name="unpack_heads",
    )(core, dp, ctx, arrived)


def finish_kernel(
    pairs, core_ref, arrived_ref, own_ref, other_ref, tokens_ref, middle_ref, gain_ref, out_ref
):
    rows, width = tokens_ref.shape
    near = len(pairs)
    half = width // 2
    total = jnp.zeros((rows, width), jnp.float32)
    for columns_ref, side in ((own_ref, core_ref[0]), (other_ref, 1 - core_ref[0])):
        for device, heads in enumerate(pairs):
            weight = jnp.concatenate(
                [
                    columns_ref[:, kind * half + head * HEAD : kind * half + (head + 1) * HEAD]
                    for kind in range(3)
                    for head in heads
                ],
                axis=1,
            )
            at = side * near + device
            total += lax.dot_general(
                arrived_ref[at, :rows], weight, NT, preferred_element_type=jnp.float32
            )
            lane = lax.broadcasted_iota(jnp.int32, (width, SCORE_ROWS), 1)
            columns = [
                columns_ref[:, 3 * half + head : 3 * half + head + 1].astype(jnp.float32)
                for head in heads
            ]
            weight = jnp.where(lane == 0, columns[0], jnp.where(lane == 1, columns[1], 0.0))
            grads = arrived_ref[at, rows:, :rows].astype(jnp.float32).T
            total += lax.dot_general(
                grads.astype(jnp.bfloat16),
                weight.astype(jnp.bfloat16),
                NT,
                preferred_element_type=jnp.float32,
            )
    hat, scale = normalize(tokens_ref[...].astype(jnp.float32))
    out_ref[...] = middle_ref[...] + normalize_back(total, hat, scale, gain_ref[...])


def finish_tokens(pairs, core, arrived, own_columns, other_columns, tokens, grad_middle, gain):
    return pl.pallas_call(
        partial(finish_kernel, pairs),
        out_shape=jax.ShapeDtypeStruct(grad_middle.shape, jnp.float32),
        in_specs=[in_smem()] + [in_vmem()] * 6,
        out_specs=in_vmem(),
        compiler_params=kernel_params(),
        name="finish_tokens",
    )(core, arrived, own_columns, other_columns, tokens, grad_middle, gain)


def ring_order(count):
    deep = 4 if count % 4 == 0 else 1
    wide = count // deep
    if deep == 1 or wide == 1:
        return list(range(count))
    walk = []
    for place in range(deep):
        across = range(1, wide) if place % 2 == 0 else range(wide - 1, 0, -1)
        walk += [place * wide + at for at in across]
    return walk + [place * wide for place in reversed(range(deep))]


def look_up(rows, index, kind=jnp.uint32):
    table = jnp.asarray(np.asarray(rows), kind)
    return lax.dynamic_slice(table, (index, jnp.uint32(0)), (1, table.shape[1]))[0]


def pick(values, index):
    start = (index,) + (jnp.uint32(0),) * (values.ndim - 1)
    return lax.dynamic_slice(values, start, (1,) + values.shape[1:])[0]


def place_on(axis):
    return lax.axis_index(axis).astype(jnp.uint32)


def ring_distances(count):
    return sorted(range(-(count // 2), (count + 1) // 2), key=lambda d: (abs(d), d))


def ring_places(order):
    count = len(order)
    spots = np.argsort(order)
    return [[order[(spots[me] + d) % count] for d in ring_distances(count)] for me in range(count)]


def ring_hops(order):
    count = len(order)
    forward = [(order[i], order[(i + 1) % count]) for i in range(count)]
    return forward, [(receiver, sender) for sender, receiver in forward]


def ring_gather(values, order):
    count = len(order)
    forward, backward = ring_hops(order)
    held = {0: values}
    for step in range(1, count // 2 + 1):
        held[-step] = lax.ppermute(held[1 - step], "ctx", forward)
        if step < count - step:
            held[step] = lax.ppermute(held[step - 1], "ctx", backward)
    return held


def after(values, *others):
    return lax.optimization_barrier((values, *others))[0]


def ring_scatter(terms, order, places, ties):
    count = len(order)
    forward, backward = ring_hops(order)
    at = {d: places[i] for i, d in enumerate(ring_distances(count))}

    def own(distance):
        here = at.get(distance, at.get(distance - count))
        return sum(pick(term, here).astype(jnp.float32) for term in terms)

    ahead = behind = 0.0
    for step in range(count // 2, 0, -1):
        outgoing = (own(step) + ahead).astype(jnp.bfloat16)
        turn_of = count // 2 - step
        if turn_of in ties:
            outgoing = after(outgoing, ties[turn_of])
        ahead = lax.ppermute(outgoing, "ctx", forward)
        ahead = ahead.astype(jnp.float32)
        if step < count - step:
            behind = lax.ppermute((own(-step) + behind).astype(jnp.bfloat16), "ctx", backward)
            behind = behind.astype(jnp.float32)
    return own(0) + ahead + behind


def dp_terms(values):
    count = values.shape[0]
    places = look_up([[(i + shift) % count for shift in range(count)] for i in range(count)], place_on("dp"))
    terms = [pick(values, places[0])]
    for shift in range(1, count):
        sent = pick(values, places[shift])
        terms.append(lax.ppermute(sent, "dp", [(i, (i + shift) % count) for i in range(count)]))
    return terms


def other_core(values):
    return lax.ppermute(values, "tensor", [(0, 1), (1, 0)])


def normalize(values):
    centred = values - jnp.mean(values, axis=-1, keepdims=True)
    scale = lax.rsqrt(jnp.mean(centred * centred, axis=-1, keepdims=True) + norm_epsilon)
    return centred * scale, scale


def normalize_back(grad, hat, scale, gain):
    scaled = grad * gain
    return scale * (
        scaled
        - jnp.mean(scaled, axis=-1, keepdims=True)
        - hat * jnp.mean(scaled * hat, axis=-1, keepdims=True)
    )


def head_plan(ctx_count, head_count, block):
    parts = 1
    while head_count * parts % ctx_count:
        parts += 1
    share = head_count * parts // ctx_count
    rows = block // parts
    lows, tables = [], []
    for device in range(ctx_count):
        pieces = range(share * device, share * (device + 1))
        lows.append(pieces[0] // parts)
        tables.append(
            [
                (piece // parts - lows[-1], at * block + (piece % parts) * rows)
                + tuple((at + more) * share + order for more in range(parts))
                for order, piece in enumerate(pieces)
                for at in range(0, ctx_count, parts)
            ]
        )
        assert all(entry[0] in (0, 1) for entry in tables[-1])
    assert ctx_count % parts == 0
    return parts, share, rows, lows, np.asarray(tables, np.int32)


def on_device(
    tokens,
    prefix,
    w_query,
    w_key,
    w_value,
    w_score,
    w_attn_out,
    w_fc,
    w_proj,
    ln1_gain,
    ln1_bias,
    ln2_gain,
    ln2_bias,
    attn_bias,
    fc_bias,
    proj_bias,
    cotangent,
    dp_count,
    ctx_count,
):
    f32, bf16 = jnp.float32, jnp.bfloat16
    micro_count, seq_count, block, width = tokens.shape
    local_heads = w_score.shape[1]
    head_count = 2 * local_heads
    assert micro_count == 2 and seq_count == 1
    core = place_on("tensor")
    me = place_on("ctx")
    both = ("dp", "ctx")
    shards = dp_count * ctx_count
    shard_rows = width // shards
    parts, share, rows, lows, tables = head_plan(ctx_count, head_count, block)
    near = ctx_count // 2
    local_low = [low % local_heads for low in lows[:near]]
    local_high = [min(low + 1, local_heads - 1) for low in local_low]

    own_tokens = pick(tokens, core)[0]
    own_cot = pick(cotangent, core)[0]
    other_cot = pick(cotangent, 1 - core)[0]
    own_prefix = pick(prefix, core)
    table = pick(jnp.asarray(tables), me)
    core_number = look_up([[0], [1]], core, jnp.int32)
    dp_number = look_up([[i] for i in range(dp_count)], place_on("dp"), jnp.int32)
    ctx_number = look_up([[i] for i in range(ctx_count)], me, jnp.int32)

    order = ring_order(ctx_count)
    blocks = ring_gather(own_tokens, order)
    places = look_up(ring_places(order), me, jnp.int32)
    ring = look_up(ring_places(order), me)

    def columns(weight, head):
        return weight[:, head * HEAD : (head + 1) * HEAD]

    vectors = jnp.stack([ln1_gain, ln1_bias, ln2_gain, ln2_bias, attn_bias, proj_bias])
    pairs = tuple(zip(local_low, local_high))
    own_columns = pack_heads(vectors, w_query, w_key, w_value, w_score)
    if dp_count == 2:
        other_columns = lax.ppermute(own_columns, "dp", [(0, 1), (1, 0)])
        first_dp = place_on("dp") == 0
        both_columns = jnp.stack(
            [jnp.where(first_dp, own_columns, other_columns), jnp.where(first_dp, other_columns, own_columns)]
        )
    else:
        both_columns = lax.all_gather(own_columns, "dp")
    half_heads = jnp.zeros((dp_count, ctx_count) + own_columns.shape, bf16)
    column_blocks = ring_gather(both_columns, order)
    zero = jnp.uint32(0)
    for spot, distance in enumerate(ring_distances(ctx_count)):
        half_heads = lax.dynamic_update_slice(
            half_heads, column_blocks[distance][:, None], (zero, ring[spot], zero, zero)
        )
    half_heads = half_heads.reshape(width, own_columns.shape[1])
    head_weights = select_heads(pairs, ctx_number, half_heads)
    from_half = (me >= near).astype(jnp.uint32)
    head_weights = jnp.where(from_half == core, head_weights, other_core(head_weights))
    gains = head_weights[:, 3 * LANES + VECTOR_LANE : 3 * LANES + VECTOR_LANE + 6].astype(f32).T
    gain_one, shift_one, gain_two, shift_two, attn_shift, proj_shift = [gains[i : i + 1] for i in range(6)]

    score_columns = head_weights[:, 4 * LANES - 2 :]
    wide_weights = jnp.concatenate(
        [head_weights[:, :LANES] * HEAD**-0.5, head_weights[:, LANES : 3 * LANES]]
        + [jnp.broadcast_to(score_columns[:, i : i + 1], (width, LANES)) for i in range(2)],
        axis=1,
    )
    length = ctx_count * block
    normed = jnp.zeros((length, width), bf16)
    projected = jnp.zeros((length, 5 * LANES), bf16)
    distances = ring_distances(ctx_count)
    early = max(ctx_count - 3, 1)
    for batch, batch_places in ((distances[:early], places[:early]), (distances[early:], places[early:])):
        normed, projected = project(
            batch_places,
            [blocks[d] for d in batch],
            gain_one,
            shift_one,
            wide_weights,
            normed,
            projected,
        )

    packed = jnp.concatenate([w_fc, w_proj.T, w_attn_out.T], axis=1)
    packed = after(packed, column_blocks[-2], column_blocks[2])
    packed = lax.all_gather(packed, both, axis=0, tiled=True)
    attended, attended_low, log_totals, pivots = attend(table, own_prefix, projected, rows, block)
    packed, _ = lax.optimization_barrier((packed, log_totals))
    hidden = w_fc.shape[1]
    full_fc, full_proj_t = packed[:, :hidden], packed[:, hidden : 2 * hidden]
    half_out_t = packed[:, 2 * hidden :]
    other_out_t = other_core(half_out_t)
    out_t = jnp.where(
        core == 0,
        jnp.concatenate([half_out_t, other_out_t], axis=1),
        jnp.concatenate([other_out_t, half_out_t], axis=1),
    )

    sent = attended_low.reshape(ctx_count, share * HEAD, rows)
    merged = lax.all_to_all(sent, "ctx", 0, 0, tiled=True)
    merged = merged.reshape(head_count, parts, HEAD, rows).transpose(0, 2, 1, 3).reshape(width, block)

    own_block = own_tokens.astype(f32)
    attn = lax.dot_general(merged, out_t, (((0,), (1,)), ((), ())), preferred_element_type=f32)
    middle = own_block + attn + attn_shift
    hat_two, scale_two = normalize(middle)
    normed_two = (hat_two * gain_two + shift_two).astype(bf16)
    normed_two = jnp.concatenate([normed_two, other_core(normed_two)])
    hidden_pre = jnp.dot(normed_two, full_fc, preferred_element_type=f32) + fc_bias.astype(f32)
    active, pull_gelu = jax.vjp(partial(jax.nn.gelu, approximate=True), hidden_pre)
    active = active.astype(bf16)
    both_cot = jnp.concatenate([own_cot, other_cot])
    grad_active = jnp.dot(both_cot, full_proj_t, preferred_element_type=f32)
    grad_pre = pull_gelu(grad_active)[0].astype(bf16)
    grad_two = lax.dot_general(grad_pre, full_fc, NT, preferred_element_type=f32)
    grad_two = grad_two[:block] + other_core(grad_two[block:].astype(bf16)).astype(f32)
    cot = own_cot.astype(f32)
    grad_middle = cot + normalize_back(grad_two, hat_two, scale_two, gain_two)
    grad_middle_low = grad_middle.astype(bf16)
    grad_merged = lax.dot_general(
        out_t, grad_middle_low, (((0,), (1,)), ((), ())), preferred_element_type=f32
    ).astype(bf16)
    sent = grad_merged.reshape(head_count, HEAD, parts, rows).transpose(0, 2, 1, 3)
    sent = sent.reshape(ctx_count, share * HEAD, rows)
    grad_attended = lax.all_to_all(sent, "ctx", 0, 0, tiled=True).reshape(attended_low.shape)

    active_last = active
    normed_two, grad_pre_low, active, grad_middle_low, _ = lax.optimization_barrier(
        (normed_two, grad_pre, active, grad_middle_low, sent)
    )
    grad_fc = lax.dot_general(normed_two, grad_pre_low, (((0,), (0,)), ((), ())), preferred_element_type=f32)
    grad_proj_t = lax.dot_general(both_cot, active, (((0,), (0,)), ((), ())), preferred_element_type=f32)
    grad_out_t = lax.dot_general(
        grad_middle_low, merged, (((0,), (1,)), ((), ())), preferred_element_type=f32
    ).astype(bf16)
    half_width = width // 2
    mine, theirs = grad_out_t[:, :half_width], grad_out_t[:, half_width:]
    mine, theirs = jnp.where(core == 0, mine, theirs), jnp.where(core == 0, theirs, mine)
    grad_out_t = (mine.astype(f32) + other_core(theirs).astype(f32)).astype(bf16)
    grad_packed = jnp.concatenate([grad_fc.astype(bf16), grad_proj_t.astype(bf16), grad_out_t], axis=1)
    grad_packed = grad_packed.reshape(dp_count, ctx_count, shard_rows, grad_packed.shape[1])
    grad_packed_terms = dp_terms(grad_packed)
    early_lines = jnp.concatenate(
        [
            jnp.sum(grad_two * hat_two, axis=0, keepdims=True),
            jnp.sum(grad_two, axis=0, keepdims=True),
            jnp.sum(grad_middle, axis=0, keepdims=True),
            jnp.sum(cot, axis=0, keepdims=True),
        ]
    )
    bias_lines = jnp.sum(grad_pre.astype(f32), axis=0).reshape(hidden // width, width)
    bias_lines = jnp.pad(bias_lines, ((0, 8 - bias_lines.shape[0]), (0, 0)))

    message, grads, grad_scores = attend_back(
        table, own_prefix, projected, grad_attended, attended, log_totals, pivots, block
    )

    log_totals_after = grad_scores[:1]
    arrived = lax.all_to_all(message, "ctx", 0, 0, tiled=True)
    active_last = after(active_last, arrived)
    mlp = lax.dot_general(active_last, full_proj_t, NT, preferred_element_type=f32)
    result = middle + mlp[:block] + other_core(mlp[block:].astype(bf16)).astype(f32) + proj_shift
    result = result.astype(bf16)
    half_heads = after(half_heads, log_totals_after)
    other_heads = other_core(half_heads)
    *grad_packed_terms, _ = lax.optimization_barrier((*grad_packed_terms, log_totals_after))
    tokens_grad = finish_tokens(
        pairs, core_number, arrived, half_heads, other_heads, own_tokens, grad_middle, gain_one
    )

    late_grads = after(grads, arrived)
    grad_normed = lax.dot_general(late_grads, head_weights[:, : 3 * LANES], NT, preferred_element_type=f32)
    grad_normed = grad_normed + lax.dot_general(
        grad_scores[:2], score_columns, (((0,), (1,)), ((), ())), preferred_element_type=f32
    )
    hat_one = (normed.astype(f32) - shift_one) / gain_one

    over_rows = (((0,), (0,)), ((), ()))
    grad_heads = lax.dot_general(normed, grads, over_rows, preferred_element_type=f32)
    grad_heads = grad_heads + other_core(grad_heads.astype(bf16)).astype(f32)
    grad_core_sum = grad_heads.astype(bf16)
    grad_heads = dp_terms(
        grad_core_sum.reshape(dp_count, ctx_count, shard_rows, 3 * LANES)
    )
    grad_columns = jnp.dot(grad_scores, normed, preferred_element_type=f32)
    lines = jnp.concatenate(
        [
            grad_columns[:2],
            jnp.sum(grad_normed * hat_one, axis=0, keepdims=True),
            jnp.sum(grad_normed, axis=0, keepdims=True),
            early_lines,
        ]
    )
    lines = lines + other_core(lines.astype(bf16)).astype(f32)
    lines = jnp.concatenate([lines, bias_lines])
    lines = jnp.broadcast_to(lines.astype(bf16)[None], (dp_count,) + lines.shape)
    lines = sum(term.astype(f32) for term in dp_terms(lines)).astype(bf16)
    lines = lines.reshape(2 * lines.shape[0], 3 * LANES)
    message = sum(term.astype(f32) for term in grad_heads).astype(bf16)
    message = jnp.concatenate(
        [message, jnp.broadcast_to(lines[None], (ctx_count,) + lines.shape)], axis=1
    )
    ties = {0: arrived}
    grad_packed = ring_scatter(grad_packed_terms, order, ring, ties)
    message, _ = lax.optimization_barrier((message, arrived))
    arrived = lax.all_to_all(message, "ctx", 0, 0, tiled=True)
    owners = [[] for _ in range(local_heads)]
    for device in range(near):
        for slot in sorted({entry[0] for entry in tables[device].tolist()}):
            owners[local_low[device] + slot].append((device, slot))
    grad_query, grad_key, grad_value, grad_score, vector_grads, fc_bias_grad = unpack_heads(
        near, owners, core_number, dp_number, ctx_number, arrived, shard_rows
    )
    fc_bias_grad = fc_bias_grad.reshape(hidden)

    def both_micro(own):
        other = other_core(own)
        return jnp.where(core == 0, jnp.stack([own, other]), jnp.stack([other, own]))[:, None]

    return (
        both_micro(result),
        both_micro(tokens_grad),
        grad_query,
        grad_key,
        grad_value,
        grad_score,
        grad_packed[:, 2 * hidden :].T,
        grad_packed[:, :hidden],
        grad_packed[:, hidden : 2 * hidden].T,
        vector_grads[0],
        vector_grads[1],
        vector_grads[2],
        vector_grads[3],
        vector_grads[4],
        fc_bias_grad,
        vector_grads[5],
    )


def solution(mesh):
    rows, columns, vector = P(("dp", "ctx"), "tensor"), P("tensor", ("dp", "ctx")), P(("dp", "ctx"))
    tokens = P(None, "dp", "ctx", None)
    in_specs = (
        (tokens, P(None, "dp"))
        + (rows,) * 4
        + (columns, rows, columns)
        + (vector,) * 5
        + (P("tensor"), vector, tokens)
    )
    out_specs = (
        (tokens, tokens)
        + (rows,) * 4
        + (columns, rows, columns)
        + (vector,) * 5
        + (P("tensor"), vector)
    )
    return jax.shard_map(
        partial(on_device, dp_count=mesh.shape["dp"], ctx_count=mesh.shape["ctx"]),
        mesh=mesh,
        in_specs=in_specs,
        out_specs=out_specs,
        check_vma=False,
    )
```

```python
from functools import partial

import jax
import jax.numpy as jnp
import numpy as np
from jax import lax
from jax.experimental import pallas as pl
from jax.experimental.pallas import tpu as pltpu
from jax.sharding import PartitionSpec as P

WIN = 64
TOPK = 64
HEAD = 64
LANES = 128

norm_epsilon = 1e-05
search_steps = 24
search_bound = 64.0

CHUNK = 256
FAR = 1e9
OPEN_PIVOT = -1e6
NEWTON_TOLERANCE = 3e-3
SCORE_ROWS = 16
NT = (((1,), (1,)), ((), ()))


def over_chunks(first, last, prefix, body, carry):
    below = lax.div(jnp.maximum(first - (WIN - 1), 0), CHUNK)
    total = lax.div(jnp.maximum(last + 1, prefix) + CHUNK - 1, CHUNK)
    above = jnp.minimum(lax.div(last + WIN + CHUNK - 1, CHUNK), total)
    whole = jnp.maximum(lax.div(prefix, CHUNK), above)
    carry = lax.fori_loop(0, below, body(False), carry)
    carry = lax.fori_loop(below, above, body(True), carry)
    carry = lax.fori_loop(above, whole, body(False), carry)
    return lax.fori_loop(whole, total, body(True), carry)


def fold(values, how):
    while values.shape[0] > 8:
        half = values.shape[0] // 2
        values = how(values[:half], values[half:])
    return values


def own_head(values, slot):
    lane = lax.broadcasted_iota(jnp.int32, values.shape, 1)
    kept = jnp.where(lax.div(lane, HEAD) == slot, values.astype(jnp.float32), 0.0)
    return kept


def rows_of(first, shape, rows, block):
    lane = lax.broadcasted_iota(jnp.int32, shape, 1)
    return first + lax.div(lane, rows) * block + lax.rem(lane, rows)


def masks(start, first, prefix, rows, block, together):
    shape = (CHUNK, rows * together)
    key = lax.broadcasted_iota(jnp.int32, shape, 0)
    behind = rows_of(first - start, shape, rows, block) - key
    allowed = (behind >= 0) | (key < prefix - start)
    return allowed, allowed & (jnp.abs(behind) < WIN)


def spread_lanes(values, lanes):
    values = values.astype(jnp.float32)
    return jnp.concatenate([values] * (lanes // LANES), axis=1)


def turn(source_ref, lanes, target_ref):
    def run(chunk, _):
        here = pl.ds(pl.multiple_of(chunk * CHUNK, CHUNK), CHUNK)
        flipped = source_ref[here, lanes : lanes + LANES].astype(jnp.float32).T
        target_ref[:, here] = flipped.astype(jnp.bfloat16)
        return 0

    lax.fori_loop(0, source_ref.shape[0] // CHUNK, run, 0)


def forward_kernel(
    block, table, prefix_ref, p_ref, o_ref, low_ref, lse_ref, pivot_ref, sm_ref, st_ref, vt_ref
):
    unit_count, _, lanes = o_ref.shape
    rows = low_ref.shape[2]
    together = lanes // rows
    prefix = prefix_ref[0]
    turn(p_ref, 2 * LANES, vt_ref)

    def unit(step, guess):
        slot, first = table[step, 0], table[step, 1]
        last = first + (together - 1) * block + rows - 1
        query = jnp.concatenate(
            [
                p_ref[pl.ds(pl.multiple_of(first + at * block, rows), rows), 0:LANES]
                for at in range(together)
            ],
            axis=0,
        )
        query_t = own_head(query, slot).T.astype(jnp.bfloat16)
        score_lane = pl.multiple_of((3 + slot) * LANES, LANES)

        def build(masked):
            def run(chunk, top):
                start = pl.multiple_of(chunk * CHUNK, CHUNK)
                here = pl.ds(start, CHUNK)
                logits = jnp.dot(
                    p_ref[here, LANES : 2 * LANES], query_t, preferred_element_type=jnp.float32
                )
                score = spread_lanes(p_ref[here, pl.ds(score_lane, LANES)], lanes)
                if masked:
                    allowed, local = masks(start, first, prefix, rows, block, together)
                    logits = jnp.where(allowed, logits, -1e30)
                    score = jnp.where(local, FAR, jnp.where(allowed, score, -FAR))
                    top = jnp.maximum(top, fold(jnp.where(local, logits, -1e30), jnp.maximum))
                st_ref[here, :] = logits
                sm_ref[here, :] = score
                return top

            return run

        top = over_chunks(first, last, prefix, build, jnp.full((8, lanes), -1e30, jnp.float32))
        top = jnp.max(top, axis=0, keepdims=True)

        row = rows_of(first, (1, lanes), rows, block)
        local_count = (
            jnp.minimum(row, WIN - 1) + 1 + jnp.clip(prefix - 1 - row, 0, WIN - 1)
        ).astype(jnp.float32)
        candidates = jnp.maximum(row + 1, prefix).astype(jnp.float32) - local_count
        chunks = lax.div(jnp.maximum(last + 1, prefix) + CHUNK - 1, CHUNK)
        entries = (chunks * CHUNK).astype(jnp.float32)
        searched = candidates > TOPK
        count = jnp.maximum(candidates, TOPK + 1.0)
        goal = jnp.log(TOPK / (count - TOPK))

        def measure(half):
            def run(chunk, sums):
                bent = jnp.tanh(sm_ref[pl.ds(pl.multiple_of(chunk * CHUNK, CHUNK), CHUNK), :] - half)
                return sums[0] + fold(bent, jnp.add), sums[1] + fold(bent * bent, jnp.add)

            zero = jnp.zeros((8, lanes), jnp.float32)
            first_sum, second_sum = lax.fori_loop(0, chunks, run, (zero, zero))
            filled = 0.5 * (entries + jnp.sum(first_sum, axis=0, keepdims=True)) - local_count
            slope = 0.25 * (entries - jnp.sum(second_sum, axis=0, keepdims=True))
            return filled, slope

        def improve(state):
            turn, _, half, lower, upper, done = state
            filled, slope = measure(half)
            above = filled > TOPK
            lower = jnp.where(above, half, lower)
            upper = jnp.where(above, upper, half)
            newton = (filled - TOPK) / slope
            held = jnp.clip(filled, 1e-3, count - 1e-3)
            bent = (jnp.log(held / (count - held)) - goal) * (held * (count - held) / (count * slope))
            close = jnp.abs(newton) <= NEWTON_TOLERANCE
            following = half + 0.5 * jnp.where(close, newton, bent)
            inside = (following > lower) & (following < upper)
            halve = (turn >= 12) & (lax.rem(turn, 2) == 1)
            middle = 0.5 * (lower + upper)
            following = jnp.where(close | (inside & jnp.logical_not(halve)), following, middle)
            half = jnp.where(done > 0.0, half, following)
            done = jnp.where(close, 1.0, done)
            return turn + 1, jnp.min(done), half, lower, upper, done

        start_done = jnp.where(searched, 0.0, 1.0)
        bound = jnp.full((1, lanes), 0.5 * search_bound, jnp.float32)
        _, _, half, lower, upper, done = lax.while_loop(
            lambda state: (state[0] < 12 + 2 * search_steps) & (state[1] < 0.5),
            improve,
            (0, jnp.min(start_done), guess, -bound, bound, start_done),
        )
        half = jnp.where(done > 0.0, half, 0.5 * (lower + upper))
        pivot = jnp.where(searched, half, OPEN_PIVOT)

        def weigh(chunk, sums):
            here = pl.ds(pl.multiple_of(chunk * CHUNK, CHUNK), CHUNK)
            raised = jnp.exp(st_ref[here, :] - top)
            weight = raised / (1.0 + jnp.exp(2.0 * (pivot - sm_ref[here, :])))
            merged = sums[1] + jnp.dot(
                vt_ref[:, here], weight.astype(jnp.bfloat16), preferred_element_type=jnp.float32
            )
            return sums[0] + fold(weight, jnp.add), merged

        total, merged = lax.fori_loop(
            0,
            chunks,
            weigh,
            (jnp.zeros((8, lanes), jnp.float32), jnp.zeros((LANES, lanes), jnp.float32)),
        )
        total = jnp.sum(total, axis=0, keepdims=True)
        merged = merged / total
        own = jnp.where(slot == 0, merged[:HEAD], merged[HEAD:])
        o_ref[step] = own
        for at in range(together):
            low_ref[table[step, 2 + at]] = own[:, at * rows : (at + 1) * rows].astype(jnp.bfloat16)
        lse_ref[step] = top + jnp.log(total)
        pivot_ref[step] = pivot
        return jnp.where(searched, half, guess)

    lax.fori_loop(0, unit_count, unit, jnp.zeros((1, lanes), jnp.float32))


def backward_kernel(
    block,
    table,
    prefix_ref,
    p_ref,
    do_ref,
    o_ref,
    lse_ref,
    pivot_ref,
    message_ref,
    d_ref,
    score_ref,
    dq_ref,
    dk_ref,
    dv_ref,
    ds_ref,
    kt_ref,
):
    unit_count, _, lanes = o_ref.shape
    rows = do_ref.shape[2]
    together = lanes // rows
    length = p_ref.shape[0]
    prefix = prefix_ref[0]
    turn(p_ref, LANES, kt_ref)

    def clear(chunk, _):
        here = pl.ds(pl.multiple_of(chunk * CHUNK, CHUNK), CHUNK)
        for ref in (dq_ref, dk_ref, dv_ref):
            ref[here, :] = jnp.zeros((CHUNK, LANES), jnp.float32)
        for slot in range(2):
            ds_ref[slot, here, :] = jnp.zeros((CHUNK, LANES), jnp.float32)
        return 0

    lax.fori_loop(0, length // CHUNK, clear, 0)

    def unit(step, _):
        slot, first = table[step, 0], table[step, 1]
        last = first + (together - 1) * block + rows - 1
        whose = [pl.ds(pl.multiple_of(first + at * block, rows), rows) for at in range(together)]
        query = own_head(jnp.concatenate([p_ref[here, 0:LANES] for here in whose], axis=0), slot)
        query_t = query.T.astype(jnp.bfloat16)
        query = query.astype(jnp.bfloat16)
        grad = jnp.concatenate([do_ref[table[step, 2 + at]] for at in range(together)], axis=1)
        grad = grad.astype(jnp.float32)
        row_dot = jnp.sum(grad * o_ref[step], axis=0, keepdims=True)
        empty = jnp.zeros_like(grad)
        grad = jnp.where(
            slot == 0,
            jnp.concatenate([grad, empty], axis=0),
            jnp.concatenate([empty, grad], axis=0),
        )
        grad_t = grad.T.astype(jnp.bfloat16)
        grad = grad.astype(jnp.bfloat16)
        lse, pivot = lse_ref[step], pivot_ref[step]
        score_lane = pl.multiple_of((3 + slot) * LANES, LANES)

        def body(masked):
            def run(chunk, grad_query):
                start = pl.multiple_of(chunk * CHUNK, CHUNK)
                here = pl.ds(start, CHUNK)
                logits = jnp.dot(
                    p_ref[here, LANES : 2 * LANES], query_t, preferred_element_type=jnp.float32
                )
                grad_probs = jnp.dot(
                    p_ref[here, 2 * LANES : 3 * LANES], grad, preferred_element_type=jnp.float32
                )
                score = spread_lanes(p_ref[here, pl.ds(score_lane, LANES)], lanes)
                if masked:
                    allowed, local = masks(start, first, prefix, rows, block, together)
                    logits = jnp.where(allowed, logits, -1e30)
                    score = jnp.where(local, FAR, jnp.where(allowed, score, -FAR))
                unit_probs = jnp.exp(logits - lse)
                gate = 1.0 / (1.0 + jnp.exp(2.0 * (pivot - score)))
                probs = gate * unit_probs
                grad_logits = probs * (grad_probs - row_dot)
                grad_score = grad_logits * (1.0 - gate)
                folded = grad_score[:, :LANES]
                for lane in range(LANES, lanes, LANES):
                    folded = folded + grad_score[:, lane : lane + LANES]
                ds_ref[slot, here, :] += folded
                low = grad_logits.astype(jnp.bfloat16)
                dk_ref[here, :] += jnp.dot(low, query, preferred_element_type=jnp.float32)
                dv_ref[here, :] += jnp.dot(
                    probs.astype(jnp.bfloat16), grad_t, preferred_element_type=jnp.float32
                )
                return grad_query + jnp.dot(
                    kt_ref[:, here], low, preferred_element_type=jnp.float32
                )

            return run

        grad_query = over_chunks(
            first, last, prefix, body, jnp.zeros((LANES, lanes), jnp.float32)
        ).T
        lane = lax.broadcasted_iota(jnp.int32, grad_query.shape, 1)
        grad_query = jnp.where(lax.div(lane, HEAD) == slot, grad_query, 0.0)
        for at, here in enumerate(whose):
            dq_ref[here, :] += grad_query[at * rows : (at + 1) * rows]
        return 0

    lax.fori_loop(0, unit_count, unit, 0)

    def finish(chunk, _):
        here = pl.ds(pl.multiple_of(chunk * CHUNK, CHUNK), CHUNK)
        lane = lax.broadcasted_iota(jnp.int32, (CHUNK, LANES), 1)
        columns = [jnp.sum(ds_ref[slot, here, :], axis=1, keepdims=True) for slot in range(2)]
        grad_score = jnp.where(lane == 0, columns[0], jnp.where(lane == 1, columns[1], 0.0))
        grad_score = grad_score.T[:SCORE_ROWS].astype(jnp.bfloat16)
        score_ref[:, here] = grad_score
        message_ref[chunk, CHUNK:, 0:CHUNK] = grad_score
        message_ref[chunk, CHUNK:, CHUNK:] = jnp.zeros_like(message_ref[chunk, CHUNK:, CHUNK:])
        grads = (dq_ref[here, :] * HEAD**-0.5, dk_ref[here, :], dv_ref[here, :])
        for kind, grad in enumerate(grads):
            low = grad.astype(jnp.bfloat16)
            d_ref[here, kind * LANES : (kind + 1) * LANES] = low
            message_ref[chunk, 0:CHUNK, kind * LANES : (kind + 1) * LANES] = low
        return 0

    lax.fori_loop(0, length // CHUNK, finish, 0)


VMEM_LIMIT = 48 * 1024 * 1024


def kernel_params():
    return pltpu.CompilerParams(vmem_limit_bytes=VMEM_LIMIT)


def in_vmem():
    return pl.BlockSpec(memory_space=pltpu.VMEM)


def in_smem():
    return pl.BlockSpec(memory_space=pltpu.SMEM)


def attend(table, prefix, projected, rows, block):
    unit_count = table.shape[0]
    together = table.shape[1] - 2
    lanes = rows * together
    length = projected.shape[0]
    pairs = unit_count * lanes * length
    return pl.pallas_call(
        partial(forward_kernel, block),
        out_shape=(
            jax.ShapeDtypeStruct((unit_count, HEAD, lanes), jnp.float32),
            jax.ShapeDtypeStruct((unit_count * together, HEAD, rows), jnp.bfloat16),
            jax.ShapeDtypeStruct((unit_count, 1, lanes), jnp.float32),
            jax.ShapeDtypeStruct((unit_count, 1, lanes), jnp.float32),
        ),
        in_specs=[in_smem(), in_smem(), in_vmem()],
        out_specs=(in_vmem(),) * 4,
        scratch_shapes=[
            pltpu.VMEM((length, lanes), jnp.float32),
            pltpu.VMEM((length, lanes), jnp.float32),
            pltpu.VMEM((LANES, length), jnp.bfloat16),
        ],
        compiler_params=kernel_params(),
        cost_estimate=pl.CostEstimate(
            flops=pairs * 12000, bytes_accessed=projected.size * 4, transcendentals=pairs * 8
        ),
        name="attend",
    )(table, prefix, projected)


def attend_back(table, prefix, projected, grads, attended, log_totals, pivots, block):
    unit_count, _, lanes = attended.shape
    length = projected.shape[0]
    pairs = unit_count * lanes * length
    return pl.pallas_call(
        partial(backward_kernel, block),
        out_shape=(
            jax.ShapeDtypeStruct((length // CHUNK, CHUNK + SCORE_ROWS, 3 * LANES), jnp.bfloat16),
            jax.ShapeDtypeStruct((length, 3 * LANES), jnp.bfloat16),
            jax.ShapeDtypeStruct((SCORE_ROWS, length), jnp.bfloat16),
        ),
        in_specs=[in_smem(), in_smem()] + [in_vmem()] * 5,
        out_specs=(in_vmem(),) * 3,
        scratch_shapes=[
            pltpu.VMEM((length, LANES), jnp.float32),
            pltpu.VMEM((length, LANES), jnp.float32),
            pltpu.VMEM((length, LANES), jnp.float32),
            pltpu.VMEM((2, length, LANES), jnp.float32),
            pltpu.VMEM((LANES, length), jnp.bfloat16),
        ],
        compiler_params=kernel_params(),
        cost_estimate=pl.CostEstimate(
            flops=pairs * 9000, bytes_accessed=projected.size * 4, transcendentals=pairs * 3
        ),
        name="attend_back",
    )(table, prefix, projected, grads, attended, log_totals, pivots)


def project_kernel(count, offset, *refs):
    tokens, (gain_ref, shift_ref, weight_ref, _, __, normed_ref, projected_ref) = refs[:count], refs[count:]
    for step, tokens_ref in enumerate(tokens):

        @pl.when(pl.program_id(0) == step)
        def _(tokens_ref=tokens_ref):
            hat, _ = normalize(tokens_ref[...].astype(jnp.float32))
            normed = (hat * gain_ref[...] + shift_ref[...]).astype(jnp.bfloat16)
            normed_ref[...] = normed
            low = jnp.dot(normed, weight_ref[...], preferred_element_type=jnp.float32)
            low = low.astype(jnp.bfloat16).astype(jnp.float32)
            lane = lax.broadcasted_iota(jnp.int32, low.shape, 1)
            projected_ref[...] = jnp.where(lane < 3 * LANES, low, 0.5 * low).astype(jnp.bfloat16)


def project(places, tokens, gain, shift, weight, normed, projected):
    count = len(tokens)
    rows, width = tokens[0].shape
    columns = weight.shape[1]

    def whole(shape):
        return pl.BlockSpec(shape, lambda i, at: (0, 0))

    anywhere = pl.BlockSpec(memory_space=pl.ANY)
    return pl.pallas_call(
        partial(project_kernel, count),
        grid_spec=pltpu.PrefetchScalarGridSpec(
            num_scalar_prefetch=1,
            grid=(count,),
            in_specs=[whole((rows, width))] * count
            + [whole((1, width)), whole((1, width)), whole((width, columns)), anywhere, anywhere],
            out_specs=(
                pl.BlockSpec((rows, width), lambda i, at: (at[i], 0)),
                pl.BlockSpec((rows, columns), lambda i, at: (at[i], 0)),
            ),
        ),
        out_shape=(
            jax.ShapeDtypeStruct(normed.shape, normed.dtype),
            jax.ShapeDtypeStruct(projected.shape, projected.dtype),
        ),
        input_output_aliases={count + 4: 0, count + 5: 1},
        compiler_params=kernel_params(),
        cost_estimate=pl.CostEstimate(
            flops=2 * count * rows * width * columns * 20,
            bytes_accessed=rows * width * 12,
            transcendentals=0,
        ),
        name="project",
    )(places, *tokens, gain, shift, weight, normed, projected)


VECTOR_LANE = 8


def pack_kernel(vector_ref, query_ref, key_ref, value_ref, score_ref, out_ref):
    rows, width = query_ref.shape
    for kind, ref in enumerate((query_ref, key_ref, value_ref)):
        out_ref[:, kind * width : (kind + 1) * width] = ref[...]
    tail = vector_ref[...].astype(jnp.float32).T[:rows]
    lane = lax.broadcasted_iota(jnp.int32, tail.shape, 1)
    for head in range(score_ref.shape[1]):
        tail = jnp.where(lane == head, score_ref[:, head : head + 1].astype(jnp.float32), tail)
    out_ref[:, 3 * width :] = tail.astype(jnp.bfloat16)


def pack_heads(vectors, query, key, value, score):
    below = LANES - VECTOR_LANE - vectors.shape[0]
    return pl.pallas_call(
        pack_kernel,
        out_shape=jax.ShapeDtypeStruct((query.shape[0], 3 * query.shape[1] + LANES), jnp.bfloat16),
        in_specs=[in_vmem()] * 5,
        out_specs=in_vmem(),
        compiler_params=kernel_params(),
        name="pack_heads",
    )(jnp.pad(vectors, ((VECTOR_LANE, below), (0, LANES - vectors.shape[1]))), query, key, value, score)


def select_kernel(pairs, ctx_ref, columns_ref, out_ref):
    half = (columns_ref.shape[1] - LANES) // 3
    for pattern, heads in enumerate(pairs):

        @pl.when(lax.rem(ctx_ref[0], len(pairs)) == pattern)
        def _(heads=heads):
            for kind in range(3):
                starts = [kind * half + head * HEAD for head in heads]
                out_ref[:, kind * LANES : (kind + 1) * LANES] = jnp.concatenate(
                    [columns_ref[:, at : at + HEAD] for at in starts], axis=1
                )
            tail = columns_ref[:, 3 * half :].astype(jnp.float32)
            lane = lax.broadcasted_iota(jnp.int32, tail.shape, 1)
            for slot, head in enumerate(heads):
                tail = jnp.where(lane == LANES - 2 + slot, tail[:, head : head + 1], tail)
            out_ref[:, 3 * LANES :] = tail.astype(jnp.bfloat16)


def select_heads(pairs, ctx, columns):
    return pl.pallas_call(
        partial(select_kernel, pairs),
        out_shape=jax.ShapeDtypeStruct((columns.shape[0], 4 * LANES), jnp.bfloat16),
        in_specs=[in_smem(), in_vmem()],
        out_specs=in_vmem(),
        compiler_params=kernel_params(),
        name="select_heads",
    )(ctx, columns)


def unpack_kernel(
    near, owners, core_ref, dp_ref, ctx_ref, arrived_ref, query_ref, key_ref, value_ref, score_ref, vector_ref, bias_ref
):
    rows = query_ref.shape[0]
    sources = [arrived_ref[core_ref[0] * near + device].astype(jnp.float32) for device in range(near)]
    for head, terms in enumerate(owners):
        for kind, ref in enumerate((query_ref, key_ref, value_ref)):
            at = [kind * LANES + slot * HEAD for _, slot in terms]
            parts = [sources[d][:rows, a : a + HEAD] for (d, _), a in zip(terms, at)]
            ref[:, head * HEAD : (head + 1) * HEAD] = sum(parts[1:], parts[0])

    def line(values, index):
        at = rows + 2 * index
        return jnp.concatenate([values[at : at + 1], values[at + 1 : at + 2]], axis=1)

    total = arrived_ref[0].astype(jnp.float32)
    for device in range(1, arrived_ref.shape[0]):
        total = total + arrived_ref[device].astype(jnp.float32)
    lines = [line(total, 2 + index) for index in range(6)]
    for terms in owners:
        parts = [line(sources[device], slot) for device, slot in terms]
        lines.append(sum(parts[1:], parts[0]))
    width = lines[0].shape[1]
    sublane = lax.broadcasted_iota(jnp.int32, (SCORE_ROWS, width), 0)
    table = jnp.zeros((SCORE_ROWS, width), jnp.float32)
    for index, values in enumerate(lines):
        table = jnp.where(sublane == index, values, table)
    first = dp_ref[0] * rows * arrived_ref.shape[0] + ctx_ref[0] * rows
    table = pltpu.roll(table, width - first, 1)[:, :LANES]
    vector_ref[...] = table[:8, :rows]
    turned = jnp.concatenate([table, jnp.zeros((LANES - SCORE_ROWS, LANES), jnp.float32)], axis=0).T
    score_ref[...] = turned[:rows, 6 : 6 + len(owners)]
    for index in range(2):
        bias_ref[index : index + 1] = line(total, 8 + index)


def unpack_heads(near, owners, core, dp, ctx, arrived, rows):
    lanes = arrived.shape[2]
    shapes = [(rows, lanes)] * 3 + [(rows, len(owners)), (8, rows), (2, 2 * lanes)]
    return pl.pallas_call(
        partial(unpack_kernel, near, owners),
        out_shape=[jax.ShapeDtypeStruct(shape, jnp.float32) for shape in shapes],
        in_specs=[in_smem(), in_smem(), in_smem(), in_vmem()],
        out_specs=[in_vmem()] * 6,
        compiler_params=kernel_params(),
        name="unpack_heads",
    )(core, dp, ctx, arrived)


def arrange_kernel(pairs, core_ref, own_ref, other_ref, out_ref, score_ref):
    width = own_ref.shape[0]
    near = len(pairs)
    half = width // 2
    lane = lax.broadcasted_iota(jnp.int32, (width, SCORE_ROWS), 1)
    for columns_ref, side in ((own_ref, core_ref[0]), (other_ref, 1 - core_ref[0])):
        for device, heads in enumerate(pairs):
            at = side * near + device
            out_ref[at] = jnp.concatenate(
                [
                    columns_ref[:, kind * half + head * HEAD : kind * half + (head + 1) * HEAD]
                    for kind in range(3)
                    for head in heads
                ],
                axis=1,
            )
            columns = [
                columns_ref[:, 3 * half + head : 3 * half + head + 1].astype(jnp.float32)
                for head in heads
            ]
            score = jnp.where(lane == 0, columns[0], jnp.where(lane == 1, columns[1], 0.0))
            score_ref[at] = score.astype(jnp.bfloat16)


def arrange_heads(pairs, core, own_columns, other_columns):
    width = own_columns.shape[0]
    count = 2 * len(pairs)
    return pl.pallas_call(
        partial(arrange_kernel, pairs),
        out_shape=(
            jax.ShapeDtypeStruct((count, width, 3 * LANES), jnp.bfloat16),
            jax.ShapeDtypeStruct((count, width, SCORE_ROWS), jnp.bfloat16),
        ),
        in_specs=[in_smem()] + [in_vmem()] * 2,
        out_specs=(in_vmem(),) * 2,
        compiler_params=kernel_params(),
        name="arrange_heads",
    )(core, own_columns, other_columns)


def finish_kernel(arrived_ref, weight_ref, score_ref, tokens_ref, middle_ref, gain_ref, out_ref):
    rows, width = tokens_ref.shape
    total = jnp.zeros((rows, width), jnp.float32)
    for device in range(arrived_ref.shape[0]):
        total += lax.dot_general(
            arrived_ref[device, :rows], weight_ref[device], NT, preferred_element_type=jnp.float32
        )
        grads = arrived_ref[device, rows:, :rows].astype(jnp.float32).T.astype(jnp.bfloat16)
        total += lax.dot_general(grads, score_ref[device], NT, preferred_element_type=jnp.float32)
    hat, scale = normalize(tokens_ref[...].astype(jnp.float32))
    out_ref[...] = middle_ref[...] + normalize_back(total, hat, scale, gain_ref[...])


def finish_tokens(arrived, weights, scores, tokens, grad_middle, gain):
    return pl.pallas_call(
        finish_kernel,
        out_shape=jax.ShapeDtypeStruct(grad_middle.shape, jnp.float32),
        in_specs=[in_vmem()] * 6,
        out_specs=in_vmem(),
        compiler_params=kernel_params(),
        name="finish_tokens",
    )(arrived, weights, scores, tokens, grad_middle, gain)


def ring_order(count):
    deep = 4 if count % 4 == 0 else 1
    wide = count // deep
    if deep == 1 or wide == 1:
        return list(range(count))
    walk = []
    for place in range(deep):
        across = range(1, wide) if place % 2 == 0 else range(wide - 1, 0, -1)
        walk += [place * wide + at for at in across]
    return walk + [place * wide for place in reversed(range(deep))]


def look_up(rows, index, kind=jnp.uint32):
    table = jnp.asarray(np.asarray(rows), kind)
    return lax.dynamic_slice(table, (index, jnp.uint32(0)), (1, table.shape[1]))[0]


def pick(values, index):
    start = (index,) + (jnp.uint32(0),) * (values.ndim - 1)
    return lax.dynamic_slice(values, start, (1,) + values.shape[1:])[0]


def place_on(axis):
    return lax.axis_index(axis).astype(jnp.uint32)


def ring_distances(count):
    return sorted(range(-(count // 2), (count + 1) // 2), key=lambda d: (abs(d), d))


def ring_places(order):
    count = len(order)
    spots = np.argsort(order)
    return [[order[(spots[me] + d) % count] for d in ring_distances(count)] for me in range(count)]


def ring_hops(order):
    count = len(order)
    forward = [(order[i], order[(i + 1) % count]) for i in range(count)]
    return forward, [(receiver, sender) for sender, receiver in forward]


def ring_gather(values, order):
    count = len(order)
    forward, backward = ring_hops(order)
    held = {0: values}
    for step in range(1, count // 2 + 1):
        held[-step] = lax.ppermute(held[1 - step], "ctx", forward)
        if step < count - step:
            held[step] = lax.ppermute(held[step - 1], "ctx", backward)
    return held


def after(values, *others):
    return lax.optimization_barrier((values, *others))[0]


def ring_scatter(values, order, places, starts):
    count = len(order)
    forward, backward = ring_hops(order)
    at = {d: places[i] for i, d in enumerate(ring_distances(count))}

    def own(distance):
        here = at.get(distance, at.get(distance - count))
        return pick(values, here).astype(jnp.float32)

    ahead = behind = 0.0
    arrivals = []
    for step in range(count // 2, 0, -1):
        outgoing = (own(step) + ahead).astype(jnp.bfloat16)
        hop = len(arrivals)
        if hop < len(starts):
            outgoing = after(outgoing, *starts[hop])
        ahead = lax.ppermute(outgoing, "ctx", forward)
        arrivals.append(ahead)
        ahead = ahead.astype(jnp.float32)
        if step < count - step:
            outgoing = (own(-step) + behind).astype(jnp.bfloat16)
            if hop < len(starts):
                outgoing = after(outgoing, *starts[hop])
            behind = lax.ppermute(outgoing, "ctx", backward)
            behind = behind.astype(jnp.float32)
    return own(0) + ahead + behind, arrivals


def dp_terms(values):
    count = values.shape[0]
    places = look_up([[(i + shift) % count for shift in range(count)] for i in range(count)], place_on("dp"))
    terms = [pick(values, places[0])]
    for shift in range(1, count):
        sent = pick(values, places[shift])
        terms.append(lax.ppermute(sent, "dp", [(i, (i + shift) % count) for i in range(count)]))
    return terms


def other_core(values):
    return lax.ppermute(values, "tensor", [(0, 1), (1, 0)])


def normalize(values):
    centred = values - jnp.mean(values, axis=-1, keepdims=True)
    scale = lax.rsqrt(jnp.mean(centred * centred, axis=-1, keepdims=True) + norm_epsilon)
    return centred * scale, scale


def normalize_back(grad, hat, scale, gain):
    scaled = grad * gain
    return scale * (
        scaled
        - jnp.mean(scaled, axis=-1, keepdims=True)
        - hat * jnp.mean(scaled * hat, axis=-1, keepdims=True)
    )


def head_plan(ctx_count, head_count, block):
    parts = 1
    while head_count * parts % ctx_count:
        parts += 1
    share = head_count * parts // ctx_count
    rows = block // parts
    lows, tables = [], []
    for device in range(ctx_count):
        pieces = range(share * device, share * (device + 1))
        lows.append(pieces[0] // parts)
        tables.append(
            [
                (piece // parts - lows[-1], at * block + (piece % parts) * rows)
                + tuple((at + more) * share + order for more in range(parts))
                for order, piece in enumerate(pieces)
                for at in range(0, ctx_count, parts)
            ]
        )
        assert all(entry[0] in (0, 1) for entry in tables[-1])
    assert ctx_count % parts == 0
    return parts, share, rows, lows, np.asarray(tables, np.int32)


def on_device(
    tokens,
    prefix,
    w_query,
    w_key,
    w_value,
    w_score,
    w_attn_out,
    w_fc,
    w_proj,
    ln1_gain,
    ln1_bias,
    ln2_gain,
    ln2_bias,
    attn_bias,
    fc_bias,
    proj_bias,
    cotangent,
    dp_count,
    ctx_count,
):
    f32, bf16 = jnp.float32, jnp.bfloat16
    micro_count, seq_count, block, width = tokens.shape
    local_heads = w_score.shape[1]
    head_count = 2 * local_heads
    assert micro_count == 2 and seq_count == 1
    core = place_on("tensor")
    me = place_on("ctx")
    both = ("dp", "ctx")
    shards = dp_count * ctx_count
    shard_rows = width // shards
    parts, share, rows, lows, tables = head_plan(ctx_count, head_count, block)
    near = ctx_count // 2
    local_low = [low % local_heads for low in lows[:near]]
    local_high = [min(low + 1, local_heads - 1) for low in local_low]

    own_tokens = pick(tokens, core)[0]
    own_cot = pick(cotangent, core)[0]
    other_cot = pick(cotangent, 1 - core)[0]
    own_prefix = pick(prefix, core)
    table = pick(jnp.asarray(tables), me)
    core_number = look_up([[0], [1]], core, jnp.int32)
    dp_number = look_up([[i] for i in range(dp_count)], place_on("dp"), jnp.int32)
    ctx_number = look_up([[i] for i in range(ctx_count)], me, jnp.int32)

    order = ring_order(ctx_count)
    blocks = ring_gather(own_tokens, order)
    places = look_up(ring_places(order), me, jnp.int32)
    ring = look_up(ring_places(order), me)

    def columns(weight, head):
        return weight[:, head * HEAD : (head + 1) * HEAD]

    vectors = jnp.stack([ln1_gain, ln1_bias, ln2_gain, ln2_bias, attn_bias, proj_bias])
    pairs = tuple(zip(local_low, local_high))
    own_columns = pack_heads(vectors, w_query, w_key, w_value, w_score)
    if dp_count == 2:
        other_columns = lax.ppermute(own_columns, "dp", [(0, 1), (1, 0)])
        first_dp = place_on("dp") == 0
        both_columns = jnp.stack(
            [jnp.where(first_dp, own_columns, other_columns), jnp.where(first_dp, other_columns, own_columns)]
        )
    else:
        both_columns = lax.all_gather(own_columns, "dp")
    half_heads = jnp.zeros((dp_count, ctx_count) + own_columns.shape, bf16)
    column_blocks = ring_gather(both_columns, order)
    zero = jnp.uint32(0)
    for spot, distance in enumerate(ring_distances(ctx_count)):
        half_heads = lax.dynamic_update_slice(
            half_heads, column_blocks[distance][:, None], (zero, ring[spot], zero, zero)
        )
    half_heads = half_heads.reshape(width, own_columns.shape[1])
    head_weights = select_heads(pairs, ctx_number, half_heads)
    from_half = (me >= near).astype(jnp.uint32)
    head_weights = jnp.where(from_half == core, head_weights, other_core(head_weights))
    gains = head_weights[:, 3 * LANES + VECTOR_LANE : 3 * LANES + VECTOR_LANE + 6].astype(f32).T
    gain_one, shift_one, gain_two, shift_two, attn_shift, proj_shift = [gains[i : i + 1] for i in range(6)]

    score_columns = head_weights[:, 4 * LANES - 2 :]
    wide_weights = jnp.concatenate(
        [head_weights[:, :LANES] * HEAD**-0.5, head_weights[:, LANES : 3 * LANES]]
        + [jnp.broadcast_to(score_columns[:, i : i + 1], (width, LANES)) for i in range(2)],
        axis=1,
    )
    length = ctx_count * block
    normed = jnp.zeros((length, width), bf16)
    projected = jnp.zeros((length, 5 * LANES), bf16)
    distances = ring_distances(ctx_count)
    early = max(ctx_count - 3, 1)
    for batch, batch_places in ((distances[:early], places[:early]), (distances[early:], places[early:])):
        normed, projected = project(
            batch_places,
            [blocks[d] for d in batch],
            gain_one,
            shift_one,
            wide_weights,
            normed,
            projected,
        )

    packed = jnp.concatenate([w_fc, w_proj.T, w_attn_out.T], axis=1)
    packed = after(packed, column_blocks[-2], column_blocks[2])
    packed = lax.all_gather(packed, both, axis=0, tiled=True)
    attended, attended_low, log_totals, pivots = attend(table, own_prefix, projected, rows, block)
    packed, _ = lax.optimization_barrier((packed, log_totals))
    hidden = w_fc.shape[1]
    full_fc, full_proj_t = packed[:, :hidden], packed[:, hidden : 2 * hidden]
    half_out_t = packed[:, 2 * hidden :]
    other_out_t = other_core(half_out_t)
    out_t = jnp.where(
        core == 0,
        jnp.concatenate([half_out_t, other_out_t], axis=1),
        jnp.concatenate([other_out_t, half_out_t], axis=1),
    )

    sent = attended_low.reshape(ctx_count, share * HEAD, rows)
    merged = lax.all_to_all(sent, "ctx", 0, 0, tiled=True)
    merged = merged.reshape(head_count, parts, HEAD, rows).transpose(0, 2, 1, 3).reshape(width, block)

    own_block = own_tokens.astype(f32)
    attn = lax.dot_general(merged, out_t, (((0,), (1,)), ((), ())), preferred_element_type=f32)
    middle = own_block + attn + attn_shift
    hat_two, scale_two = normalize(middle)
    normed_two = (hat_two * gain_two + shift_two).astype(bf16)
    normed_two = jnp.concatenate([normed_two, other_core(normed_two)])
    hidden_pre = jnp.dot(normed_two, full_fc, preferred_element_type=f32) + fc_bias.astype(f32)
    active, pull_gelu = jax.vjp(partial(jax.nn.gelu, approximate=True), hidden_pre)
    active = active.astype(bf16)
    both_cot = jnp.concatenate([own_cot, other_cot])
    grad_active = jnp.dot(both_cot, full_proj_t, preferred_element_type=f32)
    grad_pre = pull_gelu(grad_active)[0].astype(bf16)
    grad_two = lax.dot_general(grad_pre, full_fc, NT, preferred_element_type=f32)
    grad_two = grad_two[:block] + other_core(grad_two[block:].astype(bf16)).astype(f32)
    cot = own_cot.astype(f32)
    grad_middle = cot + normalize_back(grad_two, hat_two, scale_two, gain_two)
    grad_middle_low = grad_middle.astype(bf16)
    grad_merged = lax.dot_general(
        out_t, grad_middle_low, (((0,), (1,)), ((), ())), preferred_element_type=f32
    ).astype(bf16)
    sent = grad_merged.reshape(head_count, HEAD, parts, rows).transpose(0, 2, 1, 3)
    sent = sent.reshape(ctx_count, share * HEAD, rows)
    grad_attended = lax.all_to_all(sent, "ctx", 0, 0, tiled=True).reshape(attended_low.shape)

    active_last = active
    normed_two, grad_pre_low, active, grad_middle_low, _ = lax.optimization_barrier(
        (normed_two, grad_pre, active, grad_middle_low, sent)
    )
    grad_fc = lax.dot_general(normed_two, grad_pre_low, (((0,), (0,)), ((), ())), preferred_element_type=f32)
    grad_proj_t = lax.dot_general(both_cot, active, (((0,), (0,)), ((), ())), preferred_element_type=f32)
    grad_out_t = lax.dot_general(
        grad_middle_low, merged, (((0,), (1,)), ((), ())), preferred_element_type=f32
    ).astype(bf16)
    half_width = width // 2
    mine, theirs = grad_out_t[:, :half_width], grad_out_t[:, half_width:]
    mine, theirs = jnp.where(core == 0, mine, theirs), jnp.where(core == 0, theirs, mine)
    grad_out_t = (mine.astype(f32) + other_core(theirs).astype(f32)).astype(bf16)
    grad_packed = jnp.concatenate([grad_fc.astype(bf16), grad_proj_t.astype(bf16), grad_out_t], axis=1)
    grad_packed = grad_packed.reshape(dp_count, ctx_count, shard_rows, grad_packed.shape[1])
    grad_packed_terms = dp_terms(grad_packed)
    early_lines = jnp.concatenate(
        [
            jnp.sum(grad_two * hat_two, axis=0, keepdims=True),
            jnp.sum(grad_two, axis=0, keepdims=True),
            jnp.sum(grad_middle, axis=0, keepdims=True),
            jnp.sum(cot, axis=0, keepdims=True),
        ]
    )
    bias_lines = jnp.sum(grad_pre.astype(f32), axis=0).reshape(hidden // width, width)
    bias_lines = jnp.pad(bias_lines, ((0, 8 - bias_lines.shape[0]), (0, 0)))

    message, grads, grad_scores = attend_back(
        table, own_prefix, projected, grad_attended, attended, log_totals, pivots, block
    )

    log_totals_after = grad_scores[:1]
    arrived = lax.all_to_all(message, "ctx", 0, 0, tiled=True)
    over_rows = (((0,), (0,)), ((), ()))
    grad_heads = lax.dot_general(normed, grads, over_rows, preferred_element_type=f32)
    grad_heads = grad_heads + other_core(grad_heads.astype(bf16)).astype(f32)
    grad_core_sum = grad_heads.astype(bf16)
    *grad_packed_terms, _ = lax.optimization_barrier((*grad_packed_terms, log_totals_after))
    half_heads = after(half_heads, log_totals_after)
    arranged = arrange_heads(pairs, core_number, half_heads, other_core(half_heads))
    grad_packed = sum(term.astype(f32) for term in grad_packed_terms).astype(bf16)
    grad_packed, hops = ring_scatter(grad_packed, order, ring, ((grad_core_sum,), (arrived, arranged[1])))
    late_arrived = after(arrived, hops[min(1, len(hops) - 1)])
    active_last = after(active_last, grad_core_sum)
    mlp = lax.dot_general(active_last, full_proj_t, NT, preferred_element_type=f32)
    result = middle + mlp[:block] + other_core(mlp[block:].astype(bf16)).astype(f32) + proj_shift
    result = result.astype(bf16)
    tokens_grad = finish_tokens(late_arrived, *arranged, own_tokens, grad_middle, gain_one)

    late_grads = after(grads, grad_core_sum)
    grad_normed = lax.dot_general(late_grads, head_weights[:, : 3 * LANES], NT, preferred_element_type=f32)
    grad_normed = grad_normed + lax.dot_general(
        grad_scores[:2], score_columns, (((0,), (1,)), ((), ())), preferred_element_type=f32
    )
    hat_one = (normed.astype(f32) - shift_one) / gain_one

    grad_heads = dp_terms(
        grad_core_sum.reshape(dp_count, ctx_count, shard_rows, 3 * LANES)
    )
    grad_columns = jnp.dot(grad_scores, normed, preferred_element_type=f32)
    lines = jnp.concatenate(
        [
            grad_columns[:2],
            jnp.sum(grad_normed * hat_one, axis=0, keepdims=True),
            jnp.sum(grad_normed, axis=0, keepdims=True),
            early_lines,
        ]
    )
    lines = lines + other_core(lines.astype(bf16)).astype(f32)
    lines = jnp.concatenate([lines, bias_lines])
    lines = jnp.broadcast_to(lines.astype(bf16)[None], (dp_count,) + lines.shape)
    lines = sum(term.astype(f32) for term in dp_terms(lines)).astype(bf16)
    lines = lines.reshape(2 * lines.shape[0], 3 * LANES)
    message = sum(term.astype(f32) for term in grad_heads).astype(bf16)
    message = jnp.concatenate(
        [message, jnp.broadcast_to(lines[None], (ctx_count,) + lines.shape)], axis=1
    )
    message, _ = lax.optimization_barrier((message, arrived))
    arrived = lax.all_to_all(message, "ctx", 0, 0, tiled=True)
    arrived = after(arrived, hops[max(len(hops) - 2, 0)])
    owners = [[] for _ in range(local_heads)]
    for device in range(near):
        for slot in sorted({entry[0] for entry in tables[device].tolist()}):
            owners[local_low[device] + slot].append((device, slot))
    grad_query, grad_key, grad_value, grad_score, vector_grads, fc_bias_grad = unpack_heads(
        near, owners, core_number, dp_number, ctx_number, arrived, shard_rows
    )
    fc_bias_grad = fc_bias_grad.reshape(hidden)

    def both_micro(own):
        other = other_core(own)
        return jnp.where(core == 0, jnp.stack([own, other]), jnp.stack([other, own]))[:, None]

    return (
        both_micro(result),
        both_micro(tokens_grad),
        grad_query,
        grad_key,
        grad_value,
        grad_score,
        grad_packed[:, 2 * hidden :].T,
        grad_packed[:, :hidden],
        grad_packed[:, hidden : 2 * hidden].T,
        vector_grads[0],
        vector_grads[1],
        vector_grads[2],
        vector_grads[3],
        vector_grads[4],
        fc_bias_grad,
        vector_grads[5],
    )


def solution(mesh):
    rows, columns, vector = P(("dp", "ctx"), "tensor"), P("tensor", ("dp", "ctx")), P(("dp", "ctx"))
    tokens = P(None, "dp", "ctx", None)
    in_specs = (
        (tokens, P(None, "dp"))
        + (rows,) * 4
        + (columns, rows, columns)
        + (vector,) * 5
        + (P("tensor"), vector, tokens)
    )
    out_specs = (
        (tokens, tokens)
        + (rows,) * 4
        + (columns, rows, columns)
        + (vector,) * 5
        + (P("tensor"), vector)
    )
    return jax.shard_map(
        partial(on_device, dp_count=mesh.shape["dp"], ctx_count=mesh.shape["ctx"]),
        mesh=mesh,
        in_specs=in_specs,
        out_specs=out_specs,
        check_vma=False,
    )
```

```python
from functools import partial

import jax
import jax.numpy as jnp
import numpy as np
from jax import lax
from jax.experimental import pallas as pl
from jax.experimental.pallas import tpu as pltpu
from jax.sharding import PartitionSpec as P

WIN = 64
TOPK = 64
HEAD = 64
LANES = 128

norm_epsilon = 1e-05
search_steps = 24
search_bound = 64.0

CHUNK = 256
LOG2E = 1.4426950408889634
FAR = 1e9
OPEN_PIVOT = -1e6
NEWTON_TOLERANCE = 3e-3
SCORE_ROWS = 16
NT = (((1,), (1,)), ((), ()))


def over_chunks(first, last, prefix, body, carry):
    below = lax.div(jnp.maximum(first - (WIN - 1), 0), CHUNK)
    total = lax.div(jnp.maximum(last + 1, prefix) + CHUNK - 1, CHUNK)
    above = jnp.minimum(lax.div(last + WIN + CHUNK - 1, CHUNK), total)
    whole = jnp.maximum(lax.div(prefix, CHUNK), above)
    def two(pair, carry):
        return body(False)(2 * pair + 1, body(False)(2 * pair, carry))

    pairs = lax.div(below, 2)
    carry = lax.fori_loop(0, pairs, two, carry)
    carry = lax.fori_loop(2 * pairs, below, body(False), carry)
    carry = lax.fori_loop(below, above, body(True), carry)
    carry = lax.fori_loop(above, whole, body(False), carry)
    return lax.fori_loop(whole, total, body(True), carry)


def fold(values, how):
    while values.shape[0] > 8:
        half = values.shape[0] // 2
        values = how(values[:half], values[half:])
    return values


def own_head(values, slot):
    lane = lax.broadcasted_iota(jnp.int32, values.shape, 1)
    kept = jnp.where(lax.div(lane, HEAD) == slot, values.astype(jnp.float32), 0.0)
    return kept


def rows_of(first, shape, rows, block):
    lane = lax.broadcasted_iota(jnp.int32, shape, 1)
    return first + lax.div(lane, rows) * block + lax.rem(lane, rows)


def masks(start, first, prefix, rows, block, together):
    shape = (CHUNK, rows * together)
    key = lax.broadcasted_iota(jnp.int32, shape, 0)
    behind = rows_of(first - start, shape, rows, block) - key
    allowed = (behind >= 0) | (key < prefix - start)
    return allowed, allowed & (jnp.abs(behind) < WIN)


def spread_lanes(values, lanes):
    values = values.astype(jnp.float32)
    return jnp.concatenate([values] * (lanes // LANES), axis=1)


def turn(source_ref, lanes, target_ref):
    def run(chunk, _):
        here = pl.ds(pl.multiple_of(chunk * CHUNK, CHUNK), CHUNK)
        flipped = source_ref[here, lanes : lanes + LANES].astype(jnp.float32).T
        target_ref[:, here] = flipped.astype(jnp.bfloat16)
        return 0

    lax.fori_loop(0, source_ref.shape[0] // CHUNK, run, 0)


def forward_kernel(
    block, table, prefix_ref, p_ref, o_ref, low_ref, lse_ref, pivot_ref, sm_ref, st_ref, vt_ref
):
    unit_count, _, lanes = o_ref.shape
    rows = low_ref.shape[2]
    together = lanes // rows
    prefix = prefix_ref[0]
    turn(p_ref, 2 * LANES, vt_ref)

    def unit(step, guess):
        slot, first = table[step, 0], table[step, 1]
        last = first + (together - 1) * block + rows - 1
        query = jnp.concatenate(
            [
                p_ref[pl.ds(pl.multiple_of(first + at * block, rows), rows), 0:LANES]
                for at in range(together)
            ],
            axis=0,
        )
        query_t = own_head(query, slot).T.astype(jnp.bfloat16)
        score_lane = pl.multiple_of((3 + slot) * LANES, LANES)

        def build(masked):
            def run(chunk, top):
                start = pl.multiple_of(chunk * CHUNK, CHUNK)
                here = pl.ds(start, CHUNK)
                logits = jnp.dot(
                    p_ref[here, LANES : 2 * LANES], query_t, preferred_element_type=jnp.float32
                )
                score = spread_lanes(p_ref[here, pl.ds(score_lane, LANES)], lanes)
                if masked:
                    allowed, local = masks(start, first, prefix, rows, block, together)
                    logits = jnp.where(allowed, logits, -1e30)
                    score = jnp.where(local, FAR, jnp.where(allowed, score, -FAR))
                    top = jnp.maximum(top, fold(jnp.where(local, logits, -1e30), jnp.maximum))
                st_ref[here, :] = logits
                sm_ref[here, :] = score
                return top

            return run

        top = over_chunks(first, last, prefix, build, jnp.full((8, lanes), -1e30, jnp.float32))
        top = jnp.max(top, axis=0, keepdims=True)

        row = rows_of(first, (1, lanes), rows, block)
        local_count = (
            jnp.minimum(row, WIN - 1) + 1 + jnp.clip(prefix - 1 - row, 0, WIN - 1)
        ).astype(jnp.float32)
        candidates = jnp.maximum(row + 1, prefix).astype(jnp.float32) - local_count
        chunks = lax.div(jnp.maximum(last + 1, prefix) + CHUNK - 1, CHUNK)
        entries = (chunks * CHUNK).astype(jnp.float32)
        searched = candidates > TOPK
        count = jnp.maximum(candidates, TOPK + 1.0)
        goal = jnp.log(TOPK / (count - TOPK))

        def measure(half):
            def run(chunk, sums):
                bent = jnp.tanh(sm_ref[pl.ds(pl.multiple_of(chunk * CHUNK, CHUNK), CHUNK), :] - half)
                return sums[0] + fold(bent, jnp.add), sums[1] + fold(bent * bent, jnp.add)

            zero = jnp.zeros((8, lanes), jnp.float32)
            first_sum, second_sum = lax.fori_loop(0, chunks, run, (zero, zero))
            filled = 0.5 * (entries + jnp.sum(first_sum, axis=0, keepdims=True)) - local_count
            slope = 0.25 * (entries - jnp.sum(second_sum, axis=0, keepdims=True))
            return filled, slope

        def improve(state):
            turn, _, half, lower, upper, done = state
            filled, slope = measure(half)
            above = filled > TOPK
            lower = jnp.where(above, half, lower)
            upper = jnp.where(above, upper, half)
            newton = (filled - TOPK) / slope
            held = jnp.clip(filled, 1e-3, count - 1e-3)
            bent = (jnp.log(held / (count - held)) - goal) * (held * (count - held) / (count * slope))
            close = jnp.abs(newton) <= NEWTON_TOLERANCE
            following = half + 0.5 * jnp.where(close, newton, bent)
            inside = (following > lower) & (following < upper)
            halve = (turn >= 12) & (lax.rem(turn, 2) == 1)
            middle = 0.5 * (lower + upper)
            following = jnp.where(close | (inside & jnp.logical_not(halve)), following, middle)
            half = jnp.where(done > 0.0, half, following)
            done = jnp.where(close, 1.0, done)
            return turn + 1, jnp.min(done), half, lower, upper, done

        start_done = jnp.where(searched, 0.0, 1.0)
        bound = jnp.full((1, lanes), 0.5 * search_bound, jnp.float32)
        _, _, half, lower, upper, done = lax.while_loop(
            lambda state: (state[0] < 12 + 2 * search_steps) & (state[1] < 0.5),
            improve,
            (0, jnp.min(start_done), guess, -bound, bound, start_done),
        )
        half = jnp.where(done > 0.0, half, 0.5 * (lower + upper))
        pivot = jnp.where(searched, half, OPEN_PIVOT)

        def weigh(chunk, sums):
            here = pl.ds(pl.multiple_of(chunk * CHUNK, CHUNK), CHUNK)
            raised = jnp.exp(st_ref[here, :] - top)
            weight = raised / (1.0 + jnp.exp(2.0 * (pivot - sm_ref[here, :])))
            merged = sums[1] + jnp.dot(
                vt_ref[:, here], weight.astype(jnp.bfloat16), preferred_element_type=jnp.float32
            )
            return sums[0] + fold(weight, jnp.add), merged

        total, merged = lax.fori_loop(
            0,
            chunks,
            weigh,
            (jnp.zeros((8, lanes), jnp.float32), jnp.zeros((LANES, lanes), jnp.float32)),
        )
        total = jnp.sum(total, axis=0, keepdims=True)
        merged = merged / total
        own = jnp.where(slot == 0, merged[:HEAD], merged[HEAD:])
        o_ref[step] = own
        for at in range(together):
            low_ref[table[step, 2 + at]] = own[:, at * rows : (at + 1) * rows].astype(jnp.bfloat16)
        lse_ref[step] = top + jnp.log(total)
        pivot_ref[step] = pivot
        return jnp.where(searched, half, guess)

    lax.fori_loop(0, unit_count, unit, jnp.zeros((1, lanes), jnp.float32))


def backward_kernel(
    block,
    table,
    prefix_ref,
    p_ref,
    do_ref,
    o_ref,
    lse_ref,
    pivot_ref,
    message_ref,
    d_ref,
    score_ref,
    dq_ref,
    dk_ref,
    dv_ref,
    ds_ref,
    kt_ref,
):
    unit_count, _, lanes = o_ref.shape
    rows = do_ref.shape[2]
    together = lanes // rows
    length = p_ref.shape[0]
    prefix = prefix_ref[0]
    turn(p_ref, LANES, kt_ref)

    def clear(chunk, _):
        here = pl.ds(pl.multiple_of(chunk * CHUNK, CHUNK), CHUNK)
        for ref in (dq_ref, dk_ref, dv_ref):
            ref[here, :] = jnp.zeros((CHUNK, LANES), jnp.float32)
        for slot in range(2):
            ds_ref[slot, here, :] = jnp.zeros((CHUNK, LANES), jnp.float32)
        return 0

    lax.fori_loop(0, length // CHUNK, clear, 0)

    def unit(step, _):
        slot, first = table[step, 0], table[step, 1]
        last = first + (together - 1) * block + rows - 1
        whose = [pl.ds(pl.multiple_of(first + at * block, rows), rows) for at in range(together)]
        query = own_head(jnp.concatenate([p_ref[here, 0:LANES] for here in whose], axis=0), slot)
        query_t = query.T.astype(jnp.bfloat16)
        query = query.astype(jnp.bfloat16)
        grad = jnp.concatenate([do_ref[table[step, 2 + at]] for at in range(together)], axis=1)
        grad = grad.astype(jnp.float32)
        row_dot = jnp.sum(grad * o_ref[step], axis=0, keepdims=True)
        empty = jnp.zeros_like(grad)
        grad = jnp.where(
            slot == 0,
            jnp.concatenate([grad, empty], axis=0),
            jnp.concatenate([empty, grad], axis=0),
        )
        grad_t = grad.T.astype(jnp.bfloat16)
        grad = grad.astype(jnp.bfloat16)
        lse, pivot = lse_ref[step], pivot_ref[step]
        score_lane = pl.multiple_of((3 + slot) * LANES, LANES)

        def body(masked):
            def run(chunk, grad_query):
                start = pl.multiple_of(chunk * CHUNK, CHUNK)
                here = pl.ds(start, CHUNK)
                logits = jnp.dot(
                    p_ref[here, LANES : 2 * LANES], query_t, preferred_element_type=jnp.float32
                )
                grad_probs = jnp.dot(
                    p_ref[here, 2 * LANES : 3 * LANES], grad, preferred_element_type=jnp.float32
                )
                score = spread_lanes(p_ref[here, pl.ds(score_lane, LANES)], lanes)
                if masked:
                    allowed, local = masks(start, first, prefix, rows, block, together)
                    logits = jnp.where(allowed, logits, -1e30)
                    score = jnp.where(local, FAR, jnp.where(allowed, score, -FAR))
                unit_probs = jnp.exp(logits - lse)
                gate = 1.0 / (1.0 + jnp.exp2((2.0 * LOG2E) * (pivot - score)))
                probs = gate * unit_probs
                grad_logits = probs * (grad_probs - row_dot)
                grad_score = grad_logits * (1.0 - gate)
                folded = grad_score[:, :LANES]
                for lane in range(LANES, lanes, LANES):
                    folded = folded + grad_score[:, lane : lane + LANES]
                ds_ref[slot, here, :] += folded
                low = grad_logits.astype(jnp.bfloat16)
                dk_ref[here, :] += jnp.dot(low, query, preferred_element_type=jnp.float32)
                dv_ref[here, :] += jnp.dot(
                    probs.astype(jnp.bfloat16), grad_t, preferred_element_type=jnp.float32
                )
                return grad_query + jnp.dot(
                    kt_ref[:, here], low, preferred_element_type=jnp.float32
                )

            return run

        grad_query = over_chunks(
            first, last, prefix, body, jnp.zeros((LANES, lanes), jnp.float32)
        ).T
        lane = lax.broadcasted_iota(jnp.int32, grad_query.shape, 1)
        grad_query = jnp.where(lax.div(lane, HEAD) == slot, grad_query, 0.0)
        for at, here in enumerate(whose):
            dq_ref[here, :] += grad_query[at * rows : (at + 1) * rows]
        return 0

    lax.fori_loop(0, unit_count, unit, 0)

    def finish(chunk, _):
        here = pl.ds(pl.multiple_of(chunk * CHUNK, CHUNK), CHUNK)
        lane = lax.broadcasted_iota(jnp.int32, (CHUNK, LANES), 1)
        columns = [jnp.sum(ds_ref[slot, here, :], axis=1, keepdims=True) for slot in range(2)]
        grad_score = jnp.where(lane == 0, columns[0], jnp.where(lane == 1, columns[1], 0.0))
        grad_score = grad_score.T[:SCORE_ROWS].astype(jnp.bfloat16)
        score_ref[:, here] = grad_score
        message_ref[chunk, CHUNK:, 0:CHUNK] = grad_score
        message_ref[chunk, CHUNK:, CHUNK:] = jnp.zeros_like(message_ref[chunk, CHUNK:, CHUNK:])
        grads = (dq_ref[here, :] * HEAD**-0.5, dk_ref[here, :], dv_ref[here, :])
        for kind, grad in enumerate(grads):
            low = grad.astype(jnp.bfloat16)
            d_ref[here, kind * LANES : (kind + 1) * LANES] = low
            message_ref[chunk, 0:CHUNK, kind * LANES : (kind + 1) * LANES] = low
        return 0

    lax.fori_loop(0, length // CHUNK, finish, 0)


VMEM_LIMIT = 48 * 1024 * 1024


def kernel_params():
    return pltpu.CompilerParams(vmem_limit_bytes=VMEM_LIMIT)


def in_vmem():
    return pl.BlockSpec(memory_space=pltpu.VMEM)


def in_smem():
    return pl.BlockSpec(memory_space=pltpu.SMEM)


def attend(table, prefix, projected, rows, block):
    unit_count = table.shape[0]
    together = table.shape[1] - 2
    lanes = rows * together
    length = projected.shape[0]
    pairs = unit_count * lanes * length
    return pl.pallas_call(
        partial(forward_kernel, block),
        out_shape=(
            jax.ShapeDtypeStruct((unit_count, HEAD, lanes), jnp.float32),
            jax.ShapeDtypeStruct((unit_count * together, HEAD, rows), jnp.bfloat16),
            jax.ShapeDtypeStruct((unit_count, 1, lanes), jnp.float32),
            jax.ShapeDtypeStruct((unit_count, 1, lanes), jnp.float32),
        ),
        in_specs=[in_smem(), in_smem(), in_vmem()],
        out_specs=(in_vmem(),) * 4,
        scratch_shapes=[
            pltpu.VMEM((length, lanes), jnp.float32),
            pltpu.VMEM((length, lanes), jnp.float32),
            pltpu.VMEM((LANES, length), jnp.bfloat16),
        ],
        compiler_params=kernel_params(),
        cost_estimate=pl.CostEstimate(
            flops=pairs * 12000, bytes_accessed=projected.size * 4, transcendentals=pairs * 8
        ),
        name="attend",
    )(table, prefix, projected)


def attend_back(table, prefix, projected, grads, attended, log_totals, pivots, block):
    unit_count, _, lanes = attended.shape
    length = projected.shape[0]
    pairs = unit_count * lanes * length
    return pl.pallas_call(
        partial(backward_kernel, block),
        out_shape=(
            jax.ShapeDtypeStruct((length // CHUNK, CHUNK + SCORE_ROWS, 3 * LANES), jnp.bfloat16),
            jax.ShapeDtypeStruct((length, 3 * LANES), jnp.bfloat16),
            jax.ShapeDtypeStruct((SCORE_ROWS, length), jnp.bfloat16),
        ),
        in_specs=[in_smem(), in_smem()] + [in_vmem()] * 5,
        out_specs=(in_vmem(),) * 3,
        scratch_shapes=[
            pltpu.VMEM((length, LANES), jnp.float32),
            pltpu.VMEM((length, LANES), jnp.float32),
            pltpu.VMEM((length, LANES), jnp.float32),
            pltpu.VMEM((2, length, LANES), jnp.float32),
            pltpu.VMEM((LANES, length), jnp.bfloat16),
        ],
        compiler_params=kernel_params(),
        cost_estimate=pl.CostEstimate(
            flops=pairs * 9000, bytes_accessed=projected.size * 4, transcendentals=pairs * 3
        ),
        name="attend_back",
    )(table, prefix, projected, grads, attended, log_totals, pivots)


def project_kernel(count, offset, *refs):
    tokens, (gain_ref, shift_ref, weight_ref, _, __, normed_ref, projected_ref) = refs[:count], refs[count:]
    for step, tokens_ref in enumerate(tokens):

        @pl.when(pl.program_id(0) == step)
        def _(tokens_ref=tokens_ref):
            hat, _ = normalize(tokens_ref[...].astype(jnp.float32))
            normed = (hat * gain_ref[...] + shift_ref[...]).astype(jnp.bfloat16)
            normed_ref[...] = normed
            low = jnp.dot(normed, weight_ref[...], preferred_element_type=jnp.float32)
            low = low.astype(jnp.bfloat16).astype(jnp.float32)
            lane = lax.broadcasted_iota(jnp.int32, low.shape, 1)
            projected_ref[...] = jnp.where(lane < 3 * LANES, low, 0.5 * low).astype(jnp.bfloat16)


def project(places, tokens, gain, shift, weight, normed, projected):
    count = len(tokens)
    rows, width = tokens[0].shape
    columns = weight.shape[1]

    def whole(shape):
        return pl.BlockSpec(shape, lambda i, at: (0, 0))

    anywhere = pl.BlockSpec(memory_space=pl.ANY)
    return pl.pallas_call(
        partial(project_kernel, count),
        grid_spec=pltpu.PrefetchScalarGridSpec(
            num_scalar_prefetch=1,
            grid=(count,),
            in_specs=[whole((rows, width))] * count
            + [whole((1, width)), whole((1, width)), whole((width, columns)), anywhere, anywhere],
            out_specs=(
                pl.BlockSpec((rows, width), lambda i, at: (at[i], 0)),
                pl.BlockSpec((rows, columns), lambda i, at: (at[i], 0)),
            ),
        ),
        out_shape=(
            jax.ShapeDtypeStruct(normed.shape, normed.dtype),
            jax.ShapeDtypeStruct(projected.shape, projected.dtype),
        ),
        input_output_aliases={count + 4: 0, count + 5: 1},
        compiler_params=kernel_params(),
        cost_estimate=pl.CostEstimate(
            flops=2 * count * rows * width * columns * 20,
            bytes_accessed=rows * width * 12,
            transcendentals=0,
        ),
        name="project",
    )(places, *tokens, gain, shift, weight, normed, projected)


VECTOR_LANE = 8


def pack_kernel(vector_ref, query_ref, key_ref, value_ref, score_ref, out_ref):
    rows, width = query_ref.shape
    for kind, ref in enumerate((query_ref, key_ref, value_ref)):
        out_ref[:, kind * width : (kind + 1) * width] = ref[...]
    tail = vector_ref[...].astype(jnp.float32).T[:rows]
    lane = lax.broadcasted_iota(jnp.int32, tail.shape, 1)
    for head in range(score_ref.shape[1]):
        tail = jnp.where(lane == head, score_ref[:, head : head + 1].astype(jnp.float32), tail)
    out_ref[:, 3 * width :] = tail.astype(jnp.bfloat16)


def pack_heads(vectors, query, key, value, score):
    below = LANES - VECTOR_LANE - vectors.shape[0]
    return pl.pallas_call(
        pack_kernel,
        out_shape=jax.ShapeDtypeStruct((query.shape[0], 3 * query.shape[1] + LANES), jnp.bfloat16),
        in_specs=[in_vmem()] * 5,
        out_specs=in_vmem(),
        compiler_params=kernel_params(),
        name="pack_heads",
    )(jnp.pad(vectors, ((VECTOR_LANE, below), (0, LANES - vectors.shape[1]))), query, key, value, score)


def select_kernel(pairs, ctx_ref, columns_ref, out_ref):
    half = (columns_ref.shape[1] - LANES) // 3
    for pattern, heads in enumerate(pairs):

        @pl.when(lax.rem(ctx_ref[0], len(pairs)) == pattern)
        def _(heads=heads):
            for kind in range(3):
                starts = [kind * half + head * HEAD for head in heads]
                out_ref[:, kind * LANES : (kind + 1) * LANES] = jnp.concatenate(
                    [columns_ref[:, at : at + HEAD] for at in starts], axis=1
                )
            tail = columns_ref[:, 3 * half :].astype(jnp.float32)
            lane = lax.broadcasted_iota(jnp.int32, tail.shape, 1)
            for slot, head in enumerate(heads):
                tail = jnp.where(lane == LANES - 2 + slot, tail[:, head : head + 1], tail)
            out_ref[:, 3 * LANES :] = tail.astype(jnp.bfloat16)


def select_heads(pairs, ctx, columns):
    return pl.pallas_call(
        partial(select_kernel, pairs),
        out_shape=jax.ShapeDtypeStruct((columns.shape[0], 4 * LANES), jnp.bfloat16),
        in_specs=[in_smem(), in_vmem()],
        out_specs=in_vmem(),
        compiler_params=kernel_params(),
        name="select_heads",
    )(ctx, columns)


def unpack_kernel(
    near, owners, core_ref, dp_ref, ctx_ref, arrived_ref, query_ref, key_ref, value_ref, score_ref, vector_ref, bias_ref
):
    rows = query_ref.shape[0]
    sources = [arrived_ref[core_ref[0] * near + device].astype(jnp.float32) for device in range(near)]
    for head, terms in enumerate(owners):
        for kind, ref in enumerate((query_ref, key_ref, value_ref)):
            at = [kind * LANES + slot * HEAD for _, slot in terms]
            parts = [sources[d][:rows, a : a + HEAD] for (d, _), a in zip(terms, at)]
            ref[:, head * HEAD : (head + 1) * HEAD] = sum(parts[1:], parts[0])

    def line(values, index):
        at = rows + 2 * index
        return jnp.concatenate([values[at : at + 1], values[at + 1 : at + 2]], axis=1)

    total = arrived_ref[0].astype(jnp.float32)
    for device in range(1, arrived_ref.shape[0]):
        total = total + arrived_ref[device].astype(jnp.float32)
    lines = [line(total, 2 + index) for index in range(6)]
    for terms in owners:
        parts = [line(sources[device], slot) for device, slot in terms]
        lines.append(sum(parts[1:], parts[0]))
    width = lines[0].shape[1]
    sublane = lax.broadcasted_iota(jnp.int32, (SCORE_ROWS, width), 0)
    table = jnp.zeros((SCORE_ROWS, width), jnp.float32)
    for index, values in enumerate(lines):
        table = jnp.where(sublane == index, values, table)
    first = dp_ref[0] * rows * arrived_ref.shape[0] + ctx_ref[0] * rows
    table = pltpu.roll(table, width - first, 1)[:, :LANES]
    vector_ref[...] = table[:8, :rows]
    turned = jnp.concatenate([table, jnp.zeros((LANES - SCORE_ROWS, LANES), jnp.float32)], axis=0).T
    score_ref[...] = turned[:rows, 6 : 6 + len(owners)]
    for index in range(2):
        bias_ref[index : index + 1] = line(total, 8 + index)


def unpack_heads(near, owners, core, dp, ctx, arrived, rows):
    lanes = arrived.shape[2]
    shapes = [(rows, lanes)] * 3 + [(rows, len(owners)), (8, rows), (2, 2 * lanes)]
    return pl.pallas_call(
        partial(unpack_kernel, near, owners),
        out_shape=[jax.ShapeDtypeStruct(shape, jnp.float32) for shape in shapes],
        in_specs=[in_smem(), in_smem(), in_smem(), in_vmem()],
        out_specs=[in_vmem()] * 6,
        compiler_params=kernel_params(),
        name="unpack_heads",
    )(core, dp, ctx, arrived)


def arrange_kernel(pairs, core_ref, own_ref, other_ref, out_ref, score_ref):
    width = own_ref.shape[0]
    near = len(pairs)
    half = width // 2
    lane = lax.broadcasted_iota(jnp.int32, (width, SCORE_ROWS), 1)
    for columns_ref, side in ((own_ref, core_ref[0]), (other_ref, 1 - core_ref[0])):
        for device, heads in enumerate(pairs):
            at = side * near + device
            out_ref[at] = jnp.concatenate(
                [
                    columns_ref[:, kind * half + head * HEAD : kind * half + (head + 1) * HEAD]
                    for kind in range(3)
                    for head in heads
                ],
                axis=1,
            )
            columns = [
                columns_ref[:, 3 * half + head : 3 * half + head + 1].astype(jnp.float32)
                for head in heads
            ]
            score = jnp.where(lane == 0, columns[0], jnp.where(lane == 1, columns[1], 0.0))
            score_ref[at] = score.astype(jnp.bfloat16)


def arrange_heads(pairs, core, own_columns, other_columns):
    width = own_columns.shape[0]
    count = 2 * len(pairs)
    return pl.pallas_call(
        partial(arrange_kernel, pairs),
        out_shape=(
            jax.ShapeDtypeStruct((count, width, 3 * LANES), jnp.bfloat16),
            jax.ShapeDtypeStruct((count, width, SCORE_ROWS), jnp.bfloat16),
        ),
        in_specs=[in_smem()] + [in_vmem()] * 2,
        out_specs=(in_vmem(),) * 2,
        compiler_params=kernel_params(),
        name="arrange_heads",
    )(core, own_columns, other_columns)


def finish_kernel(arrived_ref, weight_ref, score_ref, tokens_ref, middle_ref, gain_ref, out_ref):
    rows, width = tokens_ref.shape
    total = jnp.zeros((rows, width), jnp.float32)
    for device in range(arrived_ref.shape[0]):
        total += lax.dot_general(
            arrived_ref[device, :rows], weight_ref[device], NT, preferred_element_type=jnp.float32
        )
        grads = arrived_ref[device, rows:, :rows].astype(jnp.float32).T.astype(jnp.bfloat16)
        total += lax.dot_general(grads, score_ref[device], NT, preferred_element_type=jnp.float32)
    hat, scale = normalize(tokens_ref[...].astype(jnp.float32))
    out_ref[...] = middle_ref[...] + normalize_back(total, hat, scale, gain_ref[...])


def finish_tokens(arrived, weights, scores, tokens, grad_middle, gain):
    return pl.pallas_call(
        finish_kernel,
        out_shape=jax.ShapeDtypeStruct(grad_middle.shape, jnp.float32),
        in_specs=[in_vmem()] * 6,
        out_specs=in_vmem(),
        compiler_params=kernel_params(),
        name="finish_tokens",
    )(arrived, weights, scores, tokens, grad_middle, gain)


def ring_order(count):
    deep = 4 if count % 4 == 0 else 1
    wide = count // deep
    if deep == 1 or wide == 1:
        return list(range(count))
    walk = []
    for place in range(deep):
        across = range(1, wide) if place % 2 == 0 else range(wide - 1, 0, -1)
        walk += [place * wide + at for at in across]
    return walk + [place * wide for place in reversed(range(deep))]


def look_up(rows, index, kind=jnp.uint32):
    table = jnp.asarray(np.asarray(rows), kind)
    return lax.dynamic_slice(table, (index, jnp.uint32(0)), (1, table.shape[1]))[0]


def pick(values, index):
    start = (index,) + (jnp.uint32(0),) * (values.ndim - 1)
    return lax.dynamic_slice(values, start, (1,) + values.shape[1:])[0]


def place_on(axis):
    return lax.axis_index(axis).astype(jnp.uint32)


def ring_distances(count):
    return sorted(range(-(count // 2), (count + 1) // 2), key=lambda d: (abs(d), d))


def ring_places(order):
    count = len(order)
    spots = np.argsort(order)
    return [[order[(spots[me] + d) % count] for d in ring_distances(count)] for me in range(count)]


def ring_hops(order):
    count = len(order)
    forward = [(order[i], order[(i + 1) % count]) for i in range(count)]
    return forward, [(receiver, sender) for sender, receiver in forward]


def ring_gather(values, order):
    count = len(order)
    forward, backward = ring_hops(order)
    held = {0: values}
    for step in range(1, count // 2 + 1):
        held[-step] = lax.ppermute(held[1 - step], "ctx", forward)
        if step < count - step:
            held[step] = lax.ppermute(held[step - 1], "ctx", backward)
    return held


def after(values, *others):
    return lax.optimization_barrier((values, *others))[0]


def ring_scatter(values, order, places, starts):
    count = len(order)
    forward, backward = ring_hops(order)
    at = {d: places[i] for i, d in enumerate(ring_distances(count))}

    def own(distance):
        here = at.get(distance, at.get(distance - count))
        return pick(values, here).astype(jnp.float32)

    ahead = behind = 0.0
    arrivals = []
    for step in range(count // 2, 0, -1):
        outgoing = (own(step) + ahead).astype(jnp.bfloat16)
        hop = len(arrivals)
        if hop < len(starts):
            outgoing = after(outgoing, *starts[hop])
        ahead = lax.ppermute(outgoing, "ctx", forward)
        arrivals.append(ahead)
        ahead = ahead.astype(jnp.float32)
        if step < count - step:
            outgoing = (own(-step) + behind).astype(jnp.bfloat16)
            if hop < len(starts):
                outgoing = after(outgoing, *starts[hop])
            behind = lax.ppermute(outgoing, "ctx", backward)
            behind = behind.astype(jnp.float32)
    return own(0) + ahead + behind, arrivals


def dp_terms(values):
    count = values.shape[0]
    places = look_up([[(i + shift) % count for shift in range(count)] for i in range(count)], place_on("dp"))
    terms = [pick(values, places[0])]
    for shift in range(1, count):
        sent = pick(values, places[shift])
        terms.append(lax.ppermute(sent, "dp", [(i, (i + shift) % count) for i in range(count)]))
    return terms


def other_core(values):
    return lax.ppermute(values, "tensor", [(0, 1), (1, 0)])


def normalize(values):
    centred = values - jnp.mean(values, axis=-1, keepdims=True)
    scale = lax.rsqrt(jnp.mean(centred * centred, axis=-1, keepdims=True) + norm_epsilon)
    return centred * scale, scale


def normalize_back(grad, hat, scale, gain):
    scaled = grad * gain
    return scale * (
        scaled
        - jnp.mean(scaled, axis=-1, keepdims=True)
        - hat * jnp.mean(scaled * hat, axis=-1, keepdims=True)
    )


def head_plan(ctx_count, head_count, block):
    parts = 1
    while head_count * parts % ctx_count:
        parts += 1
    share = head_count * parts // ctx_count
    rows = block // parts
    lows, tables = [], []
    for device in range(ctx_count):
        pieces = range(share * device, share * (device + 1))
        lows.append(pieces[0] // parts)
        tables.append(
            [
                (piece // parts - lows[-1], at * block + (piece % parts) * rows)
                + tuple((at + more) * share + order for more in range(parts))
                for order, piece in enumerate(pieces)
                for at in range(0, ctx_count, parts)
            ]
        )
        assert all(entry[0] in (0, 1) for entry in tables[-1])
    assert ctx_count % parts == 0
    return parts, share, rows, lows, np.asarray(tables, np.int32)


def on_device(
    tokens,
    prefix,
    w_query,
    w_key,
    w_value,
    w_score,
    w_attn_out,
    w_fc,
    w_proj,
    ln1_gain,
    ln1_bias,
    ln2_gain,
    ln2_bias,
    attn_bias,
    fc_bias,
    proj_bias,
    cotangent,
    dp_count,
    ctx_count,
):
    f32, bf16 = jnp.float32, jnp.bfloat16
    micro_count, seq_count, block, width = tokens.shape
    local_heads = w_score.shape[1]
    head_count = 2 * local_heads
    assert micro_count == 2 and seq_count == 1
    core = place_on("tensor")
    me = place_on("ctx")
    both = ("dp", "ctx")
    shards = dp_count * ctx_count
    shard_rows = width // shards
    parts, share, rows, lows, tables = head_plan(ctx_count, head_count, block)
    near = ctx_count // 2
    local_low = [low % local_heads for low in lows[:near]]
    local_high = [min(low + 1, local_heads - 1) for low in local_low]

    own_tokens = pick(tokens, core)[0]
    own_cot = pick(cotangent, core)[0]
    other_cot = pick(cotangent, 1 - core)[0]
    own_prefix = pick(prefix, core)
    table = pick(jnp.asarray(tables), me)
    core_number = look_up([[0], [1]], core, jnp.int32)
    dp_number = look_up([[i] for i in range(dp_count)], place_on("dp"), jnp.int32)
    ctx_number = look_up([[i] for i in range(ctx_count)], me, jnp.int32)

    order = ring_order(ctx_count)
    blocks = ring_gather(own_tokens, order)
    places = look_up(ring_places(order), me, jnp.int32)
    ring = look_up(ring_places(order), me)

    def columns(weight, head):
        return weight[:, head * HEAD : (head + 1) * HEAD]

    vectors = jnp.stack([ln1_gain, ln1_bias, ln2_gain, ln2_bias, attn_bias, proj_bias])
    pairs = tuple(zip(local_low, local_high))
    own_columns = pack_heads(vectors, w_query, w_key, w_value, w_score)
    if dp_count == 2:
        other_columns = lax.ppermute(own_columns, "dp", [(0, 1), (1, 0)])
        first_dp = place_on("dp") == 0
        both_columns = jnp.stack(
            [jnp.where(first_dp, own_columns, other_columns), jnp.where(first_dp, other_columns, own_columns)]
        )
    else:
        both_columns = lax.all_gather(own_columns, "dp")
    half_heads = jnp.zeros((dp_count, ctx_count) + own_columns.shape, bf16)
    column_blocks = ring_gather(both_columns, order)
    zero = jnp.uint32(0)
    for spot, distance in enumerate(ring_distances(ctx_count)):
        half_heads = lax.dynamic_update_slice(
            half_heads, column_blocks[distance][:, None], (zero, ring[spot], zero, zero)
        )
    half_heads = half_heads.reshape(width, own_columns.shape[1])
    head_weights = select_heads(pairs, ctx_number, half_heads)
    from_half = (me >= near).astype(jnp.uint32)
    head_weights = jnp.where(from_half == core, head_weights, other_core(head_weights))
    gains = head_weights[:, 3 * LANES + VECTOR_LANE : 3 * LANES + VECTOR_LANE + 6].astype(f32).T
    gain_one, shift_one, gain_two, shift_two, attn_shift, proj_shift = [gains[i : i + 1] for i in range(6)]

    score_columns = head_weights[:, 4 * LANES - 2 :]
    wide_weights = jnp.concatenate(
        [head_weights[:, :LANES] * HEAD**-0.5, head_weights[:, LANES : 3 * LANES]]
        + [jnp.broadcast_to(score_columns[:, i : i + 1], (width, LANES)) for i in range(2)],
        axis=1,
    )
    length = ctx_count * block
    normed = jnp.zeros((length, width), bf16)
    projected = jnp.zeros((length, 5 * LANES), bf16)
    distances = ring_distances(ctx_count)
    early = max(ctx_count - 3, 1)
    for batch, batch_places in ((distances[:early], places[:early]), (distances[early:], places[early:])):
        normed, projected = project(
            batch_places,
            [blocks[d] for d in batch],
            gain_one,
            shift_one,
            wide_weights,
            normed,
            projected,
        )

    packed = jnp.concatenate([w_fc, w_proj.T, w_attn_out.T], axis=1)
    packed = after(packed, column_blocks[-2], column_blocks[2])
    packed = lax.all_gather(packed, both, axis=0, tiled=True)
    attended, attended_low, log_totals, pivots = attend(table, own_prefix, projected, rows, block)
    packed, _ = lax.optimization_barrier((packed, log_totals))
    hidden = w_fc.shape[1]
    full_fc, full_proj_t = packed[:, :hidden], packed[:, hidden : 2 * hidden]
    half_out_t = packed[:, 2 * hidden :]
    other_out_t = other_core(half_out_t)
    out_t = jnp.where(
        core == 0,
        jnp.concatenate([half_out_t, other_out_t], axis=1),
        jnp.concatenate([other_out_t, half_out_t], axis=1),
    )

    sent = attended_low.reshape(ctx_count, share * HEAD, rows)
    merged = lax.all_to_all(sent, "ctx", 0, 0, tiled=True)
    merged = merged.reshape(head_count, parts, HEAD, rows).transpose(0, 2, 1, 3).reshape(width, block)

    own_block = own_tokens.astype(f32)
    attn = lax.dot_general(merged, out_t, (((0,), (1,)), ((), ())), preferred_element_type=f32)
    middle = own_block + attn + attn_shift
    hat_two, scale_two = normalize(middle)
    normed_two = (hat_two * gain_two + shift_two).astype(bf16)
    normed_two = jnp.concatenate([normed_two, other_core(normed_two)])
    hidden_pre = jnp.dot(normed_two, full_fc, preferred_element_type=f32) + fc_bias.astype(f32)
    active, pull_gelu = jax.vjp(partial(jax.nn.gelu, approximate=True), hidden_pre)
    active = active.astype(bf16)
    both_cot = jnp.concatenate([own_cot, other_cot])
    grad_active = jnp.dot(both_cot, full_proj_t, preferred_element_type=f32)
    grad_pre = pull_gelu(grad_active)[0].astype(bf16)
    grad_two = lax.dot_general(grad_pre, full_fc, NT, preferred_element_type=f32)
    grad_two = grad_two[:block] + other_core(grad_two[block:].astype(bf16)).astype(f32)
    cot = own_cot.astype(f32)
    grad_middle = cot + normalize_back(grad_two, hat_two, scale_two, gain_two)
    grad_middle_low = grad_middle.astype(bf16)
    grad_merged = lax.dot_general(
        out_t, grad_middle_low, (((0,), (1,)), ((), ())), preferred_element_type=f32
    ).astype(bf16)
    sent = grad_merged.reshape(head_count, HEAD, parts, rows).transpose(0, 2, 1, 3)
    sent = sent.reshape(ctx_count, share * HEAD, rows)
    grad_attended = lax.all_to_all(sent, "ctx", 0, 0, tiled=True).reshape(attended_low.shape)

    active_last = active
    normed_two, grad_pre_low, active, grad_middle_low, _ = lax.optimization_barrier(
        (normed_two, grad_pre, active, grad_middle_low, sent)
    )
    grad_fc = lax.dot_general(normed_two, grad_pre_low, (((0,), (0,)), ((), ())), preferred_element_type=f32)
    grad_proj_t = lax.dot_general(both_cot, active, (((0,), (0,)), ((), ())), preferred_element_type=f32)
    grad_out_t = lax.dot_general(
        grad_middle_low, merged, (((0,), (1,)), ((), ())), preferred_element_type=f32
    ).astype(bf16)
    half_width = width // 2
    mine, theirs = grad_out_t[:, :half_width], grad_out_t[:, half_width:]
    mine, theirs = jnp.where(core == 0, mine, theirs), jnp.where(core == 0, theirs, mine)
    grad_out_t = (mine.astype(f32) + other_core(theirs).astype(f32)).astype(bf16)
    grad_packed = jnp.concatenate([grad_fc.astype(bf16), grad_proj_t.astype(bf16), grad_out_t], axis=1)
    grad_packed = grad_packed.reshape(dp_count, ctx_count, shard_rows, grad_packed.shape[1])
    grad_packed_terms = dp_terms(grad_packed)
    early_lines = jnp.concatenate(
        [
            jnp.sum(grad_two * hat_two, axis=0, keepdims=True),
            jnp.sum(grad_two, axis=0, keepdims=True),
            jnp.sum(grad_middle, axis=0, keepdims=True),
            jnp.sum(cot, axis=0, keepdims=True),
        ]
    )
    bias_lines = jnp.sum(grad_pre.astype(f32), axis=0).reshape(hidden // width, width)
    bias_lines = jnp.pad(bias_lines, ((0, 8 - bias_lines.shape[0]), (0, 0)))

    message, grads, grad_scores = attend_back(
        table, own_prefix, projected, grad_attended, attended, log_totals, pivots, block
    )

    log_totals_after = grad_scores[:1]
    arrived = lax.all_to_all(message, "ctx", 0, 0, tiled=True)
    over_rows = (((0,), (0,)), ((), ()))
    grad_heads = lax.dot_general(normed, grads, over_rows, preferred_element_type=f32)
    grad_heads = grad_heads + other_core(grad_heads.astype(bf16)).astype(f32)
    grad_core_sum = grad_heads.astype(bf16)
    *grad_packed_terms, _ = lax.optimization_barrier((*grad_packed_terms, log_totals_after))
    half_heads = after(half_heads, log_totals_after)
    arranged = arrange_heads(pairs, core_number, half_heads, other_core(half_heads))
    grad_packed = sum(term.astype(f32) for term in grad_packed_terms).astype(bf16)
    grad_packed, hops = ring_scatter(grad_packed, order, ring, ((grad_core_sum,), (arrived, arranged[1])))
    late_arrived = after(arrived, hops[min(1, len(hops) - 1)])
    active_last = after(active_last, grad_core_sum)
    mlp = lax.dot_general(active_last, full_proj_t, NT, preferred_element_type=f32)
    result = middle + mlp[:block] + other_core(mlp[block:].astype(bf16)).astype(f32) + proj_shift
    result = result.astype(bf16)
    tokens_grad = finish_tokens(late_arrived, *arranged, own_tokens, grad_middle, gain_one)

    late_grads = after(grads, grad_core_sum)
    grad_normed = lax.dot_general(late_grads, head_weights[:, : 3 * LANES], NT, preferred_element_type=f32)
    grad_normed = grad_normed + lax.dot_general(
        grad_scores[:2], score_columns, (((0,), (1,)), ((), ())), preferred_element_type=f32
    )
    hat_one = (normed.astype(f32) - shift_one) / gain_one

    grad_heads = dp_terms(
        grad_core_sum.reshape(dp_count, ctx_count, shard_rows, 3 * LANES)
    )
    grad_columns = jnp.dot(grad_scores, normed, preferred_element_type=f32)
    lines = jnp.concatenate(
        [
            grad_columns[:2],
            jnp.sum(grad_normed * hat_one, axis=0, keepdims=True),
            jnp.sum(grad_normed, axis=0, keepdims=True),
            early_lines,
        ]
    )
    lines = lines + other_core(lines.astype(bf16)).astype(f32)
    lines = jnp.concatenate([lines, bias_lines])
    lines = jnp.broadcast_to(lines.astype(bf16)[None], (dp_count,) + lines.shape)
    lines = sum(term.astype(f32) for term in dp_terms(lines)).astype(bf16)
    lines = lines.reshape(2 * lines.shape[0], 3 * LANES)
    message = sum(term.astype(f32) for term in grad_heads).astype(bf16)
    message = jnp.concatenate(
        [message, jnp.broadcast_to(lines[None], (ctx_count,) + lines.shape)], axis=1
    )
    message, _ = lax.optimization_barrier((message, arrived))
    arrived = lax.all_to_all(message, "ctx", 0, 0, tiled=True)
    arrived = after(arrived, hops[max(len(hops) - 2, 0)])
    owners = [[] for _ in range(local_heads)]
    for device in range(near):
        for slot in sorted({entry[0] for entry in tables[device].tolist()}):
            owners[local_low[device] + slot].append((device, slot))
    grad_query, grad_key, grad_value, grad_score, vector_grads, fc_bias_grad = unpack_heads(
        near, owners, core_number, dp_number, ctx_number, arrived, shard_rows
    )
    fc_bias_grad = fc_bias_grad.reshape(hidden)

    def both_micro(own):
        other = other_core(own)
        return jnp.where(core == 0, jnp.stack([own, other]), jnp.stack([other, own]))[:, None]

    return (
        both_micro(result),
        both_micro(tokens_grad),
        grad_query,
        grad_key,
        grad_value,
        grad_score,
        grad_packed[:, 2 * hidden :].T,
        grad_packed[:, :hidden],
        grad_packed[:, hidden : 2 * hidden].T,
        vector_grads[0],
        vector_grads[1],
        vector_grads[2],
        vector_grads[3],
        vector_grads[4],
        fc_bias_grad,
        vector_grads[5],
    )


def solution(mesh):
    rows, columns, vector = P(("dp", "ctx"), "tensor"), P("tensor", ("dp", "ctx")), P(("dp", "ctx"))
    tokens = P(None, "dp", "ctx", None)
    in_specs = (
        (tokens, P(None, "dp"))
        + (rows,) * 4
        + (columns, rows, columns)
        + (vector,) * 5
        + (P("tensor"), vector, tokens)
    )
    out_specs = (
        (tokens, tokens)
        + (rows,) * 4
        + (columns, rows, columns)
        + (vector,) * 5
        + (P("tensor"), vector)
    )
    return jax.shard_map(
        partial(on_device, dp_count=mesh.shape["dp"], ctx_count=mesh.shape["ctx"]),
        mesh=mesh,
        in_specs=in_specs,
        out_specs=out_specs,
        check_vma=False,
    )
```
